512 devices in a mesh: ctx: 64 (over z, x), head: 8 (over y, core).
Axes of the slice: x: 4, y: 4, z: 16, core: 2. Of those that a mesh axis runs over, the one named last changes fastest.
Arguments:
- frames: bfloat16 [8192, 1024], P('ctx'), may hold values from -6 to 6
- w_query: bfloat16 [1024, 1024], P(None, 'head'), may hold values from -0.1875 to 0.1875
- w_keys: bfloat16 [1024, 2048], P(None, 'head'), may hold values from -0.1875 to 0.1875
- w_values: bfloat16 [1024, 2048], P(None, 'head'), may hold values from -0.1875 to 0.1875
- w_beta: bfloat16 [1024, 16], P(None, 'head'), may hold values from -0.1875 to 0.1875
- beta_bias: float32 [16], P('head'), may hold values from -1 to 7
- cotangent: bfloat16 [8192, 1024], P('ctx', 'head'), may hold values from -6 to 6
Outputs:
- outputs: bfloat16 [8192, 1024], P('ctx', 'head')
- grad_frames: bfloat16 [8192, 1024], P('ctx', 'head')
- grad_query: float32 [1024, 1024], P(None, 'head')
- grad_keys: float32 [1024, 2048], P(None, 'head')
- grad_values: float32 [1024, 2048], P(None, 'head')
- grad_beta: float32 [1024, 16], P(None, 'head')
- grad_bias: float32 [16], P('head')
The draws below stay inside these ranges and needn't reach their ends.
All inputs are finite; a program needn't handle non-finite values.
Results may differ from the reference program's by a relative error of at most 0.007.
Values sent between devices are 32-bit elements; how exact they have to be, the bound alone decides.
No kernel may reach another device: no remote copies, remote signals or barrier semaphores. Data moves between devices by JAX's collectives and lax.ppermute only.
A program may use at most 64 MiB of HBM per device.

```python
import jax
import jax.numpy as jnp
from jax import lax

D = 1024
DH = 128
BLOCK_ROWS = 128
H = 8
TOKENS = 8192


def level_of(rng, dims, shards, least, top_value):
    level = 1.0
    for dim, blocks in shards:
        steps = jax.random.uniform(jax.random.fold_in(jax.random.fold_in(rng, 6), dim), (blocks,), jnp.float32, least / len(shards), top_value / len(shards))
        level = level * jnp.repeat(jnp.exp(steps), dims[dim] // blocks).reshape((-1,) + (1,) * (len(dims) - 1 - dim))
    return level


def centred(rng, extent, spread, reach, split=(), held_as=jnp.bfloat16):
    array = spread * jax.random.normal(rng, extent, jnp.float32)
    if split:
        array = array * level_of(rng, extent, split, -0.22, 0.18)
    return jnp.clip(array, -reach, reach).astype(held_as)


def setup_inputs(seed: int = 0) -> dict:
    arg_keys = jax.random.split(jax.random.key(seed), 8)
    frames = centred(arg_keys[0], (TOKENS, D), 1.0, 6.0, ((0, 64),))
    w_query = centred(arg_keys[1], (D, H * DH), D ** -0.5, 0.1875, ((1, 8),))
    w_keys = centred(arg_keys[2], (D, H * 2 * DH), D ** -0.5, 0.1875, ((1, 8),))
    w_values = centred(arg_keys[3], (D, H * 2 * DH), D ** -0.5, 0.1875, ((1, 8),))
    w_beta = centred(arg_keys[4], (D, H * 2), D ** -0.5, 0.1875, ((1, 8),))
    beta_bias = jnp.clip(-1.0 + 8.0 * jax.random.uniform(arg_keys[5], (H * 2,), jnp.float32) ** level_of(arg_keys[5], (H * 2,), ((0, 8),), -0.2, 0.2), -1.0, 7.0)
    cotangent = centred(arg_keys[6], (TOKENS, H * DH), 1.0, 6.0, ((0, 64), (1, 8)))
    return dict(frames=frames, w_query=w_query, w_keys=w_keys, w_values=w_values, w_beta=w_beta, beta_bias=beta_bias, cotangent=cotangent)


HIGH = lax.Precision.HIGHEST

def normalize(rows):
    return rows * lax.rsqrt(lax.optimization_barrier(jnp.sum(rows * rows, axis=-1, keepdims=True)) + 1e-06)

def block_solve(keys_block, values_block, beta_block):
    size = keys_block.shape[0]
    gram = jnp.dot(keys_block, keys_block.T, precision=HIGH)
    order = jnp.arange(size)
    below = order[:, None] > order[None, :]
    system = jnp.eye(size, dtype=gram.dtype) + jnp.where(below, beta_block[:, None] * gram, 0.0)
    right = jnp.concatenate([beta_block[:, None] * keys_block, beta_block[:, None] * values_block], axis=1)
    solved = jax.scipy.linalg.solve_triangular(system, right, lower=True, unit_diagonal=True)
    width = keys_block.shape[1]
    return (solved[:, :width], solved[:, width:])

def prepare_head(query_raw, keys_raw, values_raw, logits_raw, bias):
    count = query_raw.shape[0]
    width = query_raw.shape[1]
    blocks = 2 * count // BLOCK_ROWS
    queries = normalize(query_raw).reshape(blocks, BLOCK_ROWS // 2, width)
    keys = normalize(keys_raw.reshape(count, 2, width)).reshape(blocks, BLOCK_ROWS, width)
    values = values_raw.reshape(blocks, BLOCK_ROWS, width)
    betas = (2.0 * jax.nn.sigmoid(logits_raw + bias[None, :])).reshape(blocks, BLOCK_ROWS)
    return (queries, keys, values, betas)

@jax.checkpoint
def block_step(state, pieces):
    query_block, keys_block, values_block, beta_block = pieces
    weight_keys, weight_values = block_solve(keys_block, values_block, beta_block)
    fresh = weight_values - jnp.dot(weight_keys, state, precision=HIGH)
    scores = jnp.dot(query_block, keys_block.T, precision=HIGH)
    rows = jnp.arange(query_block.shape[0])
    cols = jnp.arange(keys_block.shape[0])
    seen = cols[None, :] <= 2 * rows[:, None] + 1
    output = jnp.dot(query_block, state, precision=HIGH) + jnp.dot(jnp.where(seen, scores, 0.0), fresh, precision=HIGH)
    return (state + jnp.dot(keys_block.T, fresh, precision=HIGH), output)

def core_head(query_raw, keys_raw, values_raw, logits_raw, bias, state):
    queries, keys, values, betas = prepare_head(query_raw, keys_raw, values_raw, logits_raw, bias)
    final, outs = lax.scan(block_step, state, (queries, keys, values, betas))
    return (outs.reshape(query_raw.shape), final)

def core_heads(query_raw, keys_raw, values_raw, logits_raw, bias, states):
    heads = states.shape[0]
    count = query_raw.shape[0]
    query_h = jnp.transpose(query_raw.reshape(count, heads, -1), (1, 0, 2))
    keys_h = jnp.transpose(keys_raw.reshape(count, heads, -1), (1, 0, 2))
    values_h = jnp.transpose(values_raw.reshape(count, heads, -1), (1, 0, 2))
    logits_h = jnp.transpose(logits_raw.reshape(count, heads, 2), (1, 0, 2))
    outs, finals = jax.vmap(core_head)(query_h, keys_h, values_h, logits_h, bias.reshape(heads, 2), states)
    return (jnp.transpose(outs, (1, 0, 2)).reshape(count, -1), finals)

def reference(frames, w_query, w_keys, w_values, w_beta, beta_bias, cotangent):
    query_raw = jnp.dot(frames.astype(jnp.float32), w_query.astype(jnp.float32), preferred_element_type=jnp.float32)
    keys_raw = jnp.dot(frames.astype(jnp.float32), w_keys.astype(jnp.float32), preferred_element_type=jnp.float32)
    values_raw = jnp.dot(frames.astype(jnp.float32), w_values.astype(jnp.float32), preferred_element_type=jnp.float32)
    logits_raw = jnp.dot(frames.astype(jnp.float32), w_beta.astype(jnp.float32), preferred_element_type=jnp.float32)
    heads = w_query.shape[1] // DH
    start = jnp.zeros((heads, DH, DH), jnp.float32)

    def forward(query_in, keys_in, values_in, logits_in, bias_in):
        return core_heads(query_in, keys_in, values_in, logits_in, bias_in, start)
    (outputs, finals), pull = jax.vjp(forward, query_raw, keys_raw, values_raw, logits_raw, beta_bias)
    grads = pull((cotangent.astype(jnp.float32), jnp.zeros_like(finals)))
    g_query = grads[0].astype(jnp.bfloat16)
    g_keys = grads[1].astype(jnp.bfloat16)
    g_values = grads[2].astype(jnp.bfloat16)
    g_logits = grads[3].astype(jnp.bfloat16)
    grad_query = jnp.dot(frames.T.astype(jnp.float32), g_query.astype(jnp.float32), preferred_element_type=jnp.float32)
    grad_keys = jnp.dot(frames.T.astype(jnp.float32), g_keys.astype(jnp.float32), preferred_element_type=jnp.float32)
    grad_values = jnp.dot(frames.T.astype(jnp.float32), g_values.astype(jnp.float32), preferred_element_type=jnp.float32)
    grad_beta = jnp.dot(frames.T.astype(jnp.float32), g_logits.astype(jnp.float32), preferred_element_type=jnp.float32)
    grad_frames = jnp.dot(g_query.astype(jnp.float32), w_query.T.astype(jnp.float32), preferred_element_type=jnp.float32)
    grad_frames = grad_frames + jnp.dot(g_keys.astype(jnp.float32), w_keys.T.astype(jnp.float32), preferred_element_type=jnp.float32)
    grad_frames = grad_frames + jnp.dot(g_values.astype(jnp.float32), w_values.T.astype(jnp.float32), preferred_element_type=jnp.float32)
    grad_frames = grad_frames + jnp.dot(g_logits.astype(jnp.float32), w_beta.T.astype(jnp.float32), preferred_element_type=jnp.float32)
    return (outputs.astype(jnp.bfloat16), grad_frames.astype(jnp.bfloat16), grad_query, grad_keys, grad_values, grad_beta, grads[4])
```

```python
import jax
import jax.numpy as jnp
from jax import lax
from jax.experimental import pallas as pl
from jax.experimental.pallas import tpu as pltpu
from jax.sharding import Mesh, PartitionSpec as P

DH = 128
ROWS = 128
HALF = 64
REFL = 256
X_SIZE = 4
Y_SIZE = 4
EPS = 1e-06
VMEM_BYTES = 40 * 1024 * 1024


def halves(a):
    high = a.astype(jnp.bfloat16)
    return high, (a - high.astype(jnp.float32)).astype(jnp.bfloat16)


def dot(a, b, ca=1, cb=0):
    return lax.dot_general(a, b, (((ca,), (cb,)), ((), ())), preferred_element_type=jnp.float32)


def mm(a, b, ca=1, cb=0):
    return mm_halves(halves(a), halves(b), ca, cb)


def mm_halves(a, b, ca=1, cb=0):
    return dot(a[0], b[0], ca, cb) + (dot(a[0], b[1], ca, cb) + dot(a[1], b[0], ca, cb))


def mix(first, second):
    return jnp.concatenate([first[:HALF], second[:HALF], first[HALF:], second[HALF:]], axis=0)


def unmix(rows):
    first = jnp.concatenate([rows[:HALF], rows[ROWS : ROWS + HALF]], axis=0)
    second = jnp.concatenate([rows[HALF:ROWS], rows[ROWS + HALF :]], axis=0)
    return first, second


def place(shape, axis):
    row = lax.broadcasted_iota(jnp.int32, shape, axis)
    return (row & ROWS) + 2 * (row & (HALF - 1)) + ((row >> 6) & 1)


def seen_mask():
    frame = lax.broadcasted_iota(jnp.int32, (ROWS, REFL), 0)
    return (place((ROWS, REFL), 1) >> 1) <= frame


def prepare_kernel(
    frames_ref, wq_ref, wk_ref, wv_ref, wb_ref, bias_ref, cot_ref,
    send_ref, q_ref, k_ref, v_ref, w_ref, u_ref, z_ref, yg_ref, qt_ref, pu_ref, cols_ref, wide_ref,
):
    frames = frames_ref[...]
    wide_ref[...] = frames.astype(jnp.float32)
    q_raw = dot(frames, wq_ref[...])
    k_raw = dot(frames, wk_ref[...])
    v_raw = dot(frames, wv_ref[...])
    logits = dot(frames, wb_ref[...]) + bias_ref[...]
    rq = lax.rsqrt(jnp.sum(q_raw * q_raw, axis=1, keepdims=True) + EPS)
    q = q_raw * rq
    keys = mix(k_raw[:, :DH], k_raw[:, DH:])
    rk = lax.rsqrt(jnp.sum(keys * keys, axis=1, keepdims=True) + EPS)
    k = keys * rk
    v = mix(v_raw[:, :DH], v_raw[:, DH:])
    strength = 2.0 * jax.nn.sigmoid(logits)
    beta = mix(strength[:, 0:1], strength[:, 1:2])
    q_ref[...] = q
    k_ref[...] = k
    v_ref[...] = v
    lane = lax.broadcasted_iota(jnp.int32, (REFL, DH), 1)
    rq_long = jnp.concatenate([rq, rq], axis=0)
    cols_ref[...] = jnp.where(lane == 0, beta, jnp.where(lane == 1, rk, rq_long))

    gram = mm(k, k, 1, 1)
    system = beta * gram
    row, col = place((ROWS, ROWS), 0), place((ROWS, ROWS), 1)
    parts = [system[:ROWS, :ROWS], system[ROWS:, ROWS:]]
    pair = ((row >> 1) == (col >> 1)) & (row > col)
    eye = jnp.where(row == col, 1.0, 0.0)
    inverse = [eye - jnp.where(pair, part, 0.0) for part in parts]
    for level in range(1, 7):
        lower = ((row >> (level + 1)) == (col >> (level + 1))) & ((row >> level) > (col >> level))
        inner = [mm(jnp.where(lower, part, 0.0), inv) for part, inv in zip(parts, inverse)]
        inverse = [inv - mm(inv, mid) for inv, mid in zip(inverse, inner)]
    corner = -mm(inverse[1], mm(system[ROWS:, :ROWS], inverse[0]))
    zero = jnp.zeros((ROWS, ROWS), jnp.float32)
    inverse = jnp.concatenate(
        [
            jnp.concatenate([inverse[0], zero], axis=1),
            jnp.concatenate([corner, inverse[1]], axis=1),
        ],
        axis=0,
    )
    wu = mm(inverse, jnp.concatenate([beta * k, beta * v], axis=1))
    w, u = wu[:, :DH], wu[:, DH:]
    w_ref[...] = w
    u_ref[...] = u
    kwu = mm(k, wu, 0, 0)
    scores = jnp.where(seen_mask(), mm(q, k, 1, 1), 0.0)
    pwu = mm(scores, wu)
    qt = q - pwu[:, :DH]
    qt_ref[...] = qt
    pu_ref[...] = pwu[:, DH:]
    cot = cot_ref[...].astype(jnp.float32)
    send_ref[0] = eye_like() - kwu[:, :DH]
    send_ref[1] = kwu[:, DH:]
    send_ref[2] = mm(cot, qt, 0, 0)
    pg = mm(scores, cot, 0, 0)
    zy = mm(inverse, jnp.concatenate([k, pg], axis=1), 0, 0)
    z_ref[...] = zy[:, :DH]
    yg_ref[...] = zy[:, DH:]


def eye_like():
    row = lax.broadcasted_iota(jnp.int32, (DH, DH), 0)
    col = lax.broadcasted_iota(jnp.int32, (DH, DH), 1)
    return jnp.where(row == col, 1.0, 0.0)


def group_kernel(place_ref, parts_ref, total_ref, before_ref, after_ref):
    me = place_ref[0]
    count = parts_ref.shape[0]
    maps = [halves(parts_ref[i, 0]) for i in range(count)]
    ahead = [jnp.concatenate([parts_ref[0, 0], parts_ref[0, 1]], axis=1)]
    for i in range(1, count):
        moved = mm_halves(maps[i], halves(ahead[-1]))
        ahead.append(jnp.concatenate([moved[:, :DH], moved[:, DH:] + parts_ref[i, 1]], axis=1))
    last = count - 1
    behind = [jnp.concatenate([parts_ref[last, 0], parts_ref[last, 2]], axis=0)]
    for i in range(last - 1, -1, -1):
        moved = mm_halves(halves(behind[-1]), maps[i])
        behind.append(jnp.concatenate([moved[:DH], moved[DH:] + parts_ref[i, 2]], axis=0))
    total_ref[0] = ahead[last][:, :DH]
    total_ref[1] = ahead[last][:, DH:]
    total_ref[2] = behind[last][DH:]
    eye, zero = eye_like(), jnp.zeros((DH, DH), jnp.float32)
    before = jnp.concatenate([eye, zero], axis=1)
    after = jnp.concatenate([eye, zero], axis=0)
    for i in range(last):
        before = jnp.where(me == i + 1, ahead[i], before)
        after = jnp.where(me == last - 1 - i, behind[i], after)
    before_ref[0] = before[:, :DH]
    before_ref[1] = before[:, DH:]
    after_ref[0] = after[:DH]
    after_ref[1] = after[DH:]


def group_scan(parts, place):
    return pl.pallas_call(
        group_kernel,
        out_shape=(f32(3, DH, DH), f32(2, DH, DH), f32(2, DH, DH)),
        in_specs=[
            pl.BlockSpec(memory_space=pltpu.SMEM),
            pl.BlockSpec(memory_space=pltpu.VMEM),
        ],
        compiler_params=pltpu.CompilerParams(vmem_limit_bytes=VMEM_BYTES),
        name="group_scan",
    )(place, parts)


def finish_kernel(
    place_ref, far_ref, near_before_ref, near_after_ref, own_before_ref, own_after_ref,
    frames_ref, wq_ref, wk_ref, wv_ref, wb_ref, cot_ref,
    q_ref, k_ref, v_ref, w_ref, u_ref, z_ref, yg_ref, qt_ref, pu_ref, cols_ref,
    out_ref, pieces_ref, part_ref,
):
    me = place_ref[0]
    count = far_ref.shape[1]

    def far(group, which):
        return jnp.concatenate([far_ref[i, group, which] for i in range(far_ref.shape[0])], axis=0)

    entering = jnp.where(me > 0, far(0, 1), 0.0)
    for i in range(1, count - 1):
        entering = jnp.where(me > i, mm(far(i, 0), entering) + far(i, 1), entering)
    leaving = jnp.where(me < count - 1, far(count - 1, 2), 0.0)
    for i in range(count - 2, 0, -1):
        leaving = jnp.where(me < i, mm(leaving, far(i, 0)) + far(i, 2), leaving)
    for before_ref, after_ref in ((near_before_ref, near_after_ref), (own_before_ref, own_after_ref)):
        entering = mm(before_ref[0], entering) + before_ref[1]
        leaving = mm(leaving, after_ref[0]) + after_ref[1]
    q, k, v = q_ref[...], k_ref[...], v_ref[...]
    cot = cot_ref[...].astype(jnp.float32)
    beta, rk, rq = cols_ref[:, 0:1], cols_ref[:, 1:2], cols_ref[:ROWS, 2:3]
    out_ref[...] = (mm(qt_ref[...], entering) + pu_ref[...]).astype(jnp.bfloat16)
    fresh = u_ref[...] - mm(w_ref[...], entering)
    y = yg_ref[...] + mm(z_ref[...], leaving, 1, 1)
    gram = mm(k, k, 1, 1)
    row, col = place((REFL, REFL), 0), place((REFL, REFL), 1)
    d_system = jnp.where(row > col, -mm(y, fresh, 1, 1), 0.0)
    d_scores = jnp.where(seen_mask(), mm(cot, fresh, 1, 1), 0.0)
    d_query = mm(cot, entering, 1, 1) + mm(d_scores, k)
    error = v - mm(k, entering)
    d_beta = jnp.sum(y * error, axis=1, keepdims=True) + jnp.sum(
        d_system * gram, axis=1, keepdims=True
    )
    by = beta * y
    d_gram = beta * d_system
    d_keys = (
        mm(d_scores, q, 0, 0)
        + mm(fresh, leaving)
        - mm(by, entering, 1, 1)
        + mm(d_gram, k)
        + mm(d_gram, k, 0, 0)
    )
    d_query = rq * (d_query - q * jnp.sum(d_query * q, axis=1, keepdims=True))
    d_keys = rk * (d_keys - k * jnp.sum(d_keys * k, axis=1, keepdims=True))
    d_logits = d_beta * beta * (1.0 - 0.5 * beta)
    l_first, l_second = unmix(d_logits)
    lane2 = lax.broadcasted_iota(jnp.int32, (ROWS, 2), 1)
    g_logits_f32 = jnp.where(lane2 == 0, l_first, l_second)
    g_query = d_query.astype(jnp.bfloat16)
    k_first, k_second = unmix(d_keys)
    v_first, v_second = unmix(by)
    g_keys = jnp.concatenate([k_first, k_second], axis=1).astype(jnp.bfloat16)
    g_values = jnp.concatenate([v_first, v_second], axis=1).astype(jnp.bfloat16)
    g_logits = g_logits_f32.astype(jnp.bfloat16)
    frames = frames_ref[...]
    wide = jnp.float32
    tiles = [
        g_query.astype(wide),
        g_keys[:, :DH].astype(wide),
        g_keys[:, DH:].astype(wide),
        g_values[:, :DH].astype(wide),
    ]
    shared = g_values[:, DH:].astype(wide)
    beta_rows = dot(g_logits, frames, 0, 0)
    bias_row = jnp.sum(g_logits_f32, axis=0, keepdims=True)
    bias_lanes = jnp.where(
        lax.broadcasted_iota(jnp.int32, (1, DH), 1) == 0, bias_row[:, 0:1], bias_row[:, 1:2]
    )
    for i in range(4):
        pieces_ref[i, :ROWS] = tiles[i]
        pieces_ref[i, ROWS : 2 * ROWS] = shared
        span = beta_rows[:, 256 * i : 256 * i + 256]
        pieces_ref[i, 2 * ROWS :] = jnp.concatenate(
            [span[:, :DH], span[:, DH:], bias_lanes, jnp.zeros((3, DH), wide)], axis=0
        )
    part_ref[...] = (
        dot(g_query, wq_ref[...], 1, 1)
        + dot(g_keys, wk_ref[...], 1, 1)
        + dot(g_values, wv_ref[...], 1, 1)
        + dot(g_logits, wb_ref[...], 1, 1)
    )


def f32(*shape):
    return jax.ShapeDtypeStruct(shape, jnp.float32)


def prepare(*args):
    wide = f32(REFL, DH)
    narrow = f32(ROWS, DH)
    return pl.pallas_call(
        prepare_kernel,
        out_shape=(
            f32(3, DH, DH), narrow, wide, wide, wide, wide, wide, wide, narrow, narrow, wide,
            f32(ROWS, 1024),
        ),
        compiler_params=pltpu.CompilerParams(vmem_limit_bytes=VMEM_BYTES),
        name="prepare",
    )(*args)


def finish(*args):
    return pl.pallas_call(
        finish_kernel,
        out_shape=(
            jax.ShapeDtypeStruct((ROWS, DH), jnp.bfloat16),
            f32(4, 264, DH),
            f32(ROWS, 1024),
        ),
        in_specs=[pl.BlockSpec(memory_space=pltpu.SMEM)]
        + [pl.BlockSpec(memory_space=pltpu.VMEM)] * (len(args) - 1),
        compiler_params=pltpu.CompilerParams(vmem_limit_bytes=VMEM_BYTES),
        name="finish",
    )(*args)


def weigh_kernel(place_ref, frames_ref, pieces_ref, sums_ref):
    me = place_ref[0]
    total = jnp.zeros((1024, DH), jnp.float32)
    corner = jnp.zeros((256, DH), jnp.float32)
    extra = jnp.zeros((8, DH), jnp.float32)
    for i in range(4):
        piece = pieces_ref[i, : 2 * ROWS].astype(jnp.bfloat16)
        frames = frames_ref[i].astype(jnp.bfloat16)
        total = total + dot(frames, piece[:ROWS], 0, 0)
        quarter = frames_ref[i, :, pl.ds(pl.multiple_of(me * 256, 256), 256)].astype(jnp.bfloat16)
        corner = corner + dot(quarter, piece[ROWS:], 0, 0)
        extra = extra + pieces_ref[i, 2 * ROWS :]
    for j in range(4):
        if j < 3:
            sums_ref[j, :320] = total[320 * j : 320 * j + 320]
        else:
            sums_ref[j, :64] = total[960:]
            sums_ref[j, 64:320] = corner
        sums_ref[j, 320:] = extra


def weigh(place, frames, pieces):
    return pl.pallas_call(
        weigh_kernel,
        out_shape=f32(4, 328, DH),
        in_specs=[pl.BlockSpec(memory_space=pltpu.SMEM)]
        + [pl.BlockSpec(memory_space=pltpu.VMEM)] * 2,
        compiler_params=pltpu.CompilerParams(vmem_limit_bytes=VMEM_BYTES),
        name="weigh",
    )(place, frames, pieces)


def spread(a, axis):
    return lax.all_to_all(jnp.broadcast_to(a[None], (4, *a.shape)), axis, 0, 0, tiled=True)


def trade(a, axis):
    return lax.all_to_all(a, axis, 0, 0, tiled=True)


def local(frames, w_query, w_keys, w_values, w_beta, beta_bias, cotangent):
    at_x = lax.axis_index("x")[None]
    at_low = lax.axis_index("zl")[None]
    at_high = lax.axis_index("zh")[None]
    weights = (w_query, w_keys, w_values, w_beta)
    own, *kept, wide_frames = prepare(frames, *weights, beta_bias[None], cotangent)
    total, own_before, own_after = group_scan(spread(own, "x"), at_x)
    total, near_before, near_after = group_scan(spread(total, "zl"), at_low)
    quarter = lax.dynamic_slice_in_dim(total, lax.axis_index("x") * 32, 32, axis=1)
    far = spread(spread(quarter, "zh"), "x")
    group_frames = lax.all_gather(wide_frames, "x")
    outputs, pieces, partial = finish(
        at_high, far, near_before, near_after, own_before, own_after,
        frames, *weights, cotangent, *kept,
    )
    grad_frames = lax.psum_scatter(partial, ("y", "core"), scatter_dimension=1, tiled=True).astype(
        jnp.bfloat16
    )
    sums = weigh(at_x, group_frames, trade(pieces, "x"))
    part = jnp.sum(trade(sums, "zl"), axis=0)
    extra = part[320:]
    part = jnp.concatenate(
        [part[:320].reshape(4, 80, DH), jnp.broadcast_to(extra[None], (4, 8, DH))], axis=1
    )
    part = jnp.sum(trade(part, "zh"), axis=0)
    extra = part[80:]
    part = spread(part[:80], "zh")
    part = spread(part.reshape(320, DH), "zl").reshape(1280, DH)
    whole = spread(jnp.concatenate([part, extra], axis=0), "x")
    grad_query = whole[0, :1024]
    grad_keys = jnp.concatenate([whole[1, :1024], whole[2, :1024]], axis=1)
    grad_values = jnp.concatenate(
        [whole[3, :1024], whole[:, 1024:1280].reshape(1024, DH)], axis=1
    )
    beta_rows = whole[:, 1280:1284].reshape(4, 2, 2, DH)
    grad_beta = jnp.transpose(beta_rows, (0, 1, 3, 2)).reshape(1024, 2)
    grad_bias = whole[0, 1284, :2]
    return (outputs, grad_frames, grad_query, grad_keys, grad_values, grad_beta, grad_bias)


def solution(mesh):
    fine = Mesh(mesh.devices.reshape(4, 4, 4, 4, 2), ("zh", "zl", "x", "y", "core"))
    ctx, head = ("zh", "zl", "x"), ("y", "core")
    in_specs = (
        P(ctx, None),
        P(None, head),
        P(None, head),
        P(None, head),
        P(None, head),
        P(head),
        P(ctx, head),
    )
    out_specs = (
        P(ctx, head),
        P(ctx, head),
        P(None, head),
        P(None, head),
        P(None, head),
        P(None, head),
        P(head),
    )
    return jax.shard_map(local, mesh=fine, in_specs=in_specs, out_specs=out_specs, check_vma=False)
```

```python
import functools

import jax
import jax.numpy as jnp
from jax import lax
from jax.experimental import pallas as pl
from jax.experimental.pallas import tpu as pltpu
from jax.sharding import Mesh, PartitionSpec as P

DH = 128
ROWS = 128
HALF = 64
REFL = 256
PARTS = 4
KEPT_ROWS = (
    ("q", ROWS), ("k", REFL), ("v", REFL), ("w", REFL), ("u", REFL), ("z", REFL), ("yg", REFL),
    ("qt", ROWS), ("pu", ROWS), ("cols", REFL),
)
KEPT, KEPT_SIZE = {}, 0
for _name, _rows in KEPT_ROWS:
    KEPT[_name] = slice(KEPT_SIZE, KEPT_SIZE + _rows)
    KEPT_SIZE += _rows
EPS = 1e-06
EXTRA = 24
VMEM_BYTES = 63 * 1024 * 1024
SMALL_BYTES = 16 * 1024 * 1024


def halves(a):
    high = a.astype(jnp.bfloat16)
    return high, (a - high.astype(jnp.float32)).astype(jnp.bfloat16)


def dot(a, b, ca=1, cb=0):
    return lax.dot_general(a, b, (((ca,), (cb,)), ((), ())), preferred_element_type=jnp.float32)


def mm(a, b, ca=1, cb=0):
    return mm_halves(halves(a), halves(b), ca, cb)


def mm_halves(a, b, ca=1, cb=0):
    return dot(a[0], b[0], ca, cb) + (dot(a[0], b[1], ca, cb) + dot(a[1], b[0], ca, cb))


def mix(first, second):
    return jnp.concatenate([first[:HALF], second[:HALF], first[HALF:], second[HALF:]], axis=0)


def unmix(rows):
    first = jnp.concatenate([rows[:HALF], rows[ROWS : ROWS + HALF]], axis=0)
    second = jnp.concatenate([rows[HALF:ROWS], rows[ROWS + HALF :]], axis=0)
    return first, second


def place(shape, axis):
    row = lax.broadcasted_iota(jnp.int32, shape, axis)
    return (row & ROWS) + 2 * (row & (HALF - 1)) + ((row >> 6) & 1)


def seen_mask():
    frame = lax.broadcasted_iota(jnp.int32, (ROWS, REFL), 0)
    return (place((ROWS, REFL), 1) >> 1) <= frame


def fetch(pairs, sems):
    copies = [pltpu.make_async_copy(a, b, sems.at[i]) for i, (a, b) in enumerate(pairs)]
    for copy in copies:
        copy.start()
    return copies


def prepare_kernel(
    bias_ref, wb_ref, frames_any, wk_any, wq_any, wv_any, cot_any,
    send_ref, kept_any, wide_any,
    frames_ref, wk_ref, wq_ref, wv_ref, cot_ref, kept_ref, wide_ref, in_sems, out_sems,
):
    arrive = fetch(
        (
            (frames_any, frames_ref), (wk_any, wk_ref), (wq_any, wq_ref), (wv_any, wv_ref),
            (cot_any, cot_ref),
        ),
        in_sems,
    )

    def keep(name, value):
        kept_ref[KEPT[name], :] = value

    arrive[0].wait()
    frames = frames_ref[...]
    wide_ref[...] = frames.astype(jnp.float32)
    wide_copy = pltpu.make_async_copy(wide_ref, wide_any, out_sems.at[0])
    wide_copy.start()
    logits = dot(frames, wb_ref[...], 1, 1)
    arrive[1].wait()
    k_raw = dot(frames, wk_ref[...])
    for copy in arrive[2:]:
        copy.wait()
    q_raw = dot(frames, wq_ref[...])
    v_raw = dot(frames, wv_ref[...])
    rq = lax.rsqrt(jnp.sum(q_raw * q_raw, axis=1, keepdims=True) + EPS)
    q = q_raw * rq
    keys = mix(k_raw[:, :DH], k_raw[:, DH:])
    rk = lax.rsqrt(jnp.sum(keys * keys, axis=1, keepdims=True) + EPS)
    k = keys * rk
    v = mix(v_raw[:, :DH], v_raw[:, DH:])
    beta = 2.0 * jax.nn.sigmoid(mix(logits[:, 0:1] + bias_ref[0], logits[:, 1:2] + bias_ref[1]))
    keep("q", q)
    keep("k", k)
    keep("v", v)
    lane = lax.broadcasted_iota(jnp.int32, (REFL, DH), 1)
    rq_long = jnp.concatenate([rq, rq], axis=0)
    keep("cols", jnp.where(lane == 0, beta, jnp.where(lane == 1, rk, rq_long)))

    gram = mm(k, k, 1, 1)
    system = beta * gram
    row, col = place((ROWS, ROWS), 0), place((ROWS, ROWS), 1)
    parts = [system[:ROWS, :ROWS], system[ROWS:, ROWS:]]
    pair = ((row >> 1) == (col >> 1)) & (row > col)
    eye = jnp.where(row == col, 1.0, 0.0)
    inverse = [eye - jnp.where(pair, part, 0.0) for part in parts]
    for level in range(1, 7):
        lower = ((row >> (level + 1)) == (col >> (level + 1))) & ((row >> level) > (col >> level))
        inner = [mm(jnp.where(lower, part, 0.0), inv) for part, inv in zip(parts, inverse)]
        inverse = [inv - mm(inv, mid) for inv, mid in zip(inverse, inner)]
    corner = -mm(inverse[1], mm(system[ROWS:, :ROWS], inverse[0]))
    zero = jnp.zeros((ROWS, ROWS), jnp.float32)
    inverse = jnp.concatenate(
        [
            jnp.concatenate([inverse[0], zero], axis=1),
            jnp.concatenate([corner, inverse[1]], axis=1),
        ],
        axis=0,
    )
    wu = mm(inverse, jnp.concatenate([beta * k, beta * v], axis=1))
    w, u = wu[:, :DH], wu[:, DH:]
    keep("w", w)
    keep("u", u)
    kwu = mm(k, wu, 0, 0)
    scores = jnp.where(seen_mask(), mm(q, k, 1, 1), 0.0)
    pwu = mm(scores, wu)
    qt = q - pwu[:, :DH]
    keep("qt", qt)
    keep("pu", pwu[:, DH:])
    cot = cot_ref[...].astype(jnp.float32)
    send_ref[0] = eye_like() - kwu[:, :DH]
    send_ref[1] = kwu[:, DH:]
    send_ref[2] = mm(cot, qt, 0, 0)
    pg = mm(scores, cot, 0, 0)
    zy = mm(inverse, jnp.concatenate([k, pg], axis=1), 0, 0)
    keep("z", zy[:, :DH])
    keep("yg", zy[:, DH:])
    kept_copy = pltpu.make_async_copy(kept_ref, kept_any, out_sems.at[1])
    kept_copy.start()
    wide_copy.wait()
    kept_copy.wait()


def eye_like():
    row = lax.broadcasted_iota(jnp.int32, (DH, DH), 0)
    col = lax.broadcasted_iota(jnp.int32, (DH, DH), 1)
    return jnp.where(row == col, 1.0, 0.0)


def compose_group(me, parts):
    last = len(parts) - 1
    maps = [halves(part[0]) for part in parts]
    ahead = [jnp.concatenate([parts[0][0], parts[0][1]], axis=1)]
    behind = [jnp.concatenate([parts[last][0], parts[last][2]], axis=0)]
    for i in range(1, last + 1):
        moved = mm_halves(maps[i], halves(ahead[-1]))
        ahead.append(jnp.concatenate([moved[:, :DH], moved[:, DH:] + parts[i][1]], axis=1))
        j = last - i
        moved = mm_halves(halves(behind[-1]), maps[j])
        behind.append(jnp.concatenate([moved[:DH], moved[DH:] + parts[j][2]], axis=0))
    whole = (ahead[last][:, :DH], ahead[last][:, DH:], behind[last][DH:])
    eye, zero = eye_like(), jnp.zeros((DH, DH), jnp.float32)
    before = jnp.concatenate([eye, zero], axis=1)
    after = jnp.concatenate([eye, zero], axis=0)
    for i in range(last):
        before = jnp.where(me == i + 1, ahead[i], before)
        after = jnp.where(me == last - 1 - i, behind[i], after)
    return whole, (before[:, :DH], before[:, DH:], after[:DH], after[DH:])


def group_kernel(place_ref, parts_ref, total_ref, around_any, whole_ref, around_ref, sem, *, axis):
    parts = [tuple(parts_ref[i, j] for j in range(3)) for i in range(PARTS)]
    whole, around = compose_group(place_ref[axis], parts)
    for i, value in enumerate(around):
        around_ref[i] = value
    copy = pltpu.make_async_copy(around_ref, around_any, sem)
    copy.start()
    if total_ref.shape[1] == DH:
        for i, value in enumerate(whole):
            total_ref[i] = value
    else:
        for i, value in enumerate(whole):
            whole_ref[i] = value
        rows = DH // PARTS
        mine = pl.ds(pl.multiple_of(place_ref[0] * rows, rows), rows)
        for i in range(3):
            total_ref[i] = whole_ref[i, mine, :]
    copy.wait()


def group_scan(parts, place, axis, rows):
    return pl.pallas_call(
        functools.partial(group_kernel, axis=axis),
        out_shape=(f32(3, rows, DH), f32(4, DH, DH)),
        in_specs=[SMEM, VMEM],
        out_specs=(VMEM, ANY),
        scratch_shapes=[
            pltpu.VMEM((3, DH, DH), jnp.float32),
            pltpu.VMEM((4, DH, DH), jnp.float32),
            pltpu.SemaphoreType.DMA,
        ],
        compiler_params=pltpu.CompilerParams(vmem_limit_bytes=SMALL_BYTES),
        name="group_scan",
    )(place, parts)


def finish_kernel(
    place_ref, far_ref, wb_ref, near_any, own_any, kept_any, cot_any, frames_any, wq_any, wk_any, wv_any,
    out_ref, pieces_any, part_any,
    near_ref, own_ref, kept_ref, cot_ref, frames_ref, wq_ref, wk_ref, wv_ref, pieces_ref, part_ref,
    in_sems, out_sems,
):
    arrive = fetch(
        (
            (near_any, near_ref), (own_any, own_ref), (kept_any, kept_ref), (cot_any, cot_ref),
            (frames_any, frames_ref), (wq_any, wq_ref), (wk_any, wk_ref), (wv_any, wv_ref),
        ),
        in_sems,
    )
    me = place_ref[2]
    count = PARTS

    def far(group, which):
        return jnp.concatenate([far_ref[i, group, which] for i in range(PARTS)], axis=0)

    entering = jnp.where(me > 0, far(0, 1), 0.0)
    for i in range(1, count - 1):
        entering = jnp.where(me > i, mm(far(i, 0), entering) + far(i, 1), entering)
    leaving = jnp.where(me < count - 1, far(count - 1, 2), 0.0)
    for i in range(count - 2, 0, -1):
        leaving = jnp.where(me < i, mm(leaving, far(i, 0)) + far(i, 2), leaving)
    for copy in arrive[:4]:
        copy.wait()
    for around_ref in (near_ref, own_ref):
        entering = mm(around_ref[0], entering) + around_ref[1]
        leaving = mm(leaving, around_ref[2]) + around_ref[3]
    q, k, v = kept_ref[KEPT["q"], :], kept_ref[KEPT["k"], :], kept_ref[KEPT["v"], :]
    cot = cot_ref[...].astype(jnp.float32)
    cols = kept_ref[KEPT["cols"], :]
    beta, rk, rq = cols[:, 0:1], cols[:, 1:2], cols[:ROWS, 2:3]
    out_ref[...] = (mm(kept_ref[KEPT["qt"], :], entering) + kept_ref[KEPT["pu"], :]).astype(jnp.bfloat16)
    fresh = kept_ref[KEPT["u"], :] - mm(kept_ref[KEPT["w"], :], entering)
    y = kept_ref[KEPT["yg"], :] + mm(kept_ref[KEPT["z"], :], leaving, 1, 1)
    gram = mm(k, k, 1, 1)
    row, col = place((REFL, REFL), 0), place((REFL, REFL), 1)
    d_system = jnp.where(row > col, -mm(y, fresh, 1, 1), 0.0)
    d_scores = jnp.where(seen_mask(), mm(cot, fresh, 1, 1), 0.0)
    d_query = mm(cot, entering, 1, 1) + mm(d_scores, k)
    error = v - mm(k, entering)
    d_beta = jnp.sum(y * error, axis=1, keepdims=True) + jnp.sum(
        d_system * gram, axis=1, keepdims=True
    )
    by = beta * y
    d_gram = beta * d_system
    d_keys = (
        mm(d_scores, q, 0, 0)
        + mm(fresh, leaving)
        - mm(by, entering, 1, 1)
        + mm(d_gram, k)
        + mm(d_gram, k, 0, 0)
    )
    d_query = rq * (d_query - q * jnp.sum(d_query * q, axis=1, keepdims=True))
    d_keys = rk * (d_keys - k * jnp.sum(d_keys * k, axis=1, keepdims=True))
    d_logits = d_beta * beta * (1.0 - 0.5 * beta)
    l_first, l_second = unmix(d_logits)
    lane2 = lax.broadcasted_iota(jnp.int32, (ROWS, 2), 1)
    g_logits_f32 = jnp.where(lane2 == 0, l_first, l_second)
    g_query = d_query.astype(jnp.bfloat16)
    k_first, k_second = unmix(d_keys)
    v_first, v_second = unmix(by)
    g_keys = jnp.concatenate([k_first, k_second], axis=1).astype(jnp.bfloat16)
    g_values = jnp.concatenate([v_first, v_second], axis=1).astype(jnp.bfloat16)
    g_logits = g_logits_f32.astype(jnp.bfloat16)
    for copy in arrive[4:]:
        copy.wait()
    part_ref[...] = (
        dot(g_query, wq_ref[...], 1, 1)
        + dot(g_keys, wk_ref[...], 1, 1)
        + dot(g_values, wv_ref[...], 1, 1)
        + dot(g_logits, wb_ref[...])
    )
    part_copy = pltpu.make_async_copy(part_ref, part_any, out_sems.at[0])
    part_copy.start()
    wide = jnp.float32
    tiles = (g_query, g_keys[:, :DH], g_keys[:, DH:], g_values[:, :DH])
    shared = g_values[:, DH:].astype(wide)
    beta_rows = dot(g_logits, frames_ref[...], 0, 0)
    bias_row = jnp.sum(g_logits_f32, axis=0, keepdims=True)
    bias_lanes = jnp.where(
        lax.broadcasted_iota(jnp.int32, (1, DH), 1) == 0, bias_row[:, 0:1], bias_row[:, 1:2]
    )
    extra = [beta_rows[j : j + 1, DH * i : DH * i + DH] for j in range(2) for i in range(8)]
    extra = jnp.concatenate(extra + [bias_lanes, jnp.zeros((7, DH), wide)], axis=0)
    for i in range(PARTS):
        pieces_ref[i, :ROWS] = tiles[i].astype(wide)
        pieces_ref[i, ROWS : 2 * ROWS] = shared
        pieces_ref[i, 2 * ROWS :] = extra
    pieces_copy = pltpu.make_async_copy(pieces_ref, pieces_any, out_sems.at[1])
    pieces_copy.start()
    part_copy.wait()
    pieces_copy.wait()


def f32(*shape):
    return jax.ShapeDtypeStruct(shape, jnp.float32)


SMEM = pl.BlockSpec(memory_space=pltpu.SMEM)
VMEM = pl.BlockSpec(memory_space=pltpu.VMEM)
ANY = pl.BlockSpec(memory_space=pl.ANY)
HBM = pl.BlockSpec(memory_space=pltpu.HBM)


def held(a):
    return pltpu.VMEM(a.shape, a.dtype)


def prepare(bias, w_beta, *large):
    kept, wide = f32(KEPT_SIZE, DH), f32(ROWS, 1024)
    return pl.pallas_call(
        prepare_kernel,
        out_shape=(f32(3, DH, DH), kept, wide),
        in_specs=[SMEM, VMEM] + [HBM] * 5,
        out_specs=(VMEM, ANY, HBM),
        scratch_shapes=[held(a) for a in (*large, kept, wide)]
        + [pltpu.SemaphoreType.DMA((5,)), pltpu.SemaphoreType.DMA((2,))],
        compiler_params=pltpu.CompilerParams(vmem_limit_bytes=VMEM_BYTES),
        name="prepare",
    )(bias, w_beta, *large)


def finish(place, far, w_beta, *large):
    pieces, part = f32(PARTS, 2 * ROWS + EXTRA, DH), f32(ROWS, 1024)
    return pl.pallas_call(
        finish_kernel,
        out_shape=(
            jax.ShapeDtypeStruct((ROWS, DH), jnp.bfloat16),
            pieces,
            part,
        ),
        in_specs=[SMEM, VMEM, VMEM] + [ANY] * 3 + [HBM] * 5,
        out_specs=(VMEM, HBM, HBM),
        scratch_shapes=[held(a) for a in (*large, pieces, part)]
        + [pltpu.SemaphoreType.DMA((8,)), pltpu.SemaphoreType.DMA((2,))],
        compiler_params=pltpu.CompilerParams(vmem_limit_bytes=VMEM_BYTES),
        name="finish",
    )(place, far, w_beta, *large)


def weigh_kernel(place_ref, pieces_ref, frames_any, sums_ref, frames_ref, sems):
    arrive = fetch([(frames_any.at[i], frames_ref.at[i]) for i in range(PARTS)], sems)
    quarter = pl.ds(pl.multiple_of(place_ref[0] * 256, 256), 256)
    total = jnp.zeros((1024, DH), jnp.float32)
    corner = jnp.zeros((256, DH), jnp.float32)
    extra = jnp.zeros((EXTRA, DH), jnp.float32)
    for i in range(PARTS):
        piece = pieces_ref[i, : 2 * ROWS].astype(jnp.bfloat16)
        extra = extra + pieces_ref[i, 2 * ROWS :]
        arrive[i].wait()
        total = total + dot(frames_ref[i].astype(jnp.bfloat16), piece[:ROWS], 0, 0)
        corner = corner + dot(frames_ref[i, :, quarter].astype(jnp.bfloat16), piece[ROWS:], 0, 0)
    total = jnp.concatenate([total, corner], axis=0)
    rows = total.shape[0] // (PARTS * PARTS)
    for i in range(PARTS):
        for j in range(PARTS):
            block = PARTS * j + i
            sums_ref[i, rows * j : rows * j + rows] = total[rows * block : rows * block + rows]
        sums_ref[i, rows * PARTS :] = extra


def weigh(place, pieces, frames):
    return pl.pallas_call(
        weigh_kernel,
        out_shape=f32(PARTS, 1280 // PARTS + EXTRA, DH),
        in_specs=[SMEM, VMEM, HBM],
        scratch_shapes=[held(frames), pltpu.SemaphoreType.DMA((PARTS,))],
        compiler_params=pltpu.CompilerParams(vmem_limit_bytes=VMEM_BYTES),
        name="weigh",
    )(place, pieces, frames)


def lay_kernel(whole_any, query_any, keys_any, values_any, sems):
    left, right = pl.ds(0, DH), pl.ds(DH, DH)
    full = pl.ds(0, 1024)
    pairs = [
        (whole_any.at[0, full], query_any),
        (whole_any.at[1, full], keys_any.at[:, left]),
        (whole_any.at[2, full], keys_any.at[:, right]),
        (whole_any.at[3, full], values_any.at[:, left]),
    ]
    for i in range(PARTS):
        pairs.append(
            (whole_any.at[i, pl.ds(1024, 256)], values_any.at[pl.ds(256 * i, 256), right])
        )
    for copy in fetch(pairs, sems):
        copy.wait()


def lay(whole):
    return pl.pallas_call(
        lay_kernel,
        out_shape=(f32(1024, DH), f32(1024, 2 * DH), f32(1024, 2 * DH)),
        in_specs=[ANY],
        out_specs=(ANY, ANY, ANY),
        scratch_shapes=[pltpu.SemaphoreType.DMA((8,))],
        compiler_params=pltpu.CompilerParams(vmem_limit_bytes=VMEM_BYTES),
        name="lay",
    )(whole)


def spread(a, axis):
    return lax.all_to_all(jnp.broadcast_to(a[None], (PARTS, *a.shape)), axis, 0, 0, tiled=True)


def trade(a, axis):
    return lax.all_to_all(a, axis, 0, 0, tiled=True)


def local(frames, w_query, w_keys, w_values, w_beta, beta_bias, cotangent):
    place = jnp.stack([lax.axis_index("x"), lax.axis_index("zl"), lax.axis_index("zh")])
    beta_turned = w_beta.T
    own, kept, wide_frames = prepare(
        beta_bias, beta_turned, frames, w_keys, w_query, w_values, cotangent
    )
    row, wide_frames = lax.optimization_barrier((lax.all_gather(own, "x"), wide_frames))
    group_frames = lax.all_gather(wide_frames, "x")
    total, own_around = group_scan(row, place, 0, DH)
    total, near_around = group_scan(lax.all_gather(total, "zl"), place, 1, DH // PARTS)
    far = lax.all_gather(lax.all_gather(total, "zh"), "x")
    outputs, pieces, partial = finish(
        place, far, beta_turned, near_around, own_around, kept, cotangent,
        frames, w_query, w_keys, w_values,
    )
    summed = lax.psum_scatter(partial, ("y", "core"), scatter_dimension=1, tiled=True)
    sums = weigh(place, trade(pieces, "x"), group_frames)
    part = jnp.sum(trade(sums, "zl"), axis=0)
    part, extra = part[:320], part[320:]
    part = jnp.concatenate(
        [part.reshape(PARTS, 80, DH), jnp.broadcast_to(extra[None], (PARTS, EXTRA, DH))], axis=1
    )
    part = jnp.sum(trade(part, "zh"), axis=0)
    part, extra = part[:80], part[80:]
    part, summed = lax.optimization_barrier((part, summed))
    grad_frames = summed.astype(jnp.bfloat16)
    part = lax.all_gather(part, ("zh", "zl")).reshape(1280, DH)
    grad_query, grad_keys, grad_values = lay(spread(part, "x"))
    grad_beta = extra[:16].reshape(2, 1024).T
    grad_bias = extra[16, :2]
    return (outputs, grad_frames, grad_query, grad_keys, grad_values, grad_beta, grad_bias)


def solution(mesh):
    fine = Mesh(mesh.devices.reshape(4, 4, 4, 4, 2), ("zh", "zl", "x", "y", "core"))
    ctx, head = ("zh", "zl", "x"), ("y", "core")
    in_specs = (
        P(ctx, None),
        P(None, head),
        P(None, head),
        P(None, head),
        P(None, head),
        P(head),
        P(ctx, head),
    )
    out_specs = (
        P(ctx, head),
        P(ctx, head),
        P(None, head),
        P(None, head),
        P(None, head),
        P(None, head),
        P(head),
    )
    return jax.shard_map(local, mesh=fine, in_specs=in_specs, out_specs=out_specs, check_vma=False)
```

```python
import functools

import jax
import jax.numpy as jnp
from jax import lax
from jax.experimental import pallas as pl
from jax.experimental.pallas import tpu as pltpu
from jax.sharding import Mesh, PartitionSpec as P

DH = 128
ROWS = 128
HALF = 64
REFL = 256
PARTS = 4
KEPT_ROWS = (
    ("q", ROWS), ("k", REFL), ("v", REFL), ("w", REFL), ("u", REFL), ("qt", ROWS), ("pu", ROWS),
    ("cols", REFL), ("z", REFL), ("yg", REFL),
)
KEPT, KEPT_SIZE = {}, 0
for _name, _rows in KEPT_ROWS:
    KEPT[_name] = slice(KEPT_SIZE, KEPT_SIZE + _rows)
    KEPT_SIZE += _rows
EPS = 1e-06
EXTRA = 24
VMEM_BYTES = 63 * 1024 * 1024
SMALL_BYTES = 16 * 1024 * 1024


def halves(a):
    high = a.astype(jnp.bfloat16)
    return high, (a - high.astype(jnp.float32)).astype(jnp.bfloat16)


def dot(a, b, ca=1, cb=0):
    return lax.dot_general(a, b, (((ca,), (cb,)), ((), ())), preferred_element_type=jnp.float32)


def mm(a, b, ca=1, cb=0):
    return mm_halves(halves(a), halves(b), ca, cb)


def mm_halves(a, b, ca=1, cb=0):
    return dot(a[0], b[0], ca, cb) + (dot(a[0], b[1], ca, cb) + dot(a[1], b[0], ca, cb))


def mix(first, second):
    return jnp.concatenate([first[:HALF], second[:HALF], first[HALF:], second[HALF:]], axis=0)


def unmix(rows):
    first = jnp.concatenate([rows[:HALF], rows[ROWS : ROWS + HALF]], axis=0)
    second = jnp.concatenate([rows[HALF:ROWS], rows[ROWS + HALF :]], axis=0)
    return first, second


def place(shape, axis):
    row = lax.broadcasted_iota(jnp.int32, shape, axis)
    return (row & ROWS) + 2 * (row & (HALF - 1)) + ((row >> 6) & 1)


def seen_mask():
    frame = lax.broadcasted_iota(jnp.int32, (ROWS, REFL), 0)
    return (place((ROWS, REFL), 1) >> 1) <= frame


def fetch(pairs, sems):
    copies = [pltpu.make_async_copy(a, b, sems.at[i]) for i, (a, b) in enumerate(pairs)]
    for copy in copies:
        copy.start()
    return copies


def prepare_kernel(
    bias_ref, wb_ref, frames_any, wk_any, wq_any, wv_any, cot_any,
    send_ref, kept_any, wide_any,
    frames_ref, wk_ref, wq_ref, wv_ref, cot_ref, kept_ref, wide_ref, in_sems, out_sems,
):
    arrive = fetch(
        (
            (frames_any, frames_ref), (wk_any, wk_ref), (wq_any, wq_ref), (wv_any, wv_ref),
            (cot_any, cot_ref),
        ),
        in_sems,
    )

    def keep(name, value):
        kept_ref[KEPT[name], :] = value

    arrive[0].wait()
    frames = frames_ref[...]
    wide_ref[...] = frames.astype(jnp.float32)
    out_copies = fetch([(wide_ref, wide_any.at[i]) for i in range(PARTS)], out_sems)
    logits = dot(frames, wb_ref[...], 1, 1)
    arrive[1].wait()
    k_raw = dot(frames, wk_ref[...])
    for copy in arrive[2:]:
        copy.wait()
    q_raw = dot(frames, wq_ref[...])
    v_raw = dot(frames, wv_ref[...])
    rq = lax.rsqrt(jnp.sum(q_raw * q_raw, axis=1, keepdims=True) + EPS)
    q = q_raw * rq
    keys = mix(k_raw[:, :DH], k_raw[:, DH:])
    rk = lax.rsqrt(jnp.sum(keys * keys, axis=1, keepdims=True) + EPS)
    k = keys * rk
    v = mix(v_raw[:, :DH], v_raw[:, DH:])
    beta = 2.0 * jax.nn.sigmoid(mix(logits[:, 0:1] + bias_ref[0], logits[:, 1:2] + bias_ref[1]))
    keep("q", q)
    keep("k", k)
    keep("v", v)
    lane = lax.broadcasted_iota(jnp.int32, (REFL, DH), 1)
    rq_long = jnp.concatenate([rq, rq], axis=0)
    keep("cols", jnp.where(lane == 0, beta, jnp.where(lane == 1, rk, rq_long)))

    gram = mm(k, k, 1, 1)
    system = beta * gram
    row, col = place((ROWS, ROWS), 0), place((ROWS, ROWS), 1)
    parts = [system[:ROWS, :ROWS], system[ROWS:, ROWS:]]
    pair = ((row >> 1) == (col >> 1)) & (row > col)
    eye = jnp.where(row == col, 1.0, 0.0)
    inverse = [eye - jnp.where(pair, part, 0.0) for part in parts]
    for level in range(1, 7):
        lower = ((row >> (level + 1)) == (col >> (level + 1))) & ((row >> level) > (col >> level))
        inner = [mm(jnp.where(lower, part, 0.0), inv) for part, inv in zip(parts, inverse)]
        inverse = [inv - mm(inv, mid) for inv, mid in zip(inverse, inner)]
    corner = -mm(inverse[1], mm(system[ROWS:, :ROWS], inverse[0]))
    zero = jnp.zeros((ROWS, ROWS), jnp.float32)
    inverse = jnp.concatenate(
        [
            jnp.concatenate([inverse[0], zero], axis=1),
            jnp.concatenate([corner, inverse[1]], axis=1),
        ],
        axis=0,
    )
    wu = mm(inverse, jnp.concatenate([beta * k, beta * v], axis=1))
    w, u = wu[:, :DH], wu[:, DH:]
    keep("w", w)
    keep("u", u)
    kwu = mm(k, wu, 0, 0)
    scores = jnp.where(seen_mask(), mm(q, k, 1, 1), 0.0)
    pwu = mm(scores, wu)
    qt = q - pwu[:, :DH]
    keep("qt", qt)
    keep("pu", pwu[:, DH:])
    cot = cot_ref[...].astype(jnp.float32)
    send_ref[0] = eye_like() - kwu[:, :DH]
    send_ref[1] = kwu[:, DH:]
    send_ref[2] = mm(cot, qt, 0, 0)
    late = KEPT["z"].start
    out_copies.append(
        pltpu.make_async_copy(
            kept_ref.at[pl.ds(0, late)], kept_any.at[pl.ds(0, late)], out_sems.at[PARTS]
        )
    )
    out_copies[-1].start()
    pg = mm(scores, cot, 0, 0)
    zy = mm(inverse, jnp.concatenate([k, pg], axis=1), 0, 0)
    keep("z", zy[:, :DH])
    keep("yg", zy[:, DH:])
    late_rows = pl.ds(late, KEPT_SIZE - late)
    out_copies.append(
        pltpu.make_async_copy(
            kept_ref.at[late_rows], kept_any.at[late_rows], out_sems.at[PARTS + 1]
        )
    )
    out_copies[-1].start()
    for copy in out_copies:
        copy.wait()


def eye_like():
    row = lax.broadcasted_iota(jnp.int32, (DH, DH), 0)
    col = lax.broadcasted_iota(jnp.int32, (DH, DH), 1)
    return jnp.where(row == col, 1.0, 0.0)


def compose_group(me, parts):
    last = len(parts) - 1
    maps = [halves(part[0]) for part in parts]
    ahead = [jnp.concatenate([parts[0][0], parts[0][1]], axis=1)]
    behind = [jnp.concatenate([parts[last][0], parts[last][2]], axis=0)]
    for i in range(1, last + 1):
        moved = mm_halves(maps[i], halves(ahead[-1]))
        ahead.append(jnp.concatenate([moved[:, :DH], moved[:, DH:] + parts[i][1]], axis=1))
        j = last - i
        moved = mm_halves(halves(behind[-1]), maps[j])
        behind.append(jnp.concatenate([moved[:DH], moved[DH:] + parts[j][2]], axis=0))
    whole = (ahead[last][:, :DH], ahead[last][:, DH:], behind[last][DH:])
    eye, zero = eye_like(), jnp.zeros((DH, DH), jnp.float32)
    before = jnp.concatenate([eye, zero], axis=1)
    after = jnp.concatenate([eye, zero], axis=0)
    for i in range(last):
        before = jnp.where(me == i + 1, ahead[i], before)
        after = jnp.where(me == last - 1 - i, behind[i], after)
    return whole, (before[:, :DH], before[:, DH:], after[:DH], after[DH:])


def group_kernel(place_ref, parts_ref, total_ref, around_any, whole_ref, around_ref, sem, *, axis):
    parts = [tuple(parts_ref[i, j] for j in range(3)) for i in range(PARTS)]
    whole, around = compose_group(place_ref[axis], parts)
    for i, value in enumerate(around):
        around_ref[i] = value
    copy = pltpu.make_async_copy(around_ref, around_any, sem)
    copy.start()
    if total_ref.shape[1] == DH:
        for i, value in enumerate(whole):
            total_ref[i] = value
    else:
        for i, value in enumerate(whole):
            whole_ref[i] = value
        rows = DH // PARTS
        mine = pl.ds(pl.multiple_of(place_ref[0] * rows, rows), rows)
        for i in range(3):
            total_ref[i] = whole_ref[i, mine, :]
    copy.wait()


def group_scan(parts, place, axis, rows):
    return pl.pallas_call(
        functools.partial(group_kernel, axis=axis),
        out_shape=(f32(3, rows, DH), f32(4, DH, DH)),
        in_specs=[SMEM, VMEM],
        out_specs=(VMEM, HBM),
        scratch_shapes=[
            pltpu.VMEM((3, DH, DH), jnp.float32),
            pltpu.VMEM((4, DH, DH), jnp.float32),
            pltpu.SemaphoreType.DMA,
        ],
        compiler_params=pltpu.CompilerParams(vmem_limit_bytes=VMEM_BYTES),
        name="group_scan",
    )(place, parts)


def finish_kernel(
    place_ref, wb_ref, far_any, near_any, own_any, kept_any, cot_any, frames_any, wq_any, wk_any, wv_any,
    out_ref, pieces_any, part_any,
    far_ref, near_ref, own_ref, kept_ref, cot_ref, frames_ref, wq_ref, wk_ref, wv_ref, pieces_ref, part_ref,
    in_sems, out_sems,
):
    arrive = fetch(
        (
            (far_any, far_ref), (near_any, near_ref), (own_any, own_ref), (kept_any, kept_ref), (cot_any, cot_ref),
            (frames_any, frames_ref), (wq_any, wq_ref), (wk_any, wk_ref), (wv_any, wv_ref),
        ),
        in_sems,
    )
    me = place_ref[2]
    arrive[0].wait()
    count = PARTS

    def far(group, which):
        return jnp.concatenate([far_ref[i, group, which] for i in range(PARTS)], axis=0)

    entering = jnp.where(me > 0, far(0, 1), 0.0)
    for i in range(1, count - 1):
        entering = jnp.where(me > i, mm(far(i, 0), entering) + far(i, 1), entering)
    leaving = jnp.where(me < count - 1, far(count - 1, 2), 0.0)
    for i in range(count - 2, 0, -1):
        leaving = jnp.where(me < i, mm(leaving, far(i, 0)) + far(i, 2), leaving)
    for copy in arrive[1:5]:
        copy.wait()
    for around_ref in (near_ref, own_ref):
        entering = mm(around_ref[0], entering) + around_ref[1]
        leaving = mm(leaving, around_ref[2]) + around_ref[3]
    q, k, v = kept_ref[KEPT["q"], :], kept_ref[KEPT["k"], :], kept_ref[KEPT["v"], :]
    cot = cot_ref[...].astype(jnp.float32)
    cols = kept_ref[KEPT["cols"], :]
    beta, rk, rq = cols[:, 0:1], cols[:, 1:2], cols[:ROWS, 2:3]
    out_ref[...] = (mm(kept_ref[KEPT["qt"], :], entering) + kept_ref[KEPT["pu"], :]).astype(jnp.bfloat16)
    fresh = kept_ref[KEPT["u"], :] - mm(kept_ref[KEPT["w"], :], entering)
    y = kept_ref[KEPT["yg"], :] + mm(kept_ref[KEPT["z"], :], leaving, 1, 1)
    gram = mm(k, k, 1, 1)
    row, col = place((REFL, REFL), 0), place((REFL, REFL), 1)
    d_system = jnp.where(row > col, -mm(y, fresh, 1, 1), 0.0)
    d_scores = jnp.where(seen_mask(), mm(cot, fresh, 1, 1), 0.0)
    d_query = mm(cot, entering, 1, 1) + mm(d_scores, k)
    error = v - mm(k, entering)
    d_beta = jnp.sum(y * error, axis=1, keepdims=True) + jnp.sum(
        d_system * gram, axis=1, keepdims=True
    )
    by = beta * y
    d_gram = beta * d_system
    d_keys = (
        mm(d_scores, q, 0, 0)
        + mm(fresh, leaving)
        - mm(by, entering, 1, 1)
        + mm(d_gram, k)
        + mm(d_gram, k, 0, 0)
    )
    d_query = rq * (d_query - q * jnp.sum(d_query * q, axis=1, keepdims=True))
    d_keys = rk * (d_keys - k * jnp.sum(d_keys * k, axis=1, keepdims=True))
    d_logits = d_beta * beta * (1.0 - 0.5 * beta)
    l_first, l_second = unmix(d_logits)
    lane2 = lax.broadcasted_iota(jnp.int32, (ROWS, 2), 1)
    g_logits_f32 = jnp.where(lane2 == 0, l_first, l_second)
    g_query = d_query.astype(jnp.bfloat16)
    k_first, k_second = unmix(d_keys)
    v_first, v_second = unmix(by)
    g_keys = jnp.concatenate([k_first, k_second], axis=1).astype(jnp.bfloat16)
    g_values = jnp.concatenate([v_first, v_second], axis=1).astype(jnp.bfloat16)
    g_logits = g_logits_f32.astype(jnp.bfloat16)
    for copy in arrive[5:]:
        copy.wait()
    part = (
        dot(g_query, wq_ref[...], 1, 1)
        + dot(g_keys, wk_ref[...], 1, 1)
        + dot(g_values, wv_ref[...], 1, 1)
        + dot(g_logits, wb_ref[...])
    )
    for i in range(8):
        part_ref[i] = part[:, DH * i : DH * i + DH]
    part_copy = pltpu.make_async_copy(part_ref, part_any, out_sems.at[0])
    part_copy.start()
    wide = jnp.float32
    tiles = (g_query, g_keys[:, :DH], g_keys[:, DH:], g_values[:, :DH])
    shared = g_values[:, DH:].astype(wide)
    beta_rows = dot(g_logits, frames_ref[...], 0, 0)
    bias_row = jnp.sum(g_logits_f32, axis=0, keepdims=True)
    bias_lanes = jnp.where(
        lax.broadcasted_iota(jnp.int32, (1, DH), 1) == 0, bias_row[:, 0:1], bias_row[:, 1:2]
    )
    extra = [beta_rows[j : j + 1, DH * i : DH * i + DH] for j in range(2) for i in range(8)]
    extra = jnp.concatenate(extra + [bias_lanes, jnp.zeros((7, DH), wide)], axis=0)
    for i in range(PARTS):
        pieces_ref[i, :ROWS] = tiles[i].astype(wide)
        pieces_ref[i, ROWS : 2 * ROWS] = shared
        pieces_ref[i, 2 * ROWS :] = extra
    pieces_copy = pltpu.make_async_copy(pieces_ref, pieces_any, out_sems.at[1])
    pieces_copy.start()
    part_copy.wait()
    pieces_copy.wait()


def f32(*shape):
    return jax.ShapeDtypeStruct(shape, jnp.float32)


SMEM = pl.BlockSpec(memory_space=pltpu.SMEM)
VMEM = pl.BlockSpec(memory_space=pltpu.VMEM)
ANY = pl.BlockSpec(memory_space=pl.ANY)
HBM = pl.BlockSpec(memory_space=pltpu.HBM)


def held(a):
    return pltpu.VMEM(a.shape, a.dtype)


def prepare(bias, w_beta, *large):
    kept, wide = f32(KEPT_SIZE, DH), f32(PARTS, ROWS, 1024)
    return pl.pallas_call(
        prepare_kernel,
        out_shape=(f32(3, DH, DH), kept, wide),
        in_specs=[SMEM, VMEM] + [HBM] * 5,
        out_specs=(VMEM, HBM, HBM),
        scratch_shapes=[held(a) for a in (*large, kept, f32(ROWS, 1024))]
        + [pltpu.SemaphoreType.DMA((5,)), pltpu.SemaphoreType.DMA((PARTS + 2,))],
        compiler_params=pltpu.CompilerParams(vmem_limit_bytes=VMEM_BYTES),
        name="prepare",
    )(bias, w_beta, *large)


def finish(place, w_beta, *large):
    pieces, part = f32(PARTS, 2 * ROWS + EXTRA, DH), f32(8, ROWS, DH)
    return pl.pallas_call(
        finish_kernel,
        out_shape=(
            jax.ShapeDtypeStruct((ROWS, DH), jnp.bfloat16),
            pieces,
            part,
        ),
        in_specs=[SMEM, VMEM] + [HBM] * 9,
        out_specs=(VMEM, HBM, HBM),
        scratch_shapes=[held(a) for a in (*large, pieces, part)]
        + [pltpu.SemaphoreType.DMA((9,)), pltpu.SemaphoreType.DMA((2,))],
        compiler_params=pltpu.CompilerParams(vmem_limit_bytes=VMEM_BYTES),
        name="finish",
    )(place, w_beta, *large)


def weigh_kernel(place_ref, pieces_any, frames_any, sums_ref, pieces_ref, frames_ref, sems):
    pairs = [(pieces_any, pieces_ref)] + [(frames_any.at[i], frames_ref.at[i]) for i in range(PARTS)]
    arrive = fetch(pairs, sems)
    quarter = pl.ds(pl.multiple_of(place_ref[0] * 256, 256), 256)
    total = jnp.zeros((1024, DH), jnp.float32)
    corner = jnp.zeros((256, DH), jnp.float32)
    extra = jnp.zeros((EXTRA, DH), jnp.float32)
    arrive[0].wait()
    for i in range(PARTS):
        piece = pieces_ref[i, : 2 * ROWS].astype(jnp.bfloat16)
        extra = extra + pieces_ref[i, 2 * ROWS :]
        arrive[i + 1].wait()
        total = total + dot(frames_ref[i].astype(jnp.bfloat16), piece[:ROWS], 0, 0)
        corner = corner + dot(frames_ref[i, :, quarter].astype(jnp.bfloat16), piece[ROWS:], 0, 0)
    total = jnp.concatenate([total, corner], axis=0)
    rows = total.shape[0] // (PARTS * PARTS)
    for i in range(PARTS):
        for j in range(PARTS):
            block = PARTS * j + i
            sums_ref[i, rows * j : rows * j + rows] = total[rows * block : rows * block + rows]
        sums_ref[i, rows * PARTS :] = extra


def weigh(place, pieces, frames):
    return pl.pallas_call(
        weigh_kernel,
        out_shape=f32(PARTS, 1280 // PARTS + EXTRA, DH),
        in_specs=[SMEM, HBM, HBM],
        scratch_shapes=[held(pieces), held(frames), pltpu.SemaphoreType.DMA((PARTS + 1,))],
        compiler_params=pltpu.CompilerParams(vmem_limit_bytes=VMEM_BYTES),
        name="weigh",
    )(place, pieces, frames)


def lay_kernel(whole_ref, query_any, keys_any, values_any, sems):
    left, right = pl.ds(0, DH), pl.ds(DH, DH)
    full = pl.ds(0, 1024)
    pairs = [
        (whole_ref.at[0, full], query_any),
        (whole_ref.at[1, full], keys_any.at[:, left]),
        (whole_ref.at[2, full], keys_any.at[:, right]),
        (whole_ref.at[3, full], values_any.at[:, left]),
    ]
    for i in range(PARTS):
        pairs.append(
            (whole_ref.at[i, pl.ds(1024, 256)], values_any.at[pl.ds(256 * i, 256), right])
        )
    for copy in fetch(pairs, sems):
        copy.wait()


def lay(whole):
    return pl.pallas_call(
        lay_kernel,
        out_shape=(f32(1024, DH), f32(1024, 2 * DH), f32(1024, 2 * DH)),
        in_specs=[VMEM],
        out_specs=(HBM, HBM, HBM),
        scratch_shapes=[pltpu.SemaphoreType.DMA((8,))],
        compiler_params=pltpu.CompilerParams(vmem_limit_bytes=SMALL_BYTES),
        name="lay",
    )(whole)


def spread(a, axis):
    return lax.all_to_all(jnp.broadcast_to(a[None], (PARTS, *a.shape)), axis, 0, 0, tiled=True)


def trade(a, axis):
    return lax.all_to_all(a, axis, 0, 0, tiled=True)


def local(frames, w_query, w_keys, w_values, w_beta, beta_bias, cotangent):
    place = jnp.stack([lax.axis_index("x"), lax.axis_index("zl"), lax.axis_index("zh")])
    beta_turned = w_beta.T
    own, kept, wide_frames = prepare(
        beta_bias, beta_turned, frames, w_keys, w_query, w_values, cotangent
    )
    row, wide_frames = lax.optimization_barrier((lax.all_gather(own, "x"), wide_frames))
    group_frames = trade(wide_frames, "x")
    total, own_around = group_scan(row, place, 0, DH)
    total, near_around = group_scan(lax.all_gather(total, "zl"), place, 1, DH // PARTS)
    far = lax.all_gather(lax.all_gather(total, "zh"), "x")
    far, group_frames = lax.optimization_barrier((far, group_frames))
    outputs, pieces, partial = finish(
        place, beta_turned, far, near_around, own_around, kept, cotangent,
        frames, w_query, w_keys, w_values,
    )
    sums = weigh(place, trade(pieces, "x"), group_frames)
    part = jnp.sum(trade(sums, "zl"), axis=0)
    part, extra = part[:320], part[320:]
    part = jnp.concatenate(
        [part.reshape(PARTS, 80, DH), jnp.broadcast_to(extra[None], (PARTS, EXTRA, DH))], axis=1
    )
    part = jnp.sum(trade(part, "zh"), axis=0)
    part, extra = part[:80], part[80:]
    part, partial = lax.optimization_barrier((part, partial))
    partial = trade(partial, ("y", "core"))
    part = lax.all_gather(part, ("zh", "zl")).reshape(1280, DH)
    part, partial = lax.optimization_barrier((part, partial))
    grad_frames = jnp.sum(partial, axis=0).astype(jnp.bfloat16)
    grad_query, grad_keys, grad_values = lay(spread(part, "x"))
    grad_beta = extra[:16].reshape(2, 1024).T
    grad_bias = extra[16, :2]
    return (outputs, grad_frames, grad_query, grad_keys, grad_values, grad_beta, grad_bias)


def solution(mesh):
    fine = Mesh(mesh.devices.reshape(4, 4, 4, 4, 2), ("zh", "zl", "x", "y", "core"))
    ctx, head = ("zh", "zl", "x"), ("y", "core")
    in_specs = (
        P(ctx, None),
        P(None, head),
        P(None, head),
        P(None, head),
        P(None, head),
        P(head),
        P(ctx, head),
    )
    out_specs = (
        P(ctx, head),
        P(ctx, head),
        P(None, head),
        P(None, head),
        P(None, head),
        P(None, head),
        P(head),
    )
    return jax.shard_map(local, mesh=fine, in_specs=in_specs, out_specs=out_specs, check_vma=False)
```

```python
import functools

import jax
import jax.numpy as jnp
from jax import lax
from jax.experimental import pallas as pl
from jax.experimental.pallas import tpu as pltpu
from jax.sharding import Mesh, PartitionSpec as P

DH = 128
ROWS = 128
HALF = 64
REFL = 256
PARTS = 4
KEPT_ROWS = (
    ("q", ROWS), ("k", REFL), ("v", REFL), ("w", REFL), ("u", REFL), ("qt", ROWS), ("pu", ROWS),
    ("cols", REFL), ("z", REFL), ("yg", REFL),
)
KEPT, KEPT_SIZE = {}, 0
for _name, _rows in KEPT_ROWS:
    KEPT[_name] = slice(KEPT_SIZE, KEPT_SIZE + _rows)
    KEPT_SIZE += _rows
EPS = 1e-06
EXTRA = 8
LARGE_BYTES = 63 * 1024 * 1024
SMALL_BYTES = 16 * 1024 * 1024
FINISH_BYTES = LARGE_BYTES

SIDE_BYTES = LARGE_BYTES


def halves(a):
    high = a.astype(jnp.bfloat16)
    return high, (a - high.astype(jnp.float32)).astype(jnp.bfloat16)


def dot(a, b, ca=1, cb=0):
    return lax.dot_general(a, b, (((ca,), (cb,)), ((), ())), preferred_element_type=jnp.float32)


def mm(a, b, ca=1, cb=0):
    return mm_halves(halves(a), halves(b), ca, cb)


def mm_halves(a, b, ca=1, cb=0):
    return dot(a[0], b[0], ca, cb) + (dot(a[0], b[1], ca, cb) + dot(a[1], b[0], ca, cb))


def mix(first, second):
    return jnp.concatenate([first[:HALF], second[:HALF], first[HALF:], second[HALF:]], axis=0)


def unmix(rows):
    first = jnp.concatenate([rows[:HALF], rows[ROWS : ROWS + HALF]], axis=0)
    second = jnp.concatenate([rows[HALF:ROWS], rows[ROWS + HALF :]], axis=0)
    return first, second


def place(shape, axis):
    row = lax.broadcasted_iota(jnp.int32, shape, axis)
    return (row & ROWS) + 2 * (row & (HALF - 1)) + ((row >> 6) & 1)


def seen_mask():
    frame = lax.broadcasted_iota(jnp.int32, (ROWS, REFL), 0)
    return (place((ROWS, REFL), 1) >> 1) <= frame


def fetch(pairs, sems):
    copies = [pltpu.make_async_copy(a, b, sems.at[i]) for i, (a, b) in enumerate(pairs)]
    for copy in copies:
        copy.start()
    return copies


def prepare_kernel(
    bias_ref, wb_ref, frames_any, wk_any, wq_any, wv_any, cot_any,
    send_ref, kept_any, wide_any,
    frames_ref, wk_ref, wq_ref, wv_ref, cot_ref, kept_ref, wide_ref, in_sems, out_sems,
):
    arrive = fetch(
        (
            (frames_any, frames_ref), (wk_any, wk_ref), (wq_any, wq_ref), (wv_any, wv_ref),
            (cot_any, cot_ref),
        ),
        in_sems,
    )

    def keep(name, value):
        kept_ref[KEPT[name], :] = value

    arrive[0].wait()
    frames = frames_ref[...]
    wide_ref[...] = frames.astype(jnp.float32)
    out_copies = fetch([(wide_ref, wide_any.at[i]) for i in range(PARTS)], out_sems)
    logits = dot(frames, wb_ref[...], 1, 1)
    arrive[1].wait()
    k_raw = dot(frames, wk_ref[...])
    for copy in arrive[2:]:
        copy.wait()
    q_raw = dot(frames, wq_ref[...])
    v_raw = dot(frames, wv_ref[...])
    rq = lax.rsqrt(jnp.sum(q_raw * q_raw, axis=1, keepdims=True) + EPS)
    q = q_raw * rq
    keys = mix(k_raw[:, :DH], k_raw[:, DH:])
    rk = lax.rsqrt(jnp.sum(keys * keys, axis=1, keepdims=True) + EPS)
    k = keys * rk
    v = mix(v_raw[:, :DH], v_raw[:, DH:])
    beta = 2.0 * jax.nn.sigmoid(mix(logits[:, 0:1] + bias_ref[0], logits[:, 1:2] + bias_ref[1]))
    keep("q", q)
    keep("k", k)
    keep("v", v)
    lane = lax.broadcasted_iota(jnp.int32, (REFL, DH), 1)
    rq_long = jnp.concatenate([rq, rq], axis=0)
    keep("cols", jnp.where(lane == 0, beta, jnp.where(lane == 1, rk, rq_long)))

    gram = mm(k, k, 1, 1)
    system = beta * gram
    row, col = place((ROWS, ROWS), 0), place((ROWS, ROWS), 1)
    parts = [system[:ROWS, :ROWS], system[ROWS:, ROWS:]]
    pair = ((row >> 1) == (col >> 1)) & (row > col)
    eye = jnp.where(row == col, 1.0, 0.0)
    inverse = [eye - jnp.where(pair, part, 0.0) for part in parts]
    for level in range(1, 7):
        lower = ((row >> (level + 1)) == (col >> (level + 1))) & ((row >> level) > (col >> level))
        inner = [mm(jnp.where(lower, part, 0.0), inv) for part, inv in zip(parts, inverse)]
        inverse = [inv - mm(inv, mid) for inv, mid in zip(inverse, inner)]
    corner = -mm(inverse[1], mm(system[ROWS:, :ROWS], inverse[0]))
    zero = jnp.zeros((ROWS, ROWS), jnp.float32)
    inverse = jnp.concatenate(
        [
            jnp.concatenate([inverse[0], zero], axis=1),
            jnp.concatenate([corner, inverse[1]], axis=1),
        ],
        axis=0,
    )
    wu = mm(inverse, jnp.concatenate([beta * k, beta * v], axis=1))
    w, u = wu[:, :DH], wu[:, DH:]
    keep("w", w)
    keep("u", u)
    kwu = mm(k, wu, 0, 0)
    scores = jnp.where(seen_mask(), mm(q, k, 1, 1), 0.0)
    pwu = mm(scores, wu)
    qt = q - pwu[:, :DH]
    keep("qt", qt)
    keep("pu", pwu[:, DH:])
    cot = cot_ref[...].astype(jnp.float32)
    send_ref[0] = eye_like() - kwu[:, :DH]
    send_ref[1] = kwu[:, DH:]
    send_ref[2] = mm(cot, qt, 0, 0)
    late = KEPT["z"].start
    out_copies.append(
        pltpu.make_async_copy(
            kept_ref.at[pl.ds(0, late)], kept_any.at[pl.ds(0, late)], out_sems.at[PARTS]
        )
    )
    out_copies[-1].start()
    pg = mm(scores, cot, 0, 0)
    zy = mm(inverse, jnp.concatenate([k, pg], axis=1), 0, 0)
    keep("z", zy[:, :DH])
    keep("yg", zy[:, DH:])
    late_rows = pl.ds(late, KEPT_SIZE - late)
    out_copies.append(
        pltpu.make_async_copy(
            kept_ref.at[late_rows], kept_any.at[late_rows], out_sems.at[PARTS + 1]
        )
    )
    out_copies[-1].start()
    for copy in out_copies:
        copy.wait()


def eye_like():
    row = lax.broadcasted_iota(jnp.int32, (DH, DH), 0)
    col = lax.broadcasted_iota(jnp.int32, (DH, DH), 1)
    return jnp.where(row == col, 1.0, 0.0)


def compose_group(me, parts):
    last = len(parts) - 1
    maps = [halves(part[0]) for part in parts]
    ahead = [jnp.concatenate([parts[0][0], parts[0][1]], axis=1)]
    behind = [jnp.concatenate([parts[last][0], parts[last][2]], axis=0)]
    for i in range(1, last + 1):
        moved = mm_halves(maps[i], halves(ahead[-1]))
        ahead.append(jnp.concatenate([moved[:, :DH], moved[:, DH:] + parts[i][1]], axis=1))
        j = last - i
        moved = mm_halves(halves(behind[-1]), maps[j])
        behind.append(jnp.concatenate([moved[:DH], moved[DH:] + parts[j][2]], axis=0))
    whole = (ahead[last][:, :DH], ahead[last][:, DH:], behind[last][DH:])
    eye, zero = eye_like(), jnp.zeros((DH, DH), jnp.float32)
    before = jnp.concatenate([eye, zero], axis=1)
    after = jnp.concatenate([eye, zero], axis=0)
    for i in range(last):
        before = jnp.where(me == i + 1, ahead[i], before)
        after = jnp.where(me == last - 1 - i, behind[i], after)
    return whole, (before[:, :DH], before[:, DH:], after[:DH], after[DH:])


def group_kernel(place_ref, parts_ref, total_ref, around_any, whole_ref, around_ref, sem, *, axis):
    parts = [tuple(parts_ref[i, j] for j in range(3)) for i in range(PARTS)]
    whole, around = compose_group(place_ref[axis], parts)
    for i, value in enumerate(around):
        around_ref[i] = value
    copy = pltpu.make_async_copy(around_ref, around_any, sem)
    copy.start()
    if total_ref.shape[1] == DH:
        for i, value in enumerate(whole):
            total_ref[i] = value
    else:
        for i, value in enumerate(whole):
            whole_ref[i] = value
        rows = DH // PARTS
        mine = pl.ds(pl.multiple_of(place_ref[0] * rows, rows), rows)
        for i in range(3):
            total_ref[i] = whole_ref[i, mine, :]
    copy.wait()


def group_scan(parts, place, axis, rows):
    return pl.pallas_call(
        functools.partial(group_kernel, axis=axis),
        out_shape=(f32(3, rows, DH), f32(4, DH, DH)),
        in_specs=[SMEM, VMEM],
        out_specs=(VMEM, HBM),
        scratch_shapes=[
            pltpu.VMEM((3, DH, DH), jnp.float32),
            pltpu.VMEM((4, DH, DH), jnp.float32),
            pltpu.SemaphoreType.DMA,
        ],
        compiler_params=pltpu.CompilerParams(vmem_limit_bytes=SMALL_BYTES),
        name="group_scan",
    )(place, parts)


def finish_kernel(
    place_ref, far_any, near_any, own_any, kept_any, cot_any, frames_any,
    out_ref, pieces_any, tiles_any,
    far_ref, near_ref, own_ref, kept_ref, cot_ref, frames_ref, pieces_ref, tiles_ref,
    in_sems, out_sems,
):
    arrive = fetch(
        (
            (far_any, far_ref), (near_any, near_ref), (own_any, own_ref), (kept_any, kept_ref),
            (cot_any, cot_ref), (frames_any, frames_ref),
        ),
        in_sems,
    )
    me = place_ref[2]
    arrive[0].wait()
    count = PARTS

    def far(group, which):
        return jnp.concatenate([far_ref[i, group, which] for i in range(PARTS)], axis=0)

    entering = jnp.where(me > 0, far(0, 1), 0.0)
    for i in range(1, count - 1):
        entering = jnp.where(me > i, mm(far(i, 0), entering) + far(i, 1), entering)
    leaving = jnp.where(me < count - 1, far(count - 1, 2), 0.0)
    for i in range(count - 2, 0, -1):
        leaving = jnp.where(me < i, mm(leaving, far(i, 0)) + far(i, 2), leaving)
    for copy in arrive[1:5]:
        copy.wait()
    for around_ref in (near_ref, own_ref):
        entering = mm(around_ref[0], entering) + around_ref[1]
        leaving = mm(leaving, around_ref[2]) + around_ref[3]
    q, k, v = kept_ref[KEPT["q"], :], kept_ref[KEPT["k"], :], kept_ref[KEPT["v"], :]
    cot = cot_ref[...].astype(jnp.float32)
    cols = kept_ref[KEPT["cols"], :]
    beta, rk, rq = cols[:, 0:1], cols[:, 1:2], cols[:ROWS, 2:3]
    out_ref[...] = (mm(kept_ref[KEPT["qt"], :], entering) + kept_ref[KEPT["pu"], :]).astype(jnp.bfloat16)
    fresh = kept_ref[KEPT["u"], :] - mm(kept_ref[KEPT["w"], :], entering)
    y = kept_ref[KEPT["yg"], :] + mm(kept_ref[KEPT["z"], :], leaving, 1, 1)
    gram = mm(k, k, 1, 1)
    row, col = place((REFL, REFL), 0), place((REFL, REFL), 1)
    d_system = jnp.where(row > col, -mm(y, fresh, 1, 1), 0.0)
    d_scores = jnp.where(seen_mask(), mm(cot, fresh, 1, 1), 0.0)
    d_query = mm(cot, entering, 1, 1) + mm(d_scores, k)
    error = v - mm(k, entering)
    d_beta = jnp.sum(y * error, axis=1, keepdims=True) + jnp.sum(
        d_system * gram, axis=1, keepdims=True
    )
    by = beta * y
    d_gram = beta * d_system
    d_keys = (
        mm(d_scores, q, 0, 0)
        + mm(fresh, leaving)
        - mm(by, entering, 1, 1)
        + mm(d_gram, k)
        + mm(d_gram, k, 0, 0)
    )
    d_query = rq * (d_query - q * jnp.sum(d_query * q, axis=1, keepdims=True))
    d_keys = rk * (d_keys - k * jnp.sum(d_keys * k, axis=1, keepdims=True))
    d_logits = d_beta * beta * (1.0 - 0.5 * beta)
    l_first, l_second = unmix(d_logits)
    lane2 = lax.broadcasted_iota(jnp.int32, (ROWS, 2), 1)
    g_logits_f32 = jnp.where(lane2 == 0, l_first, l_second)
    g_query = d_query.astype(jnp.bfloat16)
    k_first, k_second = unmix(d_keys)
    v_first, v_second = unmix(by)
    g_keys = jnp.concatenate([k_first, k_second], axis=1).astype(jnp.bfloat16)
    g_values = jnp.concatenate([v_first, v_second], axis=1).astype(jnp.bfloat16)
    g_logits = g_logits_f32.astype(jnp.bfloat16)
    tiles_ref[:, :DH] = g_query
    tiles_ref[:, DH : 3 * DH] = g_keys
    tiles_ref[:, 3 * DH : 5 * DH] = g_values
    lane = lax.broadcasted_iota(jnp.int32, (ROWS, DH), 1)
    padded = jnp.where(lane == 0, l_first, jnp.where(lane == 1, l_second, 0.0))
    tiles_ref[:, 5 * DH :] = padded.astype(jnp.bfloat16)
    tiles_copy = pltpu.make_async_copy(tiles_ref, tiles_any, out_sems.at[0])
    tiles_copy.start()
    arrive[5].wait()
    wide = jnp.float32
    tiles = (g_query, g_keys[:, :DH], g_keys[:, DH:], g_values[:, :DH])
    shared = g_values[:, DH:].astype(wide)
    beta_rows = dot(g_logits, frames_ref[...], 0, 0)
    bias_row = jnp.sum(g_logits_f32, axis=0, keepdims=True)
    bias_lanes = jnp.where(
        lax.broadcasted_iota(jnp.int32, (1, DH), 1) == 0, bias_row[:, 0:1], bias_row[:, 1:2]
    )
    for i in range(PARTS):
        pieces_ref[i, :ROWS] = tiles[i].astype(wide)
        pieces_ref[i, ROWS : 2 * ROWS] = shared
        span = beta_rows[:, 256 * i : 256 * i + 256]
        pieces_ref[i, 2 * ROWS :] = jnp.concatenate(
            [span[:, :DH], span[:, DH:], bias_lanes, jnp.zeros((EXTRA - 5, DH), wide)], axis=0
        )
    pieces_copy = pltpu.make_async_copy(pieces_ref, pieces_any, out_sems.at[1])
    pieces_copy.start()
    tiles_copy.wait()
    pieces_copy.wait()


def f32(*shape):
    return jax.ShapeDtypeStruct(shape, jnp.float32)


SMEM = pl.BlockSpec(memory_space=pltpu.SMEM)
VMEM = pl.BlockSpec(memory_space=pltpu.VMEM)
ANY = pl.BlockSpec(memory_space=pl.ANY)
HBM = pl.BlockSpec(memory_space=pltpu.HBM)


def held(a):
    return pltpu.VMEM(a.shape, a.dtype)


def prepare(bias, w_beta, *large):
    kept, wide = f32(KEPT_SIZE, DH), f32(PARTS, ROWS, 1024)
    return pl.pallas_call(
        prepare_kernel,
        out_shape=(f32(3, DH, DH), kept, wide),
        in_specs=[SMEM, VMEM] + [HBM] * 5,
        out_specs=(VMEM, HBM, HBM),
        scratch_shapes=[held(a) for a in (*large, kept, f32(ROWS, 1024))]
        + [pltpu.SemaphoreType.DMA((5,)), pltpu.SemaphoreType.DMA((PARTS + 2,))],
        compiler_params=pltpu.CompilerParams(vmem_limit_bytes=LARGE_BYTES),
        name="prepare",
    )(bias, w_beta, *large)


def finish(place, *large):
    pieces = f32(PARTS, 2 * ROWS + EXTRA, DH)
    tiles = jax.ShapeDtypeStruct((ROWS, 6 * DH), jnp.bfloat16)
    return pl.pallas_call(
        finish_kernel,
        out_shape=(jax.ShapeDtypeStruct((ROWS, DH), jnp.bfloat16), pieces, tiles),
        in_specs=[SMEM] + [HBM] * 6,
        out_specs=(VMEM, HBM, HBM),
        scratch_shapes=[held(a) for a in (*large, pieces, tiles)]
        + [pltpu.SemaphoreType.DMA((6,)), pltpu.SemaphoreType.DMA((2,))],
        compiler_params=pltpu.CompilerParams(vmem_limit_bytes=FINISH_BYTES),
        name="finish",
    )(place, *large)


def side_kernel(
    tiles_any, wb_ref, wq_any, wk_any, wv_any, frames_any, part_any, narrow_any,
    tiles_ref, wq_ref, wk_ref, wv_ref, frames_ref, part_ref, narrow_ref, in_sems, out_sems,
):
    arrive = fetch(
        (
            (frames_any, frames_ref), (tiles_any, tiles_ref), (wq_any, wq_ref), (wk_any, wk_ref),
            (wv_any, wv_ref),
        ),
        in_sems,
    )
    arrive[0].wait()
    narrow_ref[...] = frames_ref[...].astype(jnp.bfloat16)
    out_copies = fetch([(narrow_ref, narrow_any)], out_sems)
    for copy in arrive[1:]:
        copy.wait()
    part = (
        dot(tiles_ref[:, :DH], wq_ref[...], 1, 1)
        + dot(tiles_ref[:, DH : 3 * DH], wk_ref[...], 1, 1)
        + dot(tiles_ref[:, 3 * DH : 5 * DH], wv_ref[...], 1, 1)
        + dot(tiles_ref[:, 5 * DH : 5 * DH + 2], wb_ref[...])
    )
    for i in range(8):
        part_ref[i] = part[:, DH * i : DH * i + DH]
    out_copies.append(pltpu.make_async_copy(part_ref, part_any, out_sems.at[1]))
    out_copies[1].start()
    for copy in out_copies:
        copy.wait()


def side(tiles, w_beta, *large):
    part = f32(8, ROWS, DH)
    narrow = jax.ShapeDtypeStruct((PARTS, ROWS, 1024), jnp.bfloat16)
    return pl.pallas_call(
        side_kernel,
        out_shape=(part, narrow),
        in_specs=[HBM, VMEM] + [HBM] * 4,
        out_specs=(HBM, HBM),
        scratch_shapes=[held(a) for a in (tiles, *large, part, narrow)]
        + [pltpu.SemaphoreType.DMA((5,)), pltpu.SemaphoreType.DMA((2,))],
        compiler_params=pltpu.CompilerParams(vmem_limit_bytes=SIDE_BYTES),
        cost_estimate=pl.CostEstimate(flops=170_000_000, bytes_accessed=6_000_000, transcendentals=0),
        name="side",
    )(tiles, w_beta, *large)


def weigh_kernel(place_ref, pieces_ref, frames_ref, sums_ref):
    quarter = pl.ds(pl.multiple_of(place_ref[0] * 256, 256), 256)
    total = jnp.zeros((1024, DH), jnp.float32)
    corner = jnp.zeros((256, DH), jnp.float32)
    extra = jnp.zeros((EXTRA, DH), jnp.float32)
    for i in range(PARTS):
        piece = pieces_ref[i, : 2 * ROWS].astype(jnp.bfloat16)
        extra = extra + pieces_ref[i, 2 * ROWS :]
        total = total + dot(frames_ref[i], piece[:ROWS], 0, 0)
        corner = corner + dot(frames_ref[i, :, quarter], piece[ROWS:], 0, 0)
    total = jnp.concatenate([total, corner], axis=0)
    rows = total.shape[0] // (PARTS * PARTS)
    for i in range(PARTS):
        for j in range(PARTS):
            block = PARTS * j + i
            sums_ref[i, rows * j : rows * j + rows] = total[rows * block : rows * block + rows]
        sums_ref[i, rows * PARTS :] = extra


def weigh(place, pieces, frames):
    return pl.pallas_call(
        weigh_kernel,
        out_shape=f32(PARTS, 1280 // PARTS + EXTRA, DH),
        in_specs=[SMEM, VMEM, VMEM],
        compiler_params=pltpu.CompilerParams(vmem_limit_bytes=SMALL_BYTES),
        name="weigh",
    )(place, pieces, frames)


def lay_kernel(whole_ref, query_any, keys_any, values_any, beta_ref, bias_ref, sems):
    left, right = pl.ds(0, DH), pl.ds(DH, DH)
    full = pl.ds(0, 1024)
    pairs = [
        (whole_ref.at[0, full], query_any),
        (whole_ref.at[1, full], keys_any.at[:, left]),
        (whole_ref.at[2, full], keys_any.at[:, right]),
        (whole_ref.at[3, full], values_any.at[:, left]),
    ]
    for i in range(PARTS):
        pairs.append(
            (whole_ref.at[i, pl.ds(1024, 256)], values_any.at[pl.ds(256 * i, 256), right])
        )
    copies = fetch(pairs, sems)
    rows = [whole_ref[i, 1280:] for i in range(PARTS)]
    beta_ref[...] = jnp.concatenate(
        [row[2 * half : 2 * half + 2] for row in rows for half in range(2)], axis=1
    )
    bias_ref[...] = rows[0][4:5, :2]
    for copy in copies:
        copy.wait()


def lay(whole):
    return pl.pallas_call(
        lay_kernel,
        out_shape=(
            f32(1024, DH), f32(1024, 2 * DH), f32(1024, 2 * DH), f32(2, 1024), f32(1, 2),
        ),
        in_specs=[VMEM],
        out_specs=(HBM, HBM, HBM, VMEM, VMEM),
        scratch_shapes=[pltpu.SemaphoreType.DMA((8,))],
        compiler_params=pltpu.CompilerParams(vmem_limit_bytes=SMALL_BYTES),
        name="lay",
    )(whole)


def spread(a, axis):
    return lax.all_to_all(jnp.broadcast_to(a[None], (PARTS, *a.shape)), axis, 0, 0, tiled=True)


def trade(a, axis):
    return lax.all_to_all(a, axis, 0, 0, tiled=True)


def local(frames, w_query, w_keys, w_values, w_beta, beta_bias, cotangent):
    place = jnp.stack([lax.axis_index("x"), lax.axis_index("zl"), lax.axis_index("zh")])
    beta_turned = w_beta.T
    own, kept, wide_frames = prepare(
        beta_bias, beta_turned, frames, w_keys, w_query, w_values, cotangent
    )
    row, wide_frames = lax.optimization_barrier((lax.all_gather(own, "x"), wide_frames))
    group_frames = trade(wide_frames, "x")
    total, own_around = group_scan(row, place, 0, DH)
    total, near_around = group_scan(lax.all_gather(total, "zl"), place, 1, DH // PARTS)
    far = lax.all_gather(lax.all_gather(total, "zh"), "x")
    far, group_frames = lax.optimization_barrier((far, group_frames))
    outputs, pieces, tiles = finish(place, far, near_around, own_around, kept, cotangent, frames)
    partial, group_frames = side(tiles, beta_turned, w_query, w_keys, w_values, group_frames)
    sums = weigh(place, trade(pieces, "x"), group_frames)
    part = jnp.sum(trade(sums, "zl"), axis=0)
    part, extra = part[:320], part[320:]
    part = jnp.concatenate(
        [part.reshape(PARTS, 80, DH), jnp.broadcast_to(extra[None], (PARTS, EXTRA, DH))], axis=1
    )
    part = jnp.sum(trade(part, "zh"), axis=0)
    part, extra = part[:80], part[80:]
    part, partial = lax.optimization_barrier((part, partial))
    partial = trade(partial, ("y", "core"))
    part = lax.all_gather(part, ("zh", "zl")).reshape(1280, DH)
    grad_frames = jnp.sum(partial, axis=0).astype(jnp.bfloat16)
    part, grad_frames = lax.optimization_barrier((part, grad_frames))
    whole = jnp.concatenate([part, extra], axis=0)
    grad_query, grad_keys, grad_values, beta_rows, bias_row = lay(spread(whole, "x"))
    grad_beta = beta_rows.T
    grad_bias = bias_row.reshape(2)
    return (outputs, grad_frames, grad_query, grad_keys, grad_values, grad_beta, grad_bias)


def solution(mesh):
    fine = Mesh(mesh.devices.reshape(4, 4, 4, 4, 2), ("zh", "zl", "x", "y", "core"))
    ctx, head = ("zh", "zl", "x"), ("y", "core")
    in_specs = (
        P(ctx, None),
        P(None, head),
        P(None, head),
        P(None, head),
        P(None, head),
        P(head),
        P(ctx, head),
    )
    out_specs = (
        P(ctx, head),
        P(ctx, head),
        P(None, head),
        P(None, head),
        P(None, head),
        P(None, head),
        P(head),
    )
    return jax.shard_map(local, mesh=fine, in_specs=in_specs, out_specs=out_specs, check_vma=False)
```

```python
import functools

import jax
import jax.numpy as jnp
from jax import lax
from jax.experimental import pallas as pl
from jax.experimental.pallas import tpu as pltpu
from jax.sharding import Mesh, PartitionSpec as P

DH = 128
ROWS = 128
HALF = 64
REFL = 256
PARTS = 4
KEPT_ROWS = (
    ("q", ROWS), ("k", REFL), ("v", REFL), ("w", REFL), ("u", REFL), ("qt", ROWS), ("pu", ROWS),
    ("cols", REFL),
)
KEPT, KEPT_PLACE, KEPT_SIZE = {}, {}, 0
for _name, _rows in KEPT_ROWS:
    KEPT[_name] = slice(KEPT_SIZE, KEPT_SIZE + _rows)
    KEPT_PLACE[_name] = pl.ds(KEPT_SIZE, _rows)
    KEPT_SIZE += _rows
EPS = 1e-06
EXTRA = 8
LARGE_BYTES = 63 * 1024 * 1024
SMALL_BYTES = 16 * 1024 * 1024


def halves(a):
    high = a.astype(jnp.bfloat16)
    return high, (a - high.astype(jnp.float32)).astype(jnp.bfloat16)


def dot(a, b, ca=1, cb=0):
    return lax.dot_general(a, b, (((ca,), (cb,)), ((), ())), preferred_element_type=jnp.float32)


def mm(a, b, ca=1, cb=0):
    return mm_halves(halves(a), halves(b), ca, cb)


def mm_halves(a, b, ca=1, cb=0):
    return dot(a[0], b[0], ca, cb) + (dot(a[0], b[1], ca, cb) + dot(a[1], b[0], ca, cb))


def mix(first, second):
    return jnp.concatenate([first[:HALF], second[:HALF], first[HALF:], second[HALF:]], axis=0)


def unmix(rows):
    first = jnp.concatenate([rows[:HALF], rows[ROWS : ROWS + HALF]], axis=0)
    second = jnp.concatenate([rows[HALF:ROWS], rows[ROWS + HALF :]], axis=0)
    return first, second


def place(shape, axis):
    row = lax.broadcasted_iota(jnp.int32, shape, axis)
    return (row & ROWS) + 2 * (row & (HALF - 1)) + ((row >> 6) & 1)


def seen_mask():
    frame = lax.broadcasted_iota(jnp.int32, (ROWS, REFL), 0)
    return (place((ROWS, REFL), 1) >> 1) <= frame


def fetch(pairs, sems):
    copies = [pltpu.make_async_copy(a, b, sems.at[i]) for i, (a, b) in enumerate(pairs)]
    for copy in copies:
        copy.start()
    return copies


def prepare_kernel(
    bias_ref, wb_ref, frames_any, wk_any, wq_any, wv_any, cot_any,
    send_any, kept_any, inner_any,
    frames_ref, wk_ref, wq_ref, wv_ref, cot_ref, send_ref, kept_ref, inner_ref, in_sems, out_sems,
):
    arrive = fetch(
        (
            (frames_any, frames_ref), (wk_any, wk_ref), (wq_any, wq_ref), (wv_any, wv_ref),
            (cot_any, cot_ref),
        ),
        in_sems,
    )

    def keep(name, value):
        kept_ref[KEPT[name], :] = value

    arrive[0].wait()
    frames = frames_ref[...]
    logits = dot(frames, wb_ref[...], 1, 1)
    arrive[1].wait()
    k_raw = dot(frames, wk_ref[...])
    for copy in arrive[2:]:
        copy.wait()
    q_raw = dot(frames, wq_ref[...])
    v_raw = dot(frames, wv_ref[...])
    rq = lax.rsqrt(jnp.sum(q_raw * q_raw, axis=1, keepdims=True) + EPS)
    q = q_raw * rq
    keys = mix(k_raw[:, :DH], k_raw[:, DH:])
    rk = lax.rsqrt(jnp.sum(keys * keys, axis=1, keepdims=True) + EPS)
    k = keys * rk
    v = mix(v_raw[:, :DH], v_raw[:, DH:])
    beta = 2.0 * jax.nn.sigmoid(mix(logits[:, 0:1] + bias_ref[0], logits[:, 1:2] + bias_ref[1]))
    keep("q", q)
    keep("k", k)
    keep("v", v)
    lane = lax.broadcasted_iota(jnp.int32, (REFL, DH), 1)
    rq_long = jnp.concatenate([rq, rq], axis=0)
    keep("cols", jnp.where(lane == 0, beta, jnp.where(lane == 1, rk, rq_long)))

    gram = mm(k, k, 1, 1)
    system = beta * gram
    row, col = place((ROWS, ROWS), 0), place((ROWS, ROWS), 1)
    parts = [system[:ROWS, :ROWS], system[ROWS:, ROWS:]]
    pair = ((row >> 1) == (col >> 1)) & (row > col)
    eye = jnp.where(row == col, 1.0, 0.0)
    inverse = [eye - jnp.where(pair, part, 0.0) for part in parts]
    for level in range(1, 7):
        lower = ((row >> (level + 1)) == (col >> (level + 1))) & ((row >> level) > (col >> level))
        inner = [mm(jnp.where(lower, part, 0.0), inv) for part, inv in zip(parts, inverse)]
        inverse = [inv - mm(inv, mid) for inv, mid in zip(inverse, inner)]
    corner = -mm(inverse[1], mm(system[ROWS:, :ROWS], inverse[0]))
    zero = jnp.zeros((ROWS, ROWS), jnp.float32)
    inverse = jnp.concatenate(
        [
            jnp.concatenate([inverse[0], zero], axis=1),
            jnp.concatenate([corner, inverse[1]], axis=1),
        ],
        axis=0,
    )
    inner_ref[:REFL] = inverse
    scores = jnp.where(seen_mask(), mm(q, k, 1, 1), 0.0)
    inner_ref[REFL:] = scores
    out_copies = fetch([(inner_ref, inner_any)], out_sems)
    wu = mm(inverse, jnp.concatenate([beta * k, beta * v], axis=1))
    w, u = wu[:, :DH], wu[:, DH:]
    keep("w", w)
    keep("u", u)
    kwu = mm(k, wu, 0, 0)
    pwu = mm(scores, wu)
    qt = q - pwu[:, :DH]
    keep("qt", qt)
    keep("pu", pwu[:, DH:])
    out_copies.append(pltpu.make_async_copy(kept_ref, kept_any, out_sems.at[1]))
    out_copies[-1].start()
    cot = cot_ref[...].astype(jnp.float32)
    send_ref[0] = eye_like() - kwu[:, :DH]
    send_ref[1] = kwu[:, DH:]
    send_ref[2] = mm(cot, qt, 0, 0)
    for i in range(PARTS):
        out_copies.append(pltpu.make_async_copy(send_ref, send_any.at[i], out_sems.at[2 + i]))
        out_copies[-1].start()
    for copy in out_copies:
        copy.wait()


def rest_kernel(
    inner_any, kept_any, cot_any, frames_any, late_any, wide_any,
    inner_ref, k_ref, cot_ref, frames_ref, late_ref, wide_ref, in_sems, out_sems,
):
    arrive = fetch(
        (
            (frames_any, frames_ref), (inner_any, inner_ref), (kept_any.at[KEPT_PLACE["k"]], k_ref),
            (cot_any, cot_ref),
        ),
        in_sems,
    )
    arrive[0].wait()
    wide_ref[...] = frames_ref[...].astype(jnp.float32)
    out_copies = fetch([(wide_ref, wide_any.at[i]) for i in range(PARTS)], out_sems)
    for copy in arrive[1:]:
        copy.wait()
    cot = cot_ref[...].astype(jnp.float32)
    pg = mm(inner_ref[REFL:], cot, 0, 0)
    zy = mm(inner_ref[:REFL], jnp.concatenate([k_ref[...], pg], axis=1), 0, 0)
    late_ref[:REFL] = zy[:, :DH]
    late_ref[REFL:] = zy[:, DH:]
    out_copies.append(pltpu.make_async_copy(late_ref, late_any, out_sems.at[PARTS]))
    out_copies[-1].start()
    for copy in out_copies:
        copy.wait()


def rest(inner, kept, cotangent, frames):
    late, wide = f32(2 * REFL, DH), f32(PARTS, ROWS, 1024)
    return pl.pallas_call(
        rest_kernel,
        out_shape=(late, wide),
        in_specs=[HBM] * 4,
        out_specs=(HBM, HBM),
        scratch_shapes=[
            held(a) for a in (inner, f32(REFL, DH), cotangent, frames, late, f32(ROWS, 1024))
        ]
        + [pltpu.SemaphoreType.DMA((4,)), pltpu.SemaphoreType.DMA((PARTS + 1,))],
        compiler_params=pltpu.CompilerParams(vmem_limit_bytes=LARGE_BYTES),
        cost_estimate=pl.CostEstimate(flops=170_000_000, bytes_accessed=6_000_000, transcendentals=0),
        name="rest",
    )(inner, kept, cotangent, frames)


def eye_like():
    row = lax.broadcasted_iota(jnp.int32, (DH, DH), 0)
    col = lax.broadcasted_iota(jnp.int32, (DH, DH), 1)
    return jnp.where(row == col, 1.0, 0.0)


def compose_group(me, parts):
    last = len(parts) - 1
    maps = [halves(part[0]) for part in parts]
    ahead = [jnp.concatenate([parts[0][0], parts[0][1]], axis=1)]
    behind = [jnp.concatenate([parts[last][0], parts[last][2]], axis=0)]
    for i in range(1, last + 1):
        moved = mm_halves(maps[i], halves(ahead[-1]))
        ahead.append(jnp.concatenate([moved[:, :DH], moved[:, DH:] + parts[i][1]], axis=1))
        j = last - i
        moved = mm_halves(halves(behind[-1]), maps[j])
        behind.append(jnp.concatenate([moved[:DH], moved[DH:] + parts[j][2]], axis=0))
    whole = (ahead[last][:, :DH], ahead[last][:, DH:], behind[last][DH:])
    eye, zero = eye_like(), jnp.zeros((DH, DH), jnp.float32)
    before = jnp.concatenate([eye, zero], axis=1)
    after = jnp.concatenate([eye, zero], axis=0)
    for i in range(last):
        before = jnp.where(me == i + 1, ahead[i], before)
        after = jnp.where(me == last - 1 - i, behind[i], after)
    return whole, (before[:, :DH], before[:, DH:], after[:DH], after[DH:])


def group_kernel(place_ref, parts_ref, total_ref, around_any, whole_ref, around_ref, sem, *, axis):
    parts = [tuple(parts_ref[i, j] for j in range(3)) for i in range(PARTS)]
    whole, around = compose_group(place_ref[axis], parts)
    for i, value in enumerate(around):
        around_ref[i] = value
    copy = pltpu.make_async_copy(around_ref, around_any, sem)
    copy.start()
    if total_ref.shape[1] == DH:
        for i, value in enumerate(whole):
            total_ref[i] = value
    else:
        for i, value in enumerate(whole):
            whole_ref[i] = value
        rows = DH // PARTS
        mine = pl.ds(pl.multiple_of(place_ref[0] * rows, rows), rows)
        for i in range(3):
            total_ref[i] = whole_ref[i, mine, :]
    copy.wait()


def group_scan(parts, place, axis, rows):
    return pl.pallas_call(
        functools.partial(group_kernel, axis=axis),
        out_shape=(f32(3, rows, DH), f32(4, DH, DH)),
        in_specs=[SMEM, VMEM],
        out_specs=(VMEM, HBM),
        scratch_shapes=[
            pltpu.VMEM((3, DH, DH), jnp.float32),
            pltpu.VMEM((4, DH, DH), jnp.float32),
            pltpu.SemaphoreType.DMA,
        ],
        compiler_params=pltpu.CompilerParams(vmem_limit_bytes=SMALL_BYTES),
        name="group_scan",
    )(place, parts)


def finish_kernel(
    place_ref, far_any, near_any, own_any, kept_any, late_any, cot_any, frames_any,
    out_ref, pieces_any, tiles_any,
    far_ref, near_ref, own_ref, kept_ref, late_ref, cot_ref, frames_ref, pieces_ref, tiles_ref,
    in_sems, out_sems,
):
    arrive = fetch(
        (
            (far_any, far_ref), (near_any, near_ref), (own_any, own_ref), (kept_any, kept_ref),
            (late_any, late_ref), (cot_any, cot_ref), (frames_any, frames_ref),
        ),
        in_sems,
    )
    me = place_ref[2]
    arrive[0].wait()
    count = PARTS

    def far(group, which):
        return jnp.concatenate([far_ref[group, i, which] for i in range(PARTS)], axis=0)

    entering = jnp.where(me > 0, far(0, 1), 0.0)
    for i in range(1, count - 1):
        entering = jnp.where(me > i, mm(far(i, 0), entering) + far(i, 1), entering)
    leaving = jnp.where(me < count - 1, far(count - 1, 2), 0.0)
    for i in range(count - 2, 0, -1):
        leaving = jnp.where(me < i, mm(leaving, far(i, 0)) + far(i, 2), leaving)
    for copy in arrive[1:6]:
        copy.wait()
    for around_ref in (near_ref, own_ref):
        entering = mm(around_ref[0], entering) + around_ref[1]
        leaving = mm(leaving, around_ref[2]) + around_ref[3]
    q, k, v = kept_ref[KEPT["q"], :], kept_ref[KEPT["k"], :], kept_ref[KEPT["v"], :]
    cot = cot_ref[...].astype(jnp.float32)
    cols = kept_ref[KEPT["cols"], :]
    beta, rk, rq = cols[:, 0:1], cols[:, 1:2], cols[:ROWS, 2:3]
    out_ref[...] = (mm(kept_ref[KEPT["qt"], :], entering) + kept_ref[KEPT["pu"], :]).astype(jnp.bfloat16)
    fresh = kept_ref[KEPT["u"], :] - mm(kept_ref[KEPT["w"], :], entering)
    y = late_ref[REFL:] + mm(late_ref[:REFL], leaving, 1, 1)
    gram = mm(k, k, 1, 1)
    row, col = place((REFL, REFL), 0), place((REFL, REFL), 1)
    d_system = jnp.where(row > col, -mm(y, fresh, 1, 1), 0.0)
    d_scores = jnp.where(seen_mask(), mm(cot, fresh, 1, 1), 0.0)
    d_query = mm(cot, entering, 1, 1) + mm(d_scores, k)
    error = v - mm(k, entering)
    d_beta = jnp.sum(y * error, axis=1, keepdims=True) + jnp.sum(
        d_system * gram, axis=1, keepdims=True
    )
    by = beta * y
    d_gram = beta * d_system
    d_keys = (
        mm(d_scores, q, 0, 0)
        + mm(fresh, leaving)
        - mm(by, entering, 1, 1)
        + mm(d_gram, k)
        + mm(d_gram, k, 0, 0)
    )
    d_query = rq * (d_query - q * jnp.sum(d_query * q, axis=1, keepdims=True))
    d_keys = rk * (d_keys - k * jnp.sum(d_keys * k, axis=1, keepdims=True))
    d_logits = d_beta * beta * (1.0 - 0.5 * beta)
    l_first, l_second = unmix(d_logits)
    lane2 = lax.broadcasted_iota(jnp.int32, (ROWS, 2), 1)
    g_logits_f32 = jnp.where(lane2 == 0, l_first, l_second)
    g_query = d_query.astype(jnp.bfloat16)
    k_first, k_second = unmix(d_keys)
    v_first, v_second = unmix(by)
    g_keys = jnp.concatenate([k_first, k_second], axis=1).astype(jnp.bfloat16)
    g_values = jnp.concatenate([v_first, v_second], axis=1).astype(jnp.bfloat16)
    g_logits = g_logits_f32.astype(jnp.bfloat16)
    tiles_ref[:, :DH] = g_query
    tiles_ref[:, DH : 3 * DH] = g_keys
    tiles_ref[:, 3 * DH : 5 * DH] = g_values
    lane = lax.broadcasted_iota(jnp.int32, (ROWS, DH), 1)
    padded = jnp.where(lane == 0, l_first, jnp.where(lane == 1, l_second, 0.0))
    tiles_ref[:, 5 * DH :] = padded.astype(jnp.bfloat16)
    tiles_copy = pltpu.make_async_copy(tiles_ref, tiles_any, out_sems.at[0])
    tiles_copy.start()
    arrive[6].wait()
    wide = jnp.float32
    tiles = (g_query, g_keys[:, :DH], g_keys[:, DH:], g_values[:, :DH])
    shared = g_values[:, DH:].astype(wide)
    beta_rows = dot(g_logits, frames_ref[...], 0, 0)
    bias_row = jnp.sum(g_logits_f32, axis=0, keepdims=True)
    bias_lanes = jnp.where(
        lax.broadcasted_iota(jnp.int32, (1, DH), 1) == 0, bias_row[:, 0:1], bias_row[:, 1:2]
    )
    for i in range(PARTS):
        pieces_ref[i, :ROWS] = tiles[i].astype(wide)
        pieces_ref[i, ROWS : 2 * ROWS] = shared
        span = beta_rows[:, 256 * i : 256 * i + 256]
        pieces_ref[i, 2 * ROWS :] = jnp.concatenate(
            [span[:, :DH], span[:, DH:], bias_lanes, jnp.zeros((EXTRA - 5, DH), wide)], axis=0
        )
    pieces_copy = pltpu.make_async_copy(pieces_ref, pieces_any, out_sems.at[1])
    pieces_copy.start()
    tiles_copy.wait()
    pieces_copy.wait()


def f32(*shape):
    return jax.ShapeDtypeStruct(shape, jnp.float32)


SMEM = pl.BlockSpec(memory_space=pltpu.SMEM)
VMEM = pl.BlockSpec(memory_space=pltpu.VMEM)
ANY = pl.BlockSpec(memory_space=pl.ANY)
HBM = pl.BlockSpec(memory_space=pltpu.HBM)


def held(a):
    return pltpu.VMEM(a.shape, a.dtype)


def prepare(bias, w_beta, *large):
    send, kept, inner = f32(3, DH, DH), f32(KEPT_SIZE, DH), f32(REFL + ROWS, REFL)
    return pl.pallas_call(
        prepare_kernel,
        out_shape=(f32(PARTS, 3, DH, DH), kept, inner),
        in_specs=[SMEM, VMEM] + [HBM] * 5,
        out_specs=(HBM, HBM, HBM),
        scratch_shapes=[held(a) for a in (*large, send, kept, inner)]
        + [pltpu.SemaphoreType.DMA((5,)), pltpu.SemaphoreType.DMA((PARTS + 2,))],
        compiler_params=pltpu.CompilerParams(vmem_limit_bytes=LARGE_BYTES),
        name="prepare",
    )(bias, w_beta, *large)


def finish(place, *large):
    pieces = f32(PARTS, 2 * ROWS + EXTRA, DH)
    tiles = jax.ShapeDtypeStruct((ROWS, 6 * DH), jnp.bfloat16)
    return pl.pallas_call(
        finish_kernel,
        out_shape=(jax.ShapeDtypeStruct((ROWS, DH), jnp.bfloat16), pieces, tiles),
        in_specs=[SMEM] + [HBM] * 7,
        out_specs=(VMEM, HBM, HBM),
        scratch_shapes=[held(a) for a in (*large, pieces, tiles)]
        + [pltpu.SemaphoreType.DMA((7,)), pltpu.SemaphoreType.DMA((2,))],
        compiler_params=pltpu.CompilerParams(vmem_limit_bytes=LARGE_BYTES),
        name="finish",
    )(place, *large)


def side_kernel(
    tiles_any, wb_ref, wq_any, wk_any, wv_any, frames_any, part_any, narrow_any,
    tiles_ref, wq_ref, wk_ref, wv_ref, frames_ref, part_ref, narrow_ref, in_sems, out_sems,
):
    arrive = fetch(
        (
            (frames_any, frames_ref), (tiles_any, tiles_ref), (wq_any, wq_ref), (wk_any, wk_ref),
            (wv_any, wv_ref),
        ),
        in_sems,
    )
    arrive[0].wait()
    narrow_ref[...] = frames_ref[...].astype(jnp.bfloat16)
    out_copies = fetch([(narrow_ref, narrow_any)], out_sems)
    for copy in arrive[1:]:
        copy.wait()
    part = (
        dot(tiles_ref[:, :DH], wq_ref[...], 1, 1)
        + dot(tiles_ref[:, DH : 3 * DH], wk_ref[...], 1, 1)
        + dot(tiles_ref[:, 3 * DH : 5 * DH], wv_ref[...], 1, 1)
        + dot(tiles_ref[:, 5 * DH : 5 * DH + 2], wb_ref[...])
    )
    for i in range(8):
        part_ref[i] = part[:, DH * i : DH * i + DH]
    out_copies.append(pltpu.make_async_copy(part_ref, part_any, out_sems.at[1]))
    out_copies[1].start()
    for copy in out_copies:
        copy.wait()


def side(tiles, w_beta, *large):
    part = f32(8, ROWS, DH)
    narrow = jax.ShapeDtypeStruct((PARTS, ROWS, 1024), jnp.bfloat16)
    return pl.pallas_call(
        side_kernel,
        out_shape=(part, narrow),
        in_specs=[HBM, VMEM] + [HBM] * 4,
        out_specs=(HBM, HBM),
        scratch_shapes=[held(a) for a in (tiles, *large, part, narrow)]
        + [pltpu.SemaphoreType.DMA((5,)), pltpu.SemaphoreType.DMA((2,))],
        compiler_params=pltpu.CompilerParams(vmem_limit_bytes=LARGE_BYTES),
        cost_estimate=pl.CostEstimate(flops=170_000_000, bytes_accessed=6_000_000, transcendentals=0),
        name="side",
    )(tiles, w_beta, *large)


def weigh_kernel(place_ref, pieces_ref, frames_ref, sums_ref):
    quarter = pl.ds(pl.multiple_of(place_ref[0] * 256, 256), 256)
    total = jnp.zeros((1024, DH), jnp.float32)
    corner = jnp.zeros((256, DH), jnp.float32)
    extra = jnp.zeros((EXTRA, DH), jnp.float32)
    for i in range(PARTS):
        piece = pieces_ref[i, : 2 * ROWS].astype(jnp.bfloat16)
        extra = extra + pieces_ref[i, 2 * ROWS :]
        total = total + dot(frames_ref[i], piece[:ROWS], 0, 0)
        corner = corner + dot(frames_ref[i, :, quarter], piece[ROWS:], 0, 0)
    total = jnp.concatenate([total, corner], axis=0)
    rows = total.shape[0] // (PARTS * PARTS)
    for i in range(PARTS):
        for j in range(PARTS):
            block = PARTS * j + i
            sums_ref[i, rows * j : rows * j + rows] = total[rows * block : rows * block + rows]
        sums_ref[i, rows * PARTS :] = extra


def weigh(place, pieces, frames):
    return pl.pallas_call(
        weigh_kernel,
        out_shape=f32(PARTS, 1280 // PARTS + EXTRA, DH),
        in_specs=[SMEM, VMEM, VMEM],
        compiler_params=pltpu.CompilerParams(vmem_limit_bytes=SMALL_BYTES),
        name="weigh",
    )(place, pieces, frames)


def lay_kernel(
    whole_ref, query_any, keys_any, values_any, beta_any, bias_any, beta_ref, bias_ref, sems
):
    left, right = pl.ds(0, DH), pl.ds(DH, DH)
    full = pl.ds(0, 1024)
    pairs = [
        (whole_ref.at[0, full], query_any),
        (whole_ref.at[1, full], keys_any.at[:, left]),
        (whole_ref.at[2, full], keys_any.at[:, right]),
        (whole_ref.at[3, full], values_any.at[:, left]),
    ]
    for i in range(PARTS):
        pairs.append(
            (whole_ref.at[i, pl.ds(1024, 256)], values_any.at[pl.ds(256 * i, 256), right])
        )
    copies = fetch(pairs, sems)
    rows = [whole_ref[i, 1280:] for i in range(PARTS)]
    beta_ref[...] = jnp.concatenate(
        [row[2 * half : 2 * half + 2] for row in rows for half in range(2)], axis=1
    )
    bias_ref[...] = rows[0][4:5, :2]
    for i, (a, b) in enumerate(((beta_ref, beta_any), (bias_ref, bias_any))):
        copies.append(pltpu.make_async_copy(a, b, sems.at[8 + i]))
        copies[-1].start()
    for copy in copies:
        copy.wait()


def lay(whole):
    return pl.pallas_call(
        lay_kernel,
        out_shape=(
            f32(1024, DH), f32(1024, 2 * DH), f32(1024, 2 * DH), f32(2, 1024), f32(1, 2),
        ),
        in_specs=[VMEM],
        out_specs=(HBM,) * 5,
        scratch_shapes=[held(f32(2, 1024)), held(f32(1, 2)), pltpu.SemaphoreType.DMA((10,))],
        compiler_params=pltpu.CompilerParams(vmem_limit_bytes=SMALL_BYTES),
        name="lay",
    )(whole)


def spread(a, axis):
    return lax.all_to_all(jnp.broadcast_to(a[None], (PARTS, *a.shape)), axis, 0, 0, tiled=True)


def trade(a, axis):
    return lax.all_to_all(a, axis, 0, 0, tiled=True)


def local(frames, w_query, w_keys, w_values, w_beta, beta_bias, cotangent):
    place = jnp.stack([lax.axis_index("x"), lax.axis_index("zl"), lax.axis_index("zh")])
    beta_turned = w_beta.T
    own, kept, inner = prepare(
        beta_bias, beta_turned, frames, w_keys, w_query, w_values, cotangent
    )
    late, wide_frames = rest(inner, kept, cotangent, frames)
    row, wide_frames, late = lax.optimization_barrier((trade(own, "x"), wide_frames, late))
    group_frames = trade(wide_frames, "x")
    total, own_around = group_scan(row, place, 0, DH)
    total, near_around = group_scan(lax.all_gather(total, "zl"), place, 1, DH // PARTS)
    far = lax.all_gather(total, ("zh", "x")).reshape(PARTS, PARTS, 3, DH // PARTS, DH)
    far, group_frames = lax.optimization_barrier((far, group_frames))
    outputs, pieces, tiles = finish(
        place, far, near_around, own_around, kept, late, cotangent, frames
    )
    partial, group_frames = side(tiles, beta_turned, w_query, w_keys, w_values, group_frames)
    sums = weigh(place, trade(pieces, "x"), group_frames)
    part = jnp.sum(trade(sums, "zl"), axis=0)
    part, extra = part[:320], part[320:]
    part = jnp.concatenate(
        [part.reshape(PARTS, 80, DH), jnp.broadcast_to(extra[None], (PARTS, EXTRA, DH))], axis=1
    )
    part = jnp.sum(trade(part, "zh"), axis=0)
    part, extra = part[:80], part[80:]
    part, partial = lax.optimization_barrier((part, partial))
    partial = trade(partial, ("y", "core"))
    part = lax.all_gather(part, ("zh", "zl")).reshape(1280, DH)
    grad_frames = jnp.sum(partial, axis=0).astype(jnp.bfloat16)
    part, grad_frames = lax.optimization_barrier((part, grad_frames))
    whole = jnp.concatenate([part, extra], axis=0)
    grad_query, grad_keys, grad_values, beta_rows, bias_row = lay(spread(whole, "x"))
    grad_beta = beta_rows.T
    grad_bias = bias_row.reshape(2)
    return (outputs, grad_frames, grad_query, grad_keys, grad_values, grad_beta, grad_bias)


def solution(mesh):
    fine = Mesh(mesh.devices.reshape(4, 4, 4, 4, 2), ("zh", "zl", "x", "y", "core"))
    ctx, head = ("zh", "zl", "x"), ("y", "core")
    in_specs = (
        P(ctx, None),
        P(None, head),
        P(None, head),
        P(None, head),
        P(None, head),
        P(head),
        P(ctx, head),
    )
    out_specs = (
        P(ctx, head),
        P(ctx, head),
        P(None, head),
        P(None, head),
        P(None, head),
        P(None, head),
        P(head),
    )
    return jax.shard_map(local, mesh=fine, in_specs=in_specs, out_specs=out_specs, check_vma=False)
```

```python
import functools

import jax
import jax.numpy as jnp
from jax import lax
from jax.experimental import pallas as pl
from jax.experimental.pallas import tpu as pltpu
from jax.sharding import Mesh, PartitionSpec as P

DH = 128
ROWS = 128
HALF = 64
REFL = 256
PARTS = 4
KEPT_ROWS = (
    ("q", ROWS), ("k", REFL), ("v", REFL), ("w", REFL), ("u", REFL), ("qt", ROWS), ("pu", ROWS),
    ("cols", REFL),
)
KEPT, KEPT_PLACE, KEPT_SIZE = {}, {}, 0
for _name, _rows in KEPT_ROWS:
    KEPT[_name] = slice(KEPT_SIZE, KEPT_SIZE + _rows)
    KEPT_PLACE[_name] = pl.ds(KEPT_SIZE, _rows)
    KEPT_SIZE += _rows
EPS = 1e-06
EXTRA = 8
LARGE_BYTES = 63 * 1024 * 1024
SMALL_BYTES = 16 * 1024 * 1024


def halves(a):
    high = a.astype(jnp.bfloat16)
    return high, (a - high.astype(jnp.float32)).astype(jnp.bfloat16)


def dot(a, b, ca=1, cb=0):
    return lax.dot_general(a, b, (((ca,), (cb,)), ((), ())), preferred_element_type=jnp.float32)


def mm(a, b, ca=1, cb=0):
    return mm_halves(halves(a), halves(b), ca, cb)


def mm_halves(a, b, ca=1, cb=0):
    return dot(a[0], b[0], ca, cb) + (dot(a[0], b[1], ca, cb) + dot(a[1], b[0], ca, cb))


def mix(first, second):
    return jnp.concatenate([first[:HALF], second[:HALF], first[HALF:], second[HALF:]], axis=0)


def unmix(rows):
    first = jnp.concatenate([rows[:HALF], rows[ROWS : ROWS + HALF]], axis=0)
    second = jnp.concatenate([rows[HALF:ROWS], rows[ROWS + HALF :]], axis=0)
    return first, second


def place(shape, axis):
    row = lax.broadcasted_iota(jnp.int32, shape, axis)
    return (row & ROWS) + 2 * (row & (HALF - 1)) + ((row >> 6) & 1)


def seen_mask():
    frame = lax.broadcasted_iota(jnp.int32, (ROWS, REFL), 0)
    return (place((ROWS, REFL), 1) >> 1) <= frame


def fetch(pairs, sems):
    copies = [pltpu.make_async_copy(a, b, sems.at[i]) for i, (a, b) in enumerate(pairs)]
    for copy in copies:
        copy.start()
    return copies


def prepare_kernel(
    bias_ref, wb_ref, frames_any, wk_any, wq_any, wv_any, cot_any,
    send_any, kept_any, inner_any,
    frames_ref, wk_ref, wq_ref, wv_ref, cot_ref, send_ref, kept_ref, inner_ref, in_sems, out_sems,
):
    arrive = fetch(
        (
            (frames_any, frames_ref), (wk_any, wk_ref), (wq_any, wq_ref), (wv_any, wv_ref),
            (cot_any, cot_ref),
        ),
        in_sems,
    )

    def keep(name, value):
        kept_ref[KEPT[name], :] = value

    arrive[0].wait()
    frames = frames_ref[...]
    logits = dot(frames, wb_ref[...], 1, 1)
    arrive[1].wait()
    k_raw = dot(frames, wk_ref[...])
    for copy in arrive[2:]:
        copy.wait()
    q_raw = dot(frames, wq_ref[...])
    v_raw = dot(frames, wv_ref[...])
    rq = lax.rsqrt(jnp.sum(q_raw * q_raw, axis=1, keepdims=True) + EPS)
    q = q_raw * rq
    keys = mix(k_raw[:, :DH], k_raw[:, DH:])
    rk = lax.rsqrt(jnp.sum(keys * keys, axis=1, keepdims=True) + EPS)
    k = keys * rk
    v = mix(v_raw[:, :DH], v_raw[:, DH:])
    beta = 2.0 * jax.nn.sigmoid(mix(logits[:, 0:1] + bias_ref[0], logits[:, 1:2] + bias_ref[1]))
    keep("q", q)
    keep("k", k)
    keep("v", v)
    lane = lax.broadcasted_iota(jnp.int32, (REFL, DH), 1)
    rq_long = jnp.concatenate([rq, rq], axis=0)
    keep("cols", jnp.where(lane == 0, beta, jnp.where(lane == 1, rk, rq_long)))

    gram = mm(k, k, 1, 1)
    system = beta * gram
    row, col = place((ROWS, ROWS), 0), place((ROWS, ROWS), 1)
    parts = [system[:ROWS, :ROWS], system[ROWS:, ROWS:]]
    pair = ((row >> 1) == (col >> 1)) & (row > col)
    eye = jnp.where(row == col, 1.0, 0.0)
    inverse = [eye - jnp.where(pair, part, 0.0) for part in parts]
    for level in range(1, 7):
        lower = ((row >> (level + 1)) == (col >> (level + 1))) & ((row >> level) > (col >> level))
        inner = [mm(jnp.where(lower, part, 0.0), inv) for part, inv in zip(parts, inverse)]
        inverse = [inv - mm(inv, mid) for inv, mid in zip(inverse, inner)]
    corner = -mm(inverse[1], mm(system[ROWS:, :ROWS], inverse[0]))
    zero = jnp.zeros((ROWS, ROWS), jnp.float32)
    inverse = jnp.concatenate(
        [
            jnp.concatenate([inverse[0], zero], axis=1),
            jnp.concatenate([corner, inverse[1]], axis=1),
        ],
        axis=0,
    )
    inner_ref[:REFL] = inverse
    scores = jnp.where(seen_mask(), mm(q, k, 1, 1), 0.0)
    inner_ref[REFL:] = scores
    out_copies = fetch([(inner_ref, inner_any)], out_sems)
    wu = mm(inverse, jnp.concatenate([beta * k, beta * v], axis=1))
    w, u = wu[:, :DH], wu[:, DH:]
    keep("w", w)
    keep("u", u)
    kwu = mm(k, wu, 0, 0)
    pwu = mm(scores, wu)
    qt = q - pwu[:, :DH]
    keep("qt", qt)
    keep("pu", pwu[:, DH:])
    out_copies.append(pltpu.make_async_copy(kept_ref, kept_any, out_sems.at[1]))
    out_copies[-1].start()
    cot = cot_ref[...].astype(jnp.float32)
    send_ref[0] = eye_like() - kwu[:, :DH]
    send_ref[1] = kwu[:, DH:]
    send_ref[2] = mm(cot, qt, 0, 0)
    for i in range(PARTS):
        out_copies.append(pltpu.make_async_copy(send_ref, send_any.at[i], out_sems.at[2 + i]))
        out_copies[-1].start()
    for copy in out_copies:
        copy.wait()


def rest_kernel(
    inner_any, kept_any, cot_any, frames_any, late_any, wide_any,
    inner_ref, k_ref, cot_ref, frames_ref, late_ref, wide_ref, in_sems, out_sems,
):
    arrive = fetch(
        (
            (frames_any, frames_ref), (inner_any, inner_ref), (kept_any.at[KEPT_PLACE["k"]], k_ref),
            (cot_any, cot_ref),
        ),
        in_sems,
    )
    arrive[0].wait()
    wide_ref[...] = frames_ref[...].astype(jnp.float32)
    out_copies = fetch([(wide_ref, wide_any.at[i]) for i in range(PARTS)], out_sems)
    for copy in arrive[1:]:
        copy.wait()
    cot = cot_ref[...].astype(jnp.float32)
    pg = mm(inner_ref[REFL:], cot, 0, 0)
    zy = mm(inner_ref[:REFL], jnp.concatenate([k_ref[...], pg], axis=1), 0, 0)
    late_ref[:REFL] = zy[:, :DH]
    late_ref[REFL:] = zy[:, DH:]
    out_copies.append(pltpu.make_async_copy(late_ref, late_any, out_sems.at[PARTS]))
    out_copies[-1].start()
    for copy in out_copies:
        copy.wait()


def rest(inner, kept, cotangent, frames):
    late, wide = f32(2 * REFL, DH), f32(PARTS, ROWS, 1024)
    return pl.pallas_call(
        rest_kernel,
        out_shape=(late, wide),
        in_specs=[HBM] * 4,
        out_specs=(HBM, HBM),
        scratch_shapes=[
            held(a) for a in (inner, f32(REFL, DH), cotangent, frames, late, f32(ROWS, 1024))
        ]
        + [pltpu.SemaphoreType.DMA((4,)), pltpu.SemaphoreType.DMA((PARTS + 1,))],
        compiler_params=pltpu.CompilerParams(vmem_limit_bytes=LARGE_BYTES),
        cost_estimate=pl.CostEstimate(flops=170_000_000, bytes_accessed=6_000_000, transcendentals=0),
        name="rest",
    )(inner, kept, cotangent, frames)


def eye_like():
    row = lax.broadcasted_iota(jnp.int32, (DH, DH), 0)
    col = lax.broadcasted_iota(jnp.int32, (DH, DH), 1)
    return jnp.where(row == col, 1.0, 0.0)


def compose_group(me, parts):
    last = len(parts) - 1
    maps = [halves(part[0]) for part in parts]
    ahead = [jnp.concatenate([parts[0][0], parts[0][1]], axis=1)]
    behind = [jnp.concatenate([parts[last][0], parts[last][2]], axis=0)]
    for i in range(1, last + 1):
        moved = mm_halves(maps[i], halves(ahead[-1]))
        ahead.append(jnp.concatenate([moved[:, :DH], moved[:, DH:] + parts[i][1]], axis=1))
        j = last - i
        moved = mm_halves(halves(behind[-1]), maps[j])
        behind.append(jnp.concatenate([moved[:DH], moved[DH:] + parts[j][2]], axis=0))
    whole = (ahead[last][:, :DH], ahead[last][:, DH:], behind[last][DH:])
    eye, zero = eye_like(), jnp.zeros((DH, DH), jnp.float32)
    before = jnp.concatenate([eye, zero], axis=1)
    after = jnp.concatenate([eye, zero], axis=0)
    for i in range(last):
        before = jnp.where(me == i + 1, ahead[i], before)
        after = jnp.where(me == last - 1 - i, behind[i], after)
    return whole, (before[:, :DH], before[:, DH:], after[:DH], after[DH:])


def group_kernel(place_ref, parts_ref, total_ref, around_any, whole_ref, around_ref, sem, *, axis):
    parts = [tuple(parts_ref[i, j] for j in range(3)) for i in range(PARTS)]
    whole, around = compose_group(place_ref[axis], parts)
    for i, value in enumerate(around):
        around_ref[i] = value
    copy = pltpu.make_async_copy(around_ref, around_any, sem)
    copy.start()
    if total_ref.shape[1] == DH:
        for i, value in enumerate(whole):
            total_ref[i] = value
    else:
        for i, value in enumerate(whole):
            whole_ref[i] = value
        rows = DH // PARTS
        mine = pl.ds(pl.multiple_of(place_ref[0] * rows, rows), rows)
        for i in range(3):
            total_ref[i] = whole_ref[i, mine, :]
    copy.wait()


def group_scan(parts, place, axis, rows):
    return pl.pallas_call(
        functools.partial(group_kernel, axis=axis),
        out_shape=(f32(3, rows, DH), f32(4, DH, DH)),
        in_specs=[SMEM, VMEM],
        out_specs=(VMEM, HBM),
        scratch_shapes=[
            pltpu.VMEM((3, DH, DH), jnp.float32),
            pltpu.VMEM((4, DH, DH), jnp.float32),
            pltpu.SemaphoreType.DMA,
        ],
        compiler_params=pltpu.CompilerParams(vmem_limit_bytes=SMALL_BYTES),
        name="group_scan",
    )(place, parts)


def finish_kernel(
    place_ref, far_any, near_any, own_any, kept_any, late_any, cot_any, frames_any,
    out_ref, pieces_any, tiles_any,
    far_ref, near_ref, own_ref, kept_ref, late_ref, cot_ref, frames_ref, pieces_ref, tiles_ref,
    in_sems, out_sems,
):
    arrive = fetch(
        (
            (far_any, far_ref), (near_any, near_ref), (own_any, own_ref), (kept_any, kept_ref),
            (late_any, late_ref), (cot_any, cot_ref), (frames_any, frames_ref),
        ),
        in_sems,
    )
    me = place_ref[2]
    for copy in arrive[:6]:
        copy.wait()
    inward = mm(own_ref[0], jnp.concatenate([near_ref[0], near_ref[1]], axis=1))
    inward_map, inward_shift = inward[:, :DH], inward[:, DH:] + own_ref[1]
    outward = mm(jnp.concatenate([near_ref[2], near_ref[3]], axis=0), own_ref[2])
    outward_map, outward_shift = outward[:DH], outward[DH:] + own_ref[3]

    def far(group, which):
        return jnp.concatenate([far_ref[i, group, which] for i in range(PARTS)], axis=0)

    entering = jnp.where(me > 0, far(0, 1), 0.0)
    leaving = jnp.where(me < PARTS - 1, far(PARTS - 1, 2), 0.0)
    for i in range(1, PARTS - 1):
        j = PARTS - 1 - i
        entering = jnp.where(me > i, mm(far(i, 0), entering) + far(i, 1), entering)
        leaving = jnp.where(me < j, mm(leaving, far(j, 0)) + far(j, 2), leaving)
    entering = mm(inward_map, entering) + inward_shift
    leaving = mm(leaving, outward_map) + outward_shift
    q, k, v = kept_ref[KEPT["q"], :], kept_ref[KEPT["k"], :], kept_ref[KEPT["v"], :]
    cot = cot_ref[...].astype(jnp.float32)
    cols = kept_ref[KEPT["cols"], :]
    beta, rk, rq = cols[:, 0:1], cols[:, 1:2], cols[:ROWS, 2:3]
    out_ref[...] = (mm(kept_ref[KEPT["qt"], :], entering) + kept_ref[KEPT["pu"], :]).astype(jnp.bfloat16)
    fresh = kept_ref[KEPT["u"], :] - mm(kept_ref[KEPT["w"], :], entering)
    y = late_ref[REFL:] + mm(late_ref[:REFL], leaving, 1, 1)
    gram = mm(k, k, 1, 1)
    row, col = place((REFL, REFL), 0), place((REFL, REFL), 1)
    d_system = jnp.where(row > col, -mm(y, fresh, 1, 1), 0.0)
    d_scores = jnp.where(seen_mask(), mm(cot, fresh, 1, 1), 0.0)
    d_query = mm(cot, entering, 1, 1) + mm(d_scores, k)
    error = v - mm(k, entering)
    d_beta = jnp.sum(y * error, axis=1, keepdims=True) + jnp.sum(
        d_system * gram, axis=1, keepdims=True
    )
    by = beta * y
    d_gram = beta * d_system
    d_keys = (
        mm(d_scores, q, 0, 0)
        + mm(fresh, leaving)
        - mm(by, entering, 1, 1)
        + mm(d_gram, k)
        + mm(d_gram, k, 0, 0)
    )
    d_query = rq * (d_query - q * jnp.sum(d_query * q, axis=1, keepdims=True))
    d_keys = rk * (d_keys - k * jnp.sum(d_keys * k, axis=1, keepdims=True))
    d_logits = d_beta * beta * (1.0 - 0.5 * beta)
    l_first, l_second = unmix(d_logits)
    lane2 = lax.broadcasted_iota(jnp.int32, (ROWS, 2), 1)
    g_logits_f32 = jnp.where(lane2 == 0, l_first, l_second)
    g_query = d_query.astype(jnp.bfloat16)
    k_first, k_second = unmix(d_keys)
    v_first, v_second = unmix(by)
    g_keys = jnp.concatenate([k_first, k_second], axis=1).astype(jnp.bfloat16)
    g_values = jnp.concatenate([v_first, v_second], axis=1).astype(jnp.bfloat16)
    g_logits = g_logits_f32.astype(jnp.bfloat16)
    tiles_ref[:, :DH] = g_query
    tiles_ref[:, DH : 3 * DH] = g_keys
    tiles_ref[:, 3 * DH : 5 * DH] = g_values
    lane = lax.broadcasted_iota(jnp.int32, (ROWS, DH), 1)
    padded = jnp.where(lane == 0, l_first, jnp.where(lane == 1, l_second, 0.0))
    tiles_ref[:, 5 * DH :] = padded.astype(jnp.bfloat16)
    tiles_copy = pltpu.make_async_copy(tiles_ref, tiles_any, out_sems.at[0])
    tiles_copy.start()
    arrive[6].wait()
    wide = jnp.float32
    tiles = (g_query, g_keys[:, :DH], g_keys[:, DH:], g_values[:, :DH])
    shared = g_values[:, DH:].astype(wide)
    beta_rows = dot(g_logits, frames_ref[...], 0, 0)
    bias_row = jnp.sum(g_logits_f32, axis=0, keepdims=True)
    bias_lanes = jnp.where(
        lax.broadcasted_iota(jnp.int32, (1, DH), 1) == 0, bias_row[:, 0:1], bias_row[:, 1:2]
    )
    for i in range(PARTS):
        pieces_ref[i, :ROWS] = tiles[i].astype(wide)
        pieces_ref[i, ROWS : 2 * ROWS] = shared
        span = beta_rows[:, 256 * i : 256 * i + 256]
        pieces_ref[i, 2 * ROWS :] = jnp.concatenate(
            [span[:, :DH], span[:, DH:], bias_lanes, jnp.zeros((EXTRA - 5, DH), wide)], axis=0
        )
    pieces_copy = pltpu.make_async_copy(pieces_ref, pieces_any, out_sems.at[1])
    pieces_copy.start()
    tiles_copy.wait()
    pieces_copy.wait()


def f32(*shape):
    return jax.ShapeDtypeStruct(shape, jnp.float32)


SMEM = pl.BlockSpec(memory_space=pltpu.SMEM)
VMEM = pl.BlockSpec(memory_space=pltpu.VMEM)
ANY = pl.BlockSpec(memory_space=pl.ANY)
HBM = pl.BlockSpec(memory_space=pltpu.HBM)


def held(a):
    return pltpu.VMEM(a.shape, a.dtype)


def prepare(bias, w_beta, *large):
    send, kept, inner = f32(3, DH, DH), f32(KEPT_SIZE, DH), f32(REFL + ROWS, REFL)
    return pl.pallas_call(
        prepare_kernel,
        out_shape=(f32(PARTS, 3, DH, DH), kept, inner),
        in_specs=[SMEM, VMEM] + [HBM] * 5,
        out_specs=(HBM, HBM, HBM),
        scratch_shapes=[held(a) for a in (*large, send, kept, inner)]
        + [pltpu.SemaphoreType.DMA((5,)), pltpu.SemaphoreType.DMA((PARTS + 2,))],
        compiler_params=pltpu.CompilerParams(vmem_limit_bytes=LARGE_BYTES),
        name="prepare",
    )(bias, w_beta, *large)


def finish(place, *large):
    pieces = f32(PARTS, 2 * ROWS + EXTRA, DH)
    tiles = jax.ShapeDtypeStruct((ROWS, 6 * DH), jnp.bfloat16)
    return pl.pallas_call(
        finish_kernel,
        out_shape=(jax.ShapeDtypeStruct((ROWS, DH), jnp.bfloat16), pieces, tiles),
        in_specs=[SMEM] + [HBM] * 7,
        out_specs=(VMEM, HBM, HBM),
        scratch_shapes=[held(a) for a in (*large, pieces, tiles)]
        + [pltpu.SemaphoreType.DMA((7,)), pltpu.SemaphoreType.DMA((2,))],
        compiler_params=pltpu.CompilerParams(vmem_limit_bytes=LARGE_BYTES),
        name="finish",
    )(place, *large)


def side_kernel(
    tiles_any, wb_ref, wq_any, wk_any, wv_any, frames_any, part_any, narrow_any,
    tiles_ref, wq_ref, wk_ref, wv_ref, frames_ref, part_ref, narrow_ref, in_sems, out_sems,
):
    arrive = fetch(
        (
            (frames_any, frames_ref), (tiles_any, tiles_ref), (wq_any, wq_ref), (wk_any, wk_ref),
            (wv_any, wv_ref),
        ),
        in_sems,
    )
    arrive[0].wait()
    narrow_ref[...] = frames_ref[...].astype(jnp.bfloat16)
    out_copies = fetch([(narrow_ref, narrow_any)], out_sems)
    for copy in arrive[1:]:
        copy.wait()
    part = (
        dot(tiles_ref[:, :DH], wq_ref[...], 1, 1)
        + dot(tiles_ref[:, DH : 3 * DH], wk_ref[...], 1, 1)
        + dot(tiles_ref[:, 3 * DH : 5 * DH], wv_ref[...], 1, 1)
        + dot(tiles_ref[:, 5 * DH : 5 * DH + 2], wb_ref[...])
    )
    for i in range(8):
        part_ref[i] = part[:, DH * i : DH * i + DH]
    out_copies.append(pltpu.make_async_copy(part_ref, part_any, out_sems.at[1]))
    out_copies[1].start()
    for copy in out_copies:
        copy.wait()


def side(tiles, w_beta, *large):
    part = f32(8, ROWS, DH)
    narrow = jax.ShapeDtypeStruct((PARTS, ROWS, 1024), jnp.bfloat16)
    return pl.pallas_call(
        side_kernel,
        out_shape=(part, narrow),
        in_specs=[HBM, VMEM] + [HBM] * 4,
        out_specs=(HBM, HBM),
        scratch_shapes=[held(a) for a in (tiles, *large, part, narrow)]
        + [pltpu.SemaphoreType.DMA((5,)), pltpu.SemaphoreType.DMA((2,))],
        compiler_params=pltpu.CompilerParams(vmem_limit_bytes=LARGE_BYTES),
        cost_estimate=pl.CostEstimate(flops=170_000_000, bytes_accessed=6_000_000, transcendentals=0),
        name="side",
    )(tiles, w_beta, *large)


def weigh_kernel(place_ref, pieces_ref, frames_ref, sums_ref):
    quarter = pl.ds(pl.multiple_of(place_ref[0] * 256, 256), 256)
    total = jnp.zeros((1024, DH), jnp.float32)
    corner = jnp.zeros((256, DH), jnp.float32)
    extra = jnp.zeros((EXTRA, DH), jnp.float32)
    for i in range(PARTS):
        piece = pieces_ref[i, : 2 * ROWS].astype(jnp.bfloat16)
        extra = extra + pieces_ref[i, 2 * ROWS :]
        total = total + dot(frames_ref[i], piece[:ROWS], 0, 0)
        corner = corner + dot(frames_ref[i, :, quarter], piece[ROWS:], 0, 0)
    total = jnp.concatenate([total, corner], axis=0)
    rows = total.shape[0] // (PARTS * PARTS)
    for i in range(PARTS):
        for j in range(PARTS):
            block = PARTS * j + i
            sums_ref[i, rows * j : rows * j + rows] = total[rows * block : rows * block + rows]
        sums_ref[i, rows * PARTS :] = extra


def weigh(place, pieces, frames):
    return pl.pallas_call(
        weigh_kernel,
        out_shape=f32(PARTS, 1280 // PARTS + EXTRA, DH),
        in_specs=[SMEM, VMEM, VMEM],
        compiler_params=pltpu.CompilerParams(vmem_limit_bytes=SMALL_BYTES),
        name="weigh",
    )(place, pieces, frames)


def lay_kernel(
    whole_ref, heads_ref, query_any, keys_any, values_any, beta_any, bias_any, frames_any,
    beta_ref, bias_ref, sum_ref, sems,
):
    left, right = pl.ds(0, DH), pl.ds(DH, DH)
    full = pl.ds(0, 1024)
    pairs = [
        (whole_ref.at[0, full], query_any),
        (whole_ref.at[1, full], keys_any.at[:, left]),
        (whole_ref.at[2, full], keys_any.at[:, right]),
        (whole_ref.at[3, full], values_any.at[:, left]),
    ]
    for i in range(PARTS):
        pairs.append(
            (whole_ref.at[i, pl.ds(1024, 256)], values_any.at[pl.ds(256 * i, 256), right])
        )
    copies = fetch(pairs, sems)
    rows = [whole_ref[i, 1280:] for i in range(PARTS)]
    beta_ref[...] = jnp.concatenate(
        [row[2 * half : 2 * half + 2] for row in rows for half in range(2)], axis=1
    )
    bias_ref[...] = rows[0][4:5, :2]
    total = heads_ref[0]
    for i in range(1, heads_ref.shape[0]):
        total = total + heads_ref[i]
    sum_ref[...] = total.astype(jnp.bfloat16)
    small = ((beta_ref, beta_any), (bias_ref, bias_any), (sum_ref, frames_any))
    for i, (a, b) in enumerate(small):
        copies.append(pltpu.make_async_copy(a, b, sems.at[8 + i]))
        copies[-1].start()
    for copy in copies:
        copy.wait()


def lay(whole, heads):
    frames = jax.ShapeDtypeStruct((ROWS, DH), jnp.bfloat16)
    return pl.pallas_call(
        lay_kernel,
        out_shape=(
            f32(1024, DH), f32(1024, 2 * DH), f32(1024, 2 * DH), f32(2, 1024), f32(1, 2), frames,
        ),
        in_specs=[VMEM, VMEM],
        out_specs=(HBM,) * 6,
        scratch_shapes=[
            held(f32(2, 1024)), held(f32(1, 2)), held(frames), pltpu.SemaphoreType.DMA((11,)),
        ],
        compiler_params=pltpu.CompilerParams(vmem_limit_bytes=SMALL_BYTES),
        name="lay",
    )(whole, heads)


def spread(a, axis):
    return lax.all_to_all(jnp.broadcast_to(a[None], (PARTS, *a.shape)), axis, 0, 0, tiled=True)


def trade(a, axis):
    return lax.all_to_all(a, axis, 0, 0, tiled=True)


def local(frames, w_query, w_keys, w_values, w_beta, beta_bias, cotangent):
    place = jnp.stack([lax.axis_index("x"), lax.axis_index("zl"), lax.axis_index("zh")])
    beta_turned = w_beta.T
    own, kept, inner = prepare(
        beta_bias, beta_turned, frames, w_keys, w_query, w_values, cotangent
    )
    late, wide_frames = rest(inner, kept, cotangent, frames)
    row, wide_frames, late = lax.optimization_barrier((trade(own, "x"), wide_frames, late))
    group_frames = trade(wide_frames, "x")
    total, own_around = group_scan(row, place, 0, DH)
    total, near_around = group_scan(lax.all_gather(total, "zl"), place, 1, DH // PARTS)
    far = lax.all_gather(lax.all_gather(total, "zh"), "x")
    far, group_frames = lax.optimization_barrier((far, group_frames))
    outputs, pieces, tiles = finish(
        place, far, near_around, own_around, kept, late, cotangent, frames
    )
    partial, group_frames = side(tiles, beta_turned, w_query, w_keys, w_values, group_frames)
    sums = weigh(place, trade(pieces, "x"), group_frames)
    part = jnp.sum(trade(sums, "zl"), axis=0)
    part, extra = part[:320], part[320:]
    part = jnp.concatenate(
        [part.reshape(PARTS, 80, DH), jnp.broadcast_to(extra[None], (PARTS, EXTRA, DH))], axis=1
    )
    part = jnp.sum(trade(part, "zh"), axis=0)
    part, extra = part[:80], part[80:]
    part, partial = lax.optimization_barrier((part, partial))
    partial = trade(partial, ("y", "core"))
    part = lax.all_gather(part, ("zh", "zl")).reshape(1280, DH)
    part, partial = lax.optimization_barrier((part, partial))
    whole = jnp.concatenate([part, extra], axis=0)
    grad_query, grad_keys, grad_values, beta_rows, bias_row, grad_frames = lay(
        spread(whole, "x"), partial
    )
    grad_beta = beta_rows.T
    grad_bias = bias_row.reshape(2)
    return (outputs, grad_frames, grad_query, grad_keys, grad_values, grad_beta, grad_bias)


def solution(mesh):
    fine = Mesh(mesh.devices.reshape(4, 4, 4, 4, 2), ("zh", "zl", "x", "y", "core"))
    ctx, head = ("zh", "zl", "x"), ("y", "core")
    in_specs = (
        P(ctx, None),
        P(None, head),
        P(None, head),
        P(None, head),
        P(None, head),
        P(head),
        P(ctx, head),
    )
    out_specs = (
        P(ctx, head),
        P(ctx, head),
        P(None, head),
        P(None, head),
        P(None, head),
        P(None, head),
        P(head),
    )
    return jax.shard_map(local, mesh=fine, in_specs=in_specs, out_specs=out_specs, check_vma=False)
```

```python
import functools

import jax
import jax.numpy as jnp
from jax import lax
from jax.experimental import pallas as pl
from jax.experimental.pallas import tpu as pltpu
from jax.sharding import Mesh, PartitionSpec as P

DH = 128
ROWS = 128
HALF = 64
REFL = 256
PARTS = 4
KEPT_ROWS = (
    ("q", ROWS), ("k", REFL), ("v", REFL), ("w", REFL), ("u", REFL), ("z", REFL), ("yg", REFL),
    ("cols", REFL), ("cot", ROWS), ("qt", ROWS), ("pu", ROWS), ("own", 4 * DH), ("near", 4 * DH),
)
KEPT, KEPT_SIZE = {}, 0
for _name, _rows in KEPT_ROWS:
    KEPT[_name] = slice(KEPT_SIZE, KEPT_SIZE + _rows)
    KEPT_SIZE += _rows
EPS = 1e-06
EXTRA = 8
LARGE_BYTES = 63 * 1024 * 1024
SMALL_BYTES = 16 * 1024 * 1024


def halves(a):
    high = a.astype(jnp.bfloat16)
    return high, (a - high.astype(jnp.float32)).astype(jnp.bfloat16)


def dot(a, b, ca=1, cb=0):
    return lax.dot_general(a, b, (((ca,), (cb,)), ((), ())), preferred_element_type=jnp.float32)


def mm(a, b, ca=1, cb=0):
    return mm_halves(halves(a), halves(b), ca, cb)


def mm_halves(a, b, ca=1, cb=0):
    return dot(a[0], b[0], ca, cb) + (dot(a[0], b[1], ca, cb) + dot(a[1], b[0], ca, cb))


def mix(first, second):
    return jnp.concatenate([first[:HALF], second[:HALF], first[HALF:], second[HALF:]], axis=0)


def unmix(rows):
    first = jnp.concatenate([rows[:HALF], rows[ROWS : ROWS + HALF]], axis=0)
    second = jnp.concatenate([rows[HALF:ROWS], rows[ROWS + HALF :]], axis=0)
    return first, second


def place(shape, axis):
    row = lax.broadcasted_iota(jnp.int32, shape, axis)
    return (row & ROWS) + 2 * (row & (HALF - 1)) + ((row >> 6) & 1)


def seen_mask():
    frame = lax.broadcasted_iota(jnp.int32, (ROWS, REFL), 0)
    return (place((ROWS, REFL), 1) >> 1) <= frame


def fetch(pairs, sems):
    copies = [pltpu.make_async_copy(a, b, sems.at[i]) for i, (a, b) in enumerate(pairs)]
    for copy in copies:
        copy.start()
    return copies


def prepare_kernel(
    bias_ref, wb_ref, frames_any, wk_any, wq_any, wv_any, cot_any,
    send_any, kept_any, wide_any,
    frames_ref, wk_ref, wq_ref, wv_ref, cot_ref, send_ref, kept_ref, wide_ref, in_sems, out_sems,
):
    arrive = fetch(
        (
            (frames_any, frames_ref), (wk_any, wk_ref), (wq_any, wq_ref), (wv_any, wv_ref),
            (cot_any, cot_ref),
        ),
        in_sems,
    )

    def keep(name, value):
        kept_ref[KEPT[name], :] = value

    arrive[0].wait()
    frames = frames_ref[...]
    wide_ref[...] = frames.astype(jnp.float32)
    out_copies = fetch([(wide_ref, wide_any.at[i]) for i in range(PARTS)], out_sems)
    logits = dot(frames, wb_ref[...], 1, 1)
    arrive[1].wait()
    k_raw = dot(frames, wk_ref[...])
    for copy in arrive[2:]:
        copy.wait()
    q_raw = dot(frames, wq_ref[...])
    v_raw = dot(frames, wv_ref[...])
    rq = lax.rsqrt(jnp.sum(q_raw * q_raw, axis=1, keepdims=True) + EPS)
    q = q_raw * rq
    keys = mix(k_raw[:, :DH], k_raw[:, DH:])
    rk = lax.rsqrt(jnp.sum(keys * keys, axis=1, keepdims=True) + EPS)
    k = keys * rk
    v = mix(v_raw[:, :DH], v_raw[:, DH:])
    beta = 2.0 * jax.nn.sigmoid(mix(logits[:, 0:1] + bias_ref[0], logits[:, 1:2] + bias_ref[1]))
    keep("q", q)
    keep("k", k)
    keep("v", v)
    lane = lax.broadcasted_iota(jnp.int32, (REFL, DH), 1)
    rq_long = jnp.concatenate([rq, rq], axis=0)
    keep("cols", jnp.where(lane == 0, beta, jnp.where(lane == 1, rk, rq_long)))

    gram = mm(k, k, 1, 1)
    system = beta * gram
    row, col = place((ROWS, ROWS), 0), place((ROWS, ROWS), 1)
    parts = [system[:ROWS, :ROWS], system[ROWS:, ROWS:]]
    pair = ((row >> 1) == (col >> 1)) & (row > col)
    eye = jnp.where(row == col, 1.0, 0.0)
    inverse = [eye - jnp.where(pair, part, 0.0) for part in parts]
    for level in range(1, 7):
        lower = ((row >> (level + 1)) == (col >> (level + 1))) & ((row >> level) > (col >> level))
        inner = [mm(jnp.where(lower, part, 0.0), inv) for part, inv in zip(parts, inverse)]
        inverse = [inv - mm(inv, mid) for inv, mid in zip(inverse, inner)]
    corner = -mm(inverse[1], mm(system[ROWS:, :ROWS], inverse[0]))
    zero = jnp.zeros((ROWS, ROWS), jnp.float32)
    inverse = jnp.concatenate(
        [
            jnp.concatenate([inverse[0], zero], axis=1),
            jnp.concatenate([corner, inverse[1]], axis=1),
        ],
        axis=0,
    )
    wu = mm(inverse, jnp.concatenate([beta * k, beta * v], axis=1))
    w, u = wu[:, :DH], wu[:, DH:]
    keep("w", w)
    keep("u", u)
    cot = cot_ref[...].astype(jnp.float32)
    keep("cot", cot)
    scores = jnp.where(seen_mask(), mm(q, k, 1, 1), 0.0)
    pg = mm(scores, cot, 0, 0)
    zy = mm(inverse, jnp.concatenate([k, pg], axis=1), 0, 0)
    keep("z", zy[:, :DH])
    keep("yg", zy[:, DH:])
    first, second = pl.ds(0, KEPT["qt"].start), pl.ds(KEPT["qt"].start, 2 * ROWS)
    out_copies.append(
        pltpu.make_async_copy(kept_ref.at[first], kept_any.at[first], out_sems.at[PARTS])
    )
    out_copies[-1].start()
    kwu = mm(k, wu, 0, 0)
    pwu = mm(scores, wu)
    qt = q - pwu[:, :DH]
    keep("qt", qt)
    keep("pu", pwu[:, DH:])
    send_ref[0] = eye_like() - kwu[:, :DH]
    send_ref[1] = kwu[:, DH:]
    send_ref[2] = mm(cot, qt, 0, 0)
    for i, (a, b) in enumerate(
        ((send_ref, send_any), (kept_ref.at[second], kept_any.at[second]))
    ):
        out_copies.append(pltpu.make_async_copy(a, b, out_sems.at[PARTS + 1 + i]))
        out_copies[-1].start()
    for copy in out_copies:
        copy.wait()


def eye_like():
    row = lax.broadcasted_iota(jnp.int32, (DH, DH), 0)
    col = lax.broadcasted_iota(jnp.int32, (DH, DH), 1)
    return jnp.where(row == col, 1.0, 0.0)


def compose_group(me, parts):
    last = len(parts) - 1
    maps = [halves(part[0]) for part in parts]
    ahead = [jnp.concatenate([parts[0][0], parts[0][1]], axis=1)]
    behind = [jnp.concatenate([parts[last][0], parts[last][2]], axis=0)]
    for i in range(1, last + 1):
        moved = mm_halves(maps[i], halves(ahead[-1]))
        ahead.append(jnp.concatenate([moved[:, :DH], moved[:, DH:] + parts[i][1]], axis=1))
        j = last - i
        moved = mm_halves(halves(behind[-1]), maps[j])
        behind.append(jnp.concatenate([moved[:DH], moved[DH:] + parts[j][2]], axis=0))
    whole = (ahead[last][:, :DH], ahead[last][:, DH:], behind[last][DH:])
    eye, zero = eye_like(), jnp.zeros((DH, DH), jnp.float32)
    before = jnp.concatenate([eye, zero], axis=1)
    after = jnp.concatenate([eye, zero], axis=0)
    for i in range(last):
        before = jnp.where(me == i + 1, ahead[i], before)
        after = jnp.where(me == last - 1 - i, behind[i], after)
    return whole, (before[:, :DH], before[:, DH:], after[:DH], after[DH:])


def group_kernel(
    place_ref, parts_ref, kept_in, total_ref, kept_any, whole_ref, around_ref, sem, *, axis, name
):
    del kept_in
    parts = [tuple(parts_ref[i, j] for j in range(3)) for i in range(PARTS)]
    whole, around = compose_group(place_ref[axis], parts)
    for i, value in enumerate(around):
        around_ref[DH * i : DH * i + DH] = value
    rows = pl.ds(KEPT[name].start, 4 * DH)
    copy = pltpu.make_async_copy(around_ref, kept_any.at[rows], sem)
    copy.start()
    if total_ref.shape[1] == DH:
        for i, value in enumerate(whole):
            total_ref[i] = value
    else:
        for i, value in enumerate(whole):
            whole_ref[i] = value
        rows = DH // PARTS
        mine = pl.ds(pl.multiple_of(place_ref[0] * rows, rows), rows)
        for i in range(3):
            total_ref[i] = whole_ref[i, mine, :]
    copy.wait()


def group_scan(parts, kept, place, axis, name, rows):
    return pl.pallas_call(
        functools.partial(group_kernel, axis=axis, name=name),
        out_shape=(f32(3, rows, DH), kept),
        in_specs=[SMEM, VMEM, HBM],
        out_specs=(VMEM, HBM),
        scratch_shapes=[
            pltpu.VMEM((3, DH, DH), jnp.float32),
            pltpu.VMEM((4 * DH, DH), jnp.float32),
            pltpu.SemaphoreType.DMA,
        ],
        input_output_aliases={2: 1},
        compiler_params=pltpu.CompilerParams(vmem_limit_bytes=SMALL_BYTES),
        name="group_scan",
    )(place, parts, kept)


def finish_kernel(place_ref, far_ref, kept_ref, out_ref, pieces_ref, tiles_ref):
    me = place_ref[2]
    own_ref = kept_ref[KEPT["own"], :].reshape(4, DH, DH)
    near_ref = kept_ref[KEPT["near"], :].reshape(4, DH, DH)
    inward = mm(own_ref[0], jnp.concatenate([near_ref[0], near_ref[1]], axis=1))
    inward_map, inward_shift = inward[:, :DH], inward[:, DH:] + own_ref[1]
    outward = mm(jnp.concatenate([near_ref[2], near_ref[3]], axis=0), own_ref[2])
    outward_map, outward_shift = outward[:DH], outward[DH:] + own_ref[3]

    def far(group, which):
        return jnp.concatenate([far_ref[i, group, which] for i in range(PARTS)], axis=0)

    entering = jnp.where(me > 0, far(0, 1), 0.0)
    leaving = jnp.where(me < PARTS - 1, far(PARTS - 1, 2), 0.0)
    for i in range(1, PARTS - 1):
        j = PARTS - 1 - i
        entering = jnp.where(me > i, mm(far(i, 0), entering) + far(i, 1), entering)
        leaving = jnp.where(me < j, mm(leaving, far(j, 0)) + far(j, 2), leaving)
    entering = mm(inward_map, entering) + inward_shift
    leaving = mm(leaving, outward_map) + outward_shift
    q, k, v = kept_ref[KEPT["q"], :], kept_ref[KEPT["k"], :], kept_ref[KEPT["v"], :]
    cot = kept_ref[KEPT["cot"], :]
    cols = kept_ref[KEPT["cols"], :]
    beta, rk, rq = cols[:, 0:1], cols[:, 1:2], cols[:ROWS, 2:3]
    out_ref[...] = (mm(kept_ref[KEPT["qt"], :], entering) + kept_ref[KEPT["pu"], :]).astype(jnp.bfloat16)
    fresh = kept_ref[KEPT["u"], :] - mm(kept_ref[KEPT["w"], :], entering)
    y = kept_ref[KEPT["yg"], :] + mm(kept_ref[KEPT["z"], :], leaving, 1, 1)
    gram = mm(k, k, 1, 1)
    row, col = place((REFL, REFL), 0), place((REFL, REFL), 1)
    d_system = jnp.where(row > col, -mm(y, fresh, 1, 1), 0.0)
    d_scores = jnp.where(seen_mask(), mm(cot, fresh, 1, 1), 0.0)
    d_query = mm(cot, entering, 1, 1) + mm(d_scores, k)
    error = v - mm(k, entering)
    d_beta = jnp.sum(y * error, axis=1, keepdims=True) + jnp.sum(
        d_system * gram, axis=1, keepdims=True
    )
    by = beta * y
    d_gram = beta * d_system
    d_keys = (
        mm(d_scores, q, 0, 0)
        + mm(fresh, leaving)
        - mm(by, entering, 1, 1)
        + mm(d_gram, k)
        + mm(d_gram, k, 0, 0)
    )
    d_query = rq * (d_query - q * jnp.sum(d_query * q, axis=1, keepdims=True))
    d_keys = rk * (d_keys - k * jnp.sum(d_keys * k, axis=1, keepdims=True))
    d_logits = d_beta * beta * (1.0 - 0.5 * beta)
    l_first, l_second = unmix(d_logits)
    lane2 = lax.broadcasted_iota(jnp.int32, (ROWS, 2), 1)
    g_logits_f32 = jnp.where(lane2 == 0, l_first, l_second)
    g_query = d_query.astype(jnp.bfloat16)
    k_first, k_second = unmix(d_keys)
    v_first, v_second = unmix(by)
    g_keys = jnp.concatenate([k_first, k_second], axis=1).astype(jnp.bfloat16)
    g_values = jnp.concatenate([v_first, v_second], axis=1).astype(jnp.bfloat16)
    tiles_ref[:, :DH] = g_query
    tiles_ref[:, DH : 3 * DH] = g_keys
    tiles_ref[:, 3 * DH : 5 * DH] = g_values
    lane = lax.broadcasted_iota(jnp.int32, (ROWS, DH), 1)
    padded = jnp.where(lane == 0, l_first, jnp.where(lane == 1, l_second, 0.0))
    tiles_ref[:, 5 * DH :] = padded.astype(jnp.bfloat16)
    wide = jnp.float32
    tiles = (g_query, g_keys[:, :DH], g_keys[:, DH:], g_values[:, :DH])
    shared = g_values[:, DH:].astype(wide)
    turned = padded.astype(jnp.bfloat16).astype(wide).T
    bias_row = jnp.sum(g_logits_f32, axis=0, keepdims=True)
    bias_lanes = jnp.where(
        lax.broadcasted_iota(jnp.int32, (1, DH), 1) == 0, bias_row[:, 0:1], bias_row[:, 1:2]
    )
    for i in range(PARTS):
        pieces_ref[i, :ROWS] = tiles[i].astype(wide)
        pieces_ref[i, ROWS : 2 * ROWS] = shared
        pieces_ref[i, 2 * ROWS :] = jnp.concatenate(
            [turned[:2], bias_lanes, jnp.zeros((EXTRA - 3, DH), wide)], axis=0
        )


def f32(*shape):
    return jax.ShapeDtypeStruct(shape, jnp.float32)


SMEM = pl.BlockSpec(memory_space=pltpu.SMEM)
VMEM = pl.BlockSpec(memory_space=pltpu.VMEM)
ANY = pl.BlockSpec(memory_space=pl.ANY)
HBM = pl.BlockSpec(memory_space=pltpu.HBM)


def held(a):
    return pltpu.VMEM(a.shape, a.dtype)


def prepare(bias, w_beta, *large):
    send, kept, wide = f32(3, DH, DH), f32(KEPT_SIZE, DH), f32(PARTS, ROWS, 1024)
    return pl.pallas_call(
        prepare_kernel,
        out_shape=(send, kept, wide),
        in_specs=[SMEM, VMEM] + [HBM] * 5,
        out_specs=(HBM, HBM, HBM),
        scratch_shapes=[
            held(a) for a in (*large, send, f32(KEPT["own"].start, DH), f32(ROWS, 1024))
        ]
        + [pltpu.SemaphoreType.DMA((5,)), pltpu.SemaphoreType.DMA((PARTS + 3,))],
        compiler_params=pltpu.CompilerParams(vmem_limit_bytes=LARGE_BYTES),
        name="prepare",
    )(bias, w_beta, *large)


def finish(place, far, kept):
    return pl.pallas_call(
        finish_kernel,
        out_shape=(
            jax.ShapeDtypeStruct((ROWS, DH), jnp.bfloat16),
            f32(PARTS, 2 * ROWS + EXTRA, DH),
            jax.ShapeDtypeStruct((ROWS, 6 * DH), jnp.bfloat16),
        ),
        in_specs=[SMEM, VMEM, VMEM],
        compiler_params=pltpu.CompilerParams(vmem_limit_bytes=SMALL_BYTES),
        name="finish",
    )(place, far, kept)


def side_kernel(tiles_ref, wb_ref, wq_ref, wk_ref, wv_ref, part_ref):
    part = (
        dot(tiles_ref[:, :DH], wq_ref[...], 1, 1)
        + dot(tiles_ref[:, DH : 3 * DH], wk_ref[...], 1, 1)
        + dot(tiles_ref[:, 3 * DH : 5 * DH], wv_ref[...], 1, 1)
        + dot(tiles_ref[:, 5 * DH : 5 * DH + 2], wb_ref[...])
    )
    for i in range(8):
        part_ref[i] = part[:, DH * i : DH * i + DH]


def side(*args):
    return pl.pallas_call(
        side_kernel,
        out_shape=f32(8, ROWS, DH),
        compiler_params=pltpu.CompilerParams(vmem_limit_bytes=SMALL_BYTES),
        cost_estimate=pl.CostEstimate(flops=170_000_000, bytes_accessed=3_000_000, transcendentals=0),
        name="side",
    )(*args)


def narrow_kernel(frames_ref, narrow_ref):
    narrow_ref[...] = frames_ref[...].astype(jnp.bfloat16)


def narrow(frames):
    return pl.pallas_call(
        narrow_kernel,
        out_shape=jax.ShapeDtypeStruct(frames.shape, jnp.bfloat16),
        in_specs=[VMEM],
        out_specs=VMEM,
        compiler_params=pltpu.CompilerParams(vmem_limit_bytes=SMALL_BYTES),
        cost_estimate=pl.CostEstimate(flops=1_000_000, bytes_accessed=3_000_000, transcendentals=0),
        name="narrow",
    )(frames)


def weigh_kernel(place_ref, pieces_ref, frames_ref, sums_ref):
    quarter = pl.ds(pl.multiple_of(place_ref[0] * 256, 256), 256)
    total = jnp.zeros((1024, DH), jnp.float32)
    corner = jnp.zeros((256, DH), jnp.float32)
    beta = jnp.zeros((2, 256), jnp.float32)
    bias = jnp.zeros((1, DH), jnp.float32)
    for i in range(PARTS):
        piece = pieces_ref[i, : 2 * ROWS].astype(jnp.bfloat16)
        rows = pieces_ref[i, 2 * ROWS :]
        bias = bias + rows[2:3]
        beta = beta + dot(rows[:2].astype(jnp.bfloat16), frames_ref[i, :, quarter])
        total = total + dot(frames_ref[i], piece[:ROWS], 0, 0)
        corner = corner + dot(frames_ref[i, :, quarter], piece[ROWS:], 0, 0)
    extra = [beta[:, :DH], beta[:, DH:], bias, jnp.zeros((EXTRA - 5, DH), jnp.float32)]
    extra = jnp.concatenate(extra, axis=0)
    total = jnp.concatenate([total, corner], axis=0)
    rows = total.shape[0] // (PARTS * PARTS)
    for i in range(PARTS):
        for j in range(PARTS):
            block = PARTS * j + i
            sums_ref[i, rows * j : rows * j + rows] = total[rows * block : rows * block + rows]
        sums_ref[i, rows * PARTS :] = extra


def weigh(place, pieces, frames):
    return pl.pallas_call(
        weigh_kernel,
        out_shape=f32(PARTS, 1280 // PARTS + EXTRA, DH),
        in_specs=[SMEM, VMEM, VMEM],
        compiler_params=pltpu.CompilerParams(vmem_limit_bytes=SMALL_BYTES),
        name="weigh",
    )(place, pieces, frames)


def lay_kernel(
    whole_ref, heads_ref, query_any, keys_any, values_any, beta_any, bias_any, frames_any,
    beta_ref, bias_ref, sum_ref, sems,
):
    left, right = pl.ds(0, DH), pl.ds(DH, DH)
    full = pl.ds(0, 1024)
    pairs = [
        (whole_ref.at[0, full], query_any),
        (whole_ref.at[1, full], keys_any.at[:, left]),
        (whole_ref.at[2, full], keys_any.at[:, right]),
        (whole_ref.at[3, full], values_any.at[:, left]),
    ]
    for i in range(PARTS):
        pairs.append(
            (whole_ref.at[i, pl.ds(1024, 256)], values_any.at[pl.ds(256 * i, 256), right])
        )
    copies = fetch(pairs, sems)
    rows = [whole_ref[i, 1280:] for i in range(PARTS)]
    beta_ref[...] = jnp.concatenate(
        [row[2 * half : 2 * half + 2] for row in rows for half in range(2)], axis=1
    )
    bias_ref[...] = rows[0][4:5, :2]
    total = heads_ref[0]
    for i in range(1, heads_ref.shape[0]):
        total = total + heads_ref[i]
    sum_ref[...] = total.astype(jnp.bfloat16)
    small = ((beta_ref, beta_any), (bias_ref, bias_any), (sum_ref, frames_any))
    for i, (a, b) in enumerate(small):
        copies.append(pltpu.make_async_copy(a, b, sems.at[8 + i]))
        copies[-1].start()
    for copy in copies:
        copy.wait()


def lay(whole, heads):
    frames = jax.ShapeDtypeStruct((ROWS, DH), jnp.bfloat16)
    return pl.pallas_call(
        lay_kernel,
        out_shape=(
            f32(1024, DH), f32(1024, 2 * DH), f32(1024, 2 * DH), f32(2, 1024), f32(1, 2), frames,
        ),
        in_specs=[VMEM, VMEM],
        out_specs=(HBM,) * 6,
        scratch_shapes=[
            held(f32(2, 1024)), held(f32(1, 2)), held(frames), pltpu.SemaphoreType.DMA((11,)),
        ],
        compiler_params=pltpu.CompilerParams(vmem_limit_bytes=SMALL_BYTES),
        name="lay",
    )(whole, heads)


def spread(a, axis):
    return lax.all_to_all(jnp.broadcast_to(a[None], (PARTS, *a.shape)), axis, 0, 0, tiled=True)


def trade(a, axis):
    return lax.all_to_all(a, axis, 0, 0, tiled=True)


def local(frames, w_query, w_keys, w_values, w_beta, beta_bias, cotangent):
    place = jnp.stack([lax.axis_index("x"), lax.axis_index("zl"), lax.axis_index("zh")])
    beta_turned = w_beta.T
    own, kept, wide_frames = prepare(
        beta_bias, beta_turned, frames, w_keys, w_query, w_values, cotangent
    )
    row, wide_frames = lax.optimization_barrier((lax.all_gather(own, "x"), wide_frames))
    group_frames = trade(wide_frames, "x")
    total, kept = group_scan(row, kept, place, 0, "own", DH)
    total, kept = group_scan(lax.all_gather(total, "zl"), kept, place, 1, "near", DH // PARTS)
    far = lax.all_gather(lax.all_gather(total, "zh"), "x")
    outputs, pieces, tiles = finish(place, far, kept)
    partial = side(tiles, beta_turned, w_query, w_keys, w_values)
    sums = weigh(place, trade(pieces, "x"), narrow(group_frames))
    part = jnp.sum(trade(sums, "zl"), axis=0)
    part, extra = part[:320], part[320:]
    part = jnp.concatenate(
        [part.reshape(PARTS, 80, DH), jnp.broadcast_to(extra[None], (PARTS, EXTRA, DH))], axis=1
    )
    part = jnp.sum(trade(part, "zh"), axis=0)
    part, extra = part[:80], part[80:]
    part, partial = lax.optimization_barrier((part, partial))
    partial = trade(partial, ("y", "core"))
    part = lax.all_gather(part, ("zh", "zl")).reshape(1280, DH)
    part, partial = lax.optimization_barrier((part, partial))
    whole = jnp.concatenate([part, extra], axis=0)
    grad_query, grad_keys, grad_values, beta_rows, bias_row, grad_frames = lay(
        spread(whole, "x"), partial
    )
    grad_beta = beta_rows.T
    grad_bias = bias_row.reshape(2)
    return (outputs, grad_frames, grad_query, grad_keys, grad_values, grad_beta, grad_bias)


def solution(mesh):
    fine = Mesh(mesh.devices.reshape(4, 4, 4, 4, 2), ("zh", "zl", "x", "y", "core"))
    ctx, head = ("zh", "zl", "x"), ("y", "core")
    in_specs = (
        P(ctx, None),
        P(None, head),
        P(None, head),
        P(None, head),
        P(None, head),
        P(head),
        P(ctx, head),
    )
    out_specs = (
        P(ctx, head),
        P(ctx, head),
        P(None, head),
        P(None, head),
        P(None, head),
        P(None, head),
        P(head),
    )
    return jax.shard_map(local, mesh=fine, in_specs=in_specs, out_specs=out_specs, check_vma=False)
```

```python
import functools

import jax
import jax.numpy as jnp
from jax import lax
from jax.experimental import pallas as pl
from jax.experimental.pallas import tpu as pltpu
from jax.sharding import Mesh, PartitionSpec as P

DH = 128
ROWS = 128
HALF = 64
REFL = 256
PARTS = 4
KEPT_ROWS = (
    ("q", ROWS), ("k", REFL), ("v", REFL), ("w", REFL), ("u", REFL), ("z", REFL), ("yg", REFL),
    ("cols", REFL), ("cot", ROWS), ("qt", ROWS), ("pu", ROWS), ("own", 4 * DH), ("near", 4 * DH),
)
KEPT, KEPT_SIZE = {}, 0
for _name, _rows in KEPT_ROWS:
    KEPT[_name] = slice(KEPT_SIZE, KEPT_SIZE + _rows)
    KEPT_SIZE += _rows
EPS = 1e-06
EXTRA = 8
LARGE_BYTES = 63 * 1024 * 1024
SMALL_BYTES = 16 * 1024 * 1024


def halves(a):
    high = a.astype(jnp.bfloat16)
    return high, (a - high.astype(jnp.float32)).astype(jnp.bfloat16)


def dot(a, b, ca=1, cb=0):
    return lax.dot_general(a, b, (((ca,), (cb,)), ((), ())), preferred_element_type=jnp.float32)


def mm(a, b, ca=1, cb=0):
    return mm_halves(halves(a), halves(b), ca, cb)


def mm_halves(a, b, ca=1, cb=0):
    return dot(a[0], b[0], ca, cb) + (dot(a[0], b[1], ca, cb) + dot(a[1], b[0], ca, cb))


def mix(first, second):
    return jnp.concatenate([first[:HALF], second[:HALF], first[HALF:], second[HALF:]], axis=0)


def unmix(rows):
    first = jnp.concatenate([rows[:HALF], rows[ROWS : ROWS + HALF]], axis=0)
    second = jnp.concatenate([rows[HALF:ROWS], rows[ROWS + HALF :]], axis=0)
    return first, second


def place(shape, axis):
    row = lax.broadcasted_iota(jnp.int32, shape, axis)
    return (row & ROWS) + 2 * (row & (HALF - 1)) + ((row >> 6) & 1)


def seen_mask():
    frame = lax.broadcasted_iota(jnp.int32, (ROWS, REFL), 0)
    return (place((ROWS, REFL), 1) >> 1) <= frame


def fetch(pairs, sems):
    copies = [pltpu.make_async_copy(a, b, sems.at[i]) for i, (a, b) in enumerate(pairs)]
    for copy in copies:
        copy.start()
    return copies


def prepare_kernel(
    bias_ref, wb_ref, frames_any, wk_any, wq_any, wv_any, cot_any,
    send_any, kept_any, wide_any,
    frames_ref, wk_ref, wq_ref, wv_ref, cot_ref, send_ref, kept_ref, wide_ref, in_sems, out_sems,
):
    arrive = fetch(
        (
            (frames_any, frames_ref), (wk_any, wk_ref), (wq_any, wq_ref), (wv_any, wv_ref),
            (cot_any, cot_ref),
        ),
        in_sems,
    )

    def keep(name, value):
        kept_ref[KEPT[name], :] = value

    arrive[0].wait()
    frames = frames_ref[...]
    wide_ref[...] = frames.astype(jnp.float32)
    out_copies = fetch([(wide_ref, wide_any.at[i]) for i in range(PARTS)], out_sems)
    logits = dot(frames, wb_ref[...], 1, 1)
    arrive[1].wait()
    k_raw = dot(frames, wk_ref[...])
    for copy in arrive[2:]:
        copy.wait()
    q_raw = dot(frames, wq_ref[...])
    v_raw = dot(frames, wv_ref[...])
    rq = lax.rsqrt(jnp.sum(q_raw * q_raw, axis=1, keepdims=True) + EPS)
    q = q_raw * rq
    keys = mix(k_raw[:, :DH], k_raw[:, DH:])
    rk = lax.rsqrt(jnp.sum(keys * keys, axis=1, keepdims=True) + EPS)
    k = keys * rk
    v = mix(v_raw[:, :DH], v_raw[:, DH:])
    beta = 2.0 * jax.nn.sigmoid(mix(logits[:, 0:1] + bias_ref[0], logits[:, 1:2] + bias_ref[1]))
    keep("q", q)
    keep("k", k)
    keep("v", v)
    lane = lax.broadcasted_iota(jnp.int32, (REFL, DH), 1)
    rq_long = jnp.concatenate([rq, rq], axis=0)
    keep("cols", jnp.where(lane == 0, beta, jnp.where(lane == 1, rk, rq_long)))

    gram = mm(k, k, 1, 1)
    system = beta * gram
    row, col = place((ROWS, ROWS), 0), place((ROWS, ROWS), 1)
    parts = [system[:ROWS, :ROWS], system[ROWS:, ROWS:]]
    pair = ((row >> 1) == (col >> 1)) & (row > col)
    eye = jnp.where(row == col, 1.0, 0.0)
    inverse = [eye - jnp.where(pair, part, 0.0) for part in parts]
    for level in range(1, 7):
        lower = ((row >> (level + 1)) == (col >> (level + 1))) & ((row >> level) > (col >> level))
        inner = [mm(jnp.where(lower, part, 0.0), inv) for part, inv in zip(parts, inverse)]
        inverse = [inv - mm(inv, mid) for inv, mid in zip(inverse, inner)]
    corner = -mm(inverse[1], mm(system[ROWS:, :ROWS], inverse[0]))
    zero = jnp.zeros((ROWS, ROWS), jnp.float32)
    inverse = jnp.concatenate(
        [
            jnp.concatenate([inverse[0], zero], axis=1),
            jnp.concatenate([corner, inverse[1]], axis=1),
        ],
        axis=0,
    )
    wu = mm(inverse, jnp.concatenate([beta * k, beta * v], axis=1))
    w, u = wu[:, :DH], wu[:, DH:]
    keep("w", w)
    keep("u", u)
    cot = cot_ref[...].astype(jnp.float32)
    keep("cot", cot)
    scores = jnp.where(seen_mask(), mm(q, k, 1, 1), 0.0)
    pg = mm(scores, cot, 0, 0)
    zy = mm(inverse, jnp.concatenate([k, pg], axis=1), 0, 0)
    keep("z", zy[:, :DH])
    keep("yg", zy[:, DH:])
    first, second = pl.ds(0, KEPT["qt"].start), pl.ds(KEPT["qt"].start, 2 * ROWS)
    out_copies.append(
        pltpu.make_async_copy(kept_ref.at[first], kept_any.at[first], out_sems.at[PARTS])
    )
    out_copies[-1].start()
    kwu = mm(k, wu, 0, 0)
    pwu = mm(scores, wu)
    qt = q - pwu[:, :DH]
    keep("qt", qt)
    keep("pu", pwu[:, DH:])
    send_ref[0] = eye_like() - kwu[:, :DH]
    send_ref[1] = kwu[:, DH:]
    send_ref[2] = mm(cot, qt, 0, 0)
    for i, (a, b) in enumerate(
        ((send_ref, send_any), (kept_ref.at[second], kept_any.at[second]))
    ):
        out_copies.append(pltpu.make_async_copy(a, b, out_sems.at[PARTS + 1 + i]))
        out_copies[-1].start()
    for copy in out_copies:
        copy.wait()


def eye_like():
    row = lax.broadcasted_iota(jnp.int32, (DH, DH), 0)
    col = lax.broadcasted_iota(jnp.int32, (DH, DH), 1)
    return jnp.where(row == col, 1.0, 0.0)


def compose_group(me, parts):
    last = len(parts) - 1
    maps = [halves(part[0]) for part in parts]
    ahead = [jnp.concatenate([parts[0][0], parts[0][1]], axis=1)]
    behind = [jnp.concatenate([parts[last][0], parts[last][2]], axis=0)]
    for i in range(1, last + 1):
        moved = mm_halves(maps[i], halves(ahead[-1]))
        ahead.append(jnp.concatenate([moved[:, :DH], moved[:, DH:] + parts[i][1]], axis=1))
        j = last - i
        moved = mm_halves(halves(behind[-1]), maps[j])
        behind.append(jnp.concatenate([moved[:DH], moved[DH:] + parts[j][2]], axis=0))
    whole = (ahead[last][:, :DH], ahead[last][:, DH:], behind[last][DH:])
    eye, zero = eye_like(), jnp.zeros((DH, DH), jnp.float32)
    before = jnp.concatenate([eye, zero], axis=1)
    after = jnp.concatenate([eye, zero], axis=0)
    for i in range(last):
        before = jnp.where(me == i + 1, ahead[i], before)
        after = jnp.where(me == last - 1 - i, behind[i], after)
    return whole, (before[:, :DH], before[:, DH:], after[:DH], after[DH:])


def group_kernel(
    place_ref, parts_ref, kept_in, total_ref, kept_any, whole_ref, around_ref, sem, *, axis, name
):
    del kept_in
    parts = [tuple(parts_ref[i, j] for j in range(3)) for i in range(PARTS)]
    whole, around = compose_group(place_ref[axis], parts)
    for i, value in enumerate(around):
        around_ref[DH * i : DH * i + DH] = value
    rows = pl.ds(KEPT[name].start, 4 * DH)
    copy = pltpu.make_async_copy(around_ref, kept_any.at[rows], sem)
    copy.start()
    if total_ref.shape[1] == DH:
        for i, value in enumerate(whole):
            total_ref[i] = value
    else:
        for i, value in enumerate(whole):
            whole_ref[i] = value
        rows = DH // PARTS
        mine = pl.ds(pl.multiple_of(place_ref[0] * rows, rows), rows)
        for i in range(3):
            total_ref[i] = whole_ref[i, mine, :]
    copy.wait()


def group_scan(parts, kept, place, axis, name, rows):
    return pl.pallas_call(
        functools.partial(group_kernel, axis=axis, name=name),
        out_shape=(f32(3, rows, DH), kept),
        in_specs=[SMEM, VMEM, HBM],
        out_specs=(VMEM, HBM),
        scratch_shapes=[
            pltpu.VMEM((3, DH, DH), jnp.float32),
            pltpu.VMEM((4 * DH, DH), jnp.float32),
            pltpu.SemaphoreType.DMA,
        ],
        input_output_aliases={2: 1},
        compiler_params=pltpu.CompilerParams(vmem_limit_bytes=SMALL_BYTES),
        name="group_scan",
    )(place, parts, kept)


def finish_kernel(place_ref, far_ref, kept_ref, out_ref, pieces_ref, tiles_ref):
    me = place_ref[2]
    own_ref = kept_ref[KEPT["own"], :].reshape(4, DH, DH)
    near_ref = kept_ref[KEPT["near"], :].reshape(4, DH, DH)
    inward = mm(own_ref[0], jnp.concatenate([near_ref[0], near_ref[1]], axis=1))
    inward_map, inward_shift = inward[:, :DH], inward[:, DH:] + own_ref[1]
    outward = mm(jnp.concatenate([near_ref[2], near_ref[3]], axis=0), own_ref[2])
    outward_map, outward_shift = outward[:DH], outward[DH:] + own_ref[3]

    def far(group, which):
        at = (-1, PARTS - 2, 2 * PARTS - 4)[which] + group
        return jnp.concatenate([far_ref[i, at] for i in range(PARTS)], axis=0)

    entering = jnp.where(me > 0, far(0, 1), 0.0)
    leaving = jnp.where(me < PARTS - 1, far(PARTS - 1, 2), 0.0)
    for i in range(1, PARTS - 1):
        j = PARTS - 1 - i
        entering = jnp.where(me > i, mm(far(i, 0), entering) + far(i, 1), entering)
        leaving = jnp.where(me < j, mm(leaving, far(j, 0)) + far(j, 2), leaving)
    entering = mm(inward_map, entering) + inward_shift
    leaving = mm(leaving, outward_map) + outward_shift
    q, k, v = kept_ref[KEPT["q"], :], kept_ref[KEPT["k"], :], kept_ref[KEPT["v"], :]
    cot = kept_ref[KEPT["cot"], :]
    cols = kept_ref[KEPT["cols"], :]
    beta, rk, rq = cols[:, 0:1], cols[:, 1:2], cols[:ROWS, 2:3]
    out_ref[...] = (mm(kept_ref[KEPT["qt"], :], entering) + kept_ref[KEPT["pu"], :]).astype(jnp.bfloat16)
    fresh = kept_ref[KEPT["u"], :] - mm(kept_ref[KEPT["w"], :], entering)
    y = kept_ref[KEPT["yg"], :] + mm(kept_ref[KEPT["z"], :], leaving, 1, 1)
    gram = mm(k, k, 1, 1)
    row, col = place((REFL, REFL), 0), place((REFL, REFL), 1)
    d_system = jnp.where(row > col, -mm(y, fresh, 1, 1), 0.0)
    d_scores = jnp.where(seen_mask(), mm(cot, fresh, 1, 1), 0.0)
    d_query = mm(cot, entering, 1, 1) + mm(d_scores, k)
    error = v - mm(k, entering)
    d_beta = jnp.sum(y * error, axis=1, keepdims=True) + jnp.sum(
        d_system * gram, axis=1, keepdims=True
    )
    by = beta * y
    d_gram = beta * d_system
    d_keys = (
        mm(d_scores, q, 0, 0)
        + mm(fresh, leaving)
        - mm(by, entering, 1, 1)
        + mm(d_gram, k)
        + mm(d_gram, k, 0, 0)
    )
    d_query = rq * (d_query - q * jnp.sum(d_query * q, axis=1, keepdims=True))
    d_keys = rk * (d_keys - k * jnp.sum(d_keys * k, axis=1, keepdims=True))
    d_logits = d_beta * beta * (1.0 - 0.5 * beta)
    l_first, l_second = unmix(d_logits)
    lane2 = lax.broadcasted_iota(jnp.int32, (ROWS, 2), 1)
    g_logits_f32 = jnp.where(lane2 == 0, l_first, l_second)
    g_query = d_query.astype(jnp.bfloat16)
    k_first, k_second = unmix(d_keys)
    v_first, v_second = unmix(by)
    g_keys = jnp.concatenate([k_first, k_second], axis=1).astype(jnp.bfloat16)
    g_values = jnp.concatenate([v_first, v_second], axis=1).astype(jnp.bfloat16)
    tiles_ref[:, :DH] = g_query
    tiles_ref[:, DH : 3 * DH] = g_keys
    tiles_ref[:, 3 * DH : 5 * DH] = g_values
    lane = lax.broadcasted_iota(jnp.int32, (ROWS, DH), 1)
    padded = jnp.where(lane == 0, l_first, jnp.where(lane == 1, l_second, 0.0))
    tiles_ref[:, 5 * DH :] = padded.astype(jnp.bfloat16)
    wide = jnp.float32
    tiles = (g_query, g_keys[:, :DH], g_keys[:, DH:], g_values[:, :DH])
    shared = g_values[:, DH:].astype(wide)
    turned = padded.astype(jnp.bfloat16).astype(wide).T
    bias_row = jnp.sum(g_logits_f32, axis=0, keepdims=True)
    bias_lanes = jnp.where(
        lax.broadcasted_iota(jnp.int32, (1, DH), 1) == 0, bias_row[:, 0:1], bias_row[:, 1:2]
    )
    for i in range(PARTS):
        pieces_ref[i, :ROWS] = tiles[i].astype(wide)
        pieces_ref[i, ROWS : 2 * ROWS] = shared
        pieces_ref[i, 2 * ROWS :] = jnp.concatenate(
            [turned[:2], bias_lanes, jnp.zeros((EXTRA - 3, DH), wide)], axis=0
        )


def f32(*shape):
    return jax.ShapeDtypeStruct(shape, jnp.float32)


SMEM = pl.BlockSpec(memory_space=pltpu.SMEM)
VMEM = pl.BlockSpec(memory_space=pltpu.VMEM)
ANY = pl.BlockSpec(memory_space=pl.ANY)
HBM = pl.BlockSpec(memory_space=pltpu.HBM)


def held(a):
    return pltpu.VMEM(a.shape, a.dtype)


def prepare(bias, w_beta, *large):
    send, kept, wide = f32(3, DH, DH), f32(KEPT_SIZE, DH), f32(PARTS, ROWS, 1024)
    return pl.pallas_call(
        prepare_kernel,
        out_shape=(send, kept, wide),
        in_specs=[SMEM, VMEM] + [HBM] * 5,
        out_specs=(HBM, HBM, HBM),
        scratch_shapes=[
            held(a) for a in (*large, send, f32(KEPT["own"].start, DH), f32(ROWS, 1024))
        ]
        + [pltpu.SemaphoreType.DMA((5,)), pltpu.SemaphoreType.DMA((PARTS + 3,))],
        compiler_params=pltpu.CompilerParams(vmem_limit_bytes=LARGE_BYTES),
        name="prepare",
    )(bias, w_beta, *large)


def finish(place, far, kept):
    return pl.pallas_call(
        finish_kernel,
        out_shape=(
            jax.ShapeDtypeStruct((ROWS, DH), jnp.bfloat16),
            f32(PARTS, 2 * ROWS + EXTRA, DH),
            jax.ShapeDtypeStruct((ROWS, 6 * DH), jnp.bfloat16),
        ),
        in_specs=[SMEM, VMEM, VMEM],
        compiler_params=pltpu.CompilerParams(vmem_limit_bytes=SMALL_BYTES),
        name="finish",
    )(place, far, kept)


def side_kernel(place_ref, tiles_ref, wb_ref, wq_ref, wk_ref, wv_ref, *refs):
    out_refs, sum_ref = refs[:-1], refs[-1]
    sum_ref[...] = (
        dot(tiles_ref[:, :DH], wq_ref[...], 1, 1)
        + dot(tiles_ref[:, DH : 3 * DH], wk_ref[...], 1, 1)
        + dot(tiles_ref[:, 3 * DH : 5 * DH], wv_ref[...], 1, 1)
        + dot(tiles_ref[:, 5 * DH : 5 * DH + 2], wb_ref[...])
    )
    chip, core = place_ref[3], place_ref[4]
    for i, out_ref in enumerate(out_refs):
        pair = 2 * lax.rem(chip + i, PARTS)
        for j, block in enumerate((pair + core, pair + 1 - core)):
            out_ref[j] = sum_ref[:, pl.ds(pl.multiple_of(block * DH, DH), DH)]


def side(place, *args):
    return pl.pallas_call(
        side_kernel,
        out_shape=(f32(2, ROWS, DH),) * PARTS,
        in_specs=[SMEM] + [VMEM] * len(args),
        scratch_shapes=[pltpu.VMEM((ROWS, 2 * PARTS * DH), jnp.float32)],
        compiler_params=pltpu.CompilerParams(vmem_limit_bytes=SMALL_BYTES),
        cost_estimate=pl.CostEstimate(flops=170_000_000, bytes_accessed=3_000_000, transcendentals=0),
        name="side",
    )(place, *args)


def narrow_kernel(frames_ref, narrow_ref):
    narrow_ref[...] = frames_ref[...].astype(jnp.bfloat16)


def narrow(frames):
    return pl.pallas_call(
        narrow_kernel,
        out_shape=jax.ShapeDtypeStruct(frames.shape, jnp.bfloat16),
        in_specs=[VMEM],
        out_specs=VMEM,
        compiler_params=pltpu.CompilerParams(vmem_limit_bytes=SMALL_BYTES),
        cost_estimate=pl.CostEstimate(flops=1_000_000, bytes_accessed=3_000_000, transcendentals=0),
        name="narrow",
    )(frames)


def weigh_kernel(place_ref, pieces_ref, frames_ref, sums_ref):
    quarter = pl.ds(pl.multiple_of(place_ref[0] * 256, 256), 256)
    total = jnp.zeros((1024, DH), jnp.float32)
    corner = jnp.zeros((256, DH), jnp.float32)
    beta = jnp.zeros((2, 256), jnp.float32)
    bias = jnp.zeros((1, DH), jnp.float32)
    for i in range(PARTS):
        piece = pieces_ref[i, : 2 * ROWS].astype(jnp.bfloat16)
        rows = pieces_ref[i, 2 * ROWS :]
        bias = bias + rows[2:3]
        beta = beta + dot(rows[:2].astype(jnp.bfloat16), frames_ref[i, :, quarter])
        total = total + dot(frames_ref[i], piece[:ROWS], 0, 0)
        corner = corner + dot(frames_ref[i, :, quarter], piece[ROWS:], 0, 0)
    extra = [beta[:, :DH], beta[:, DH:], bias, jnp.zeros((EXTRA - 5, DH), jnp.float32)]
    extra = jnp.concatenate(extra, axis=0)
    total = jnp.concatenate([total, corner], axis=0)
    rows = total.shape[0] // (PARTS * PARTS)
    for i in range(PARTS):
        for j in range(PARTS):
            block = PARTS * j + i
            sums_ref[i, rows * j : rows * j + rows] = total[rows * block : rows * block + rows]
        sums_ref[i, rows * PARTS :] = extra


def weigh(place, pieces, frames):
    return pl.pallas_call(
        weigh_kernel,
        out_shape=f32(PARTS, 1280 // PARTS + EXTRA, DH),
        in_specs=[SMEM, VMEM, VMEM],
        compiler_params=pltpu.CompilerParams(vmem_limit_bytes=SMALL_BYTES),
        name="weigh",
    )(place, pieces, frames)


def lay_kernel(whole_ref, *refs):
    heads = refs[:2]
    query_any, keys_any, values_any, beta_any, bias_any, frames_any = refs[2:8]
    beta_ref, bias_ref, sum_ref, sems = refs[8:]
    left, right = pl.ds(0, DH), pl.ds(DH, DH)
    full = pl.ds(0, 1024)
    pairs = [
        (whole_ref.at[0, full], query_any),
        (whole_ref.at[1, full], keys_any.at[:, left]),
        (whole_ref.at[2, full], keys_any.at[:, right]),
        (whole_ref.at[3, full], values_any.at[:, left]),
    ]
    for i in range(PARTS):
        pairs.append(
            (whole_ref.at[i, pl.ds(1024, 256)], values_any.at[pl.ds(256 * i, 256), right])
        )
    copies = fetch(pairs, sems)
    rows = [whole_ref[i, 1280:] for i in range(PARTS)]
    beta_ref[...] = jnp.concatenate(
        [row[2 * half : 2 * half + 2] for row in rows for half in range(2)], axis=1
    )
    bias_ref[...] = rows[0][4:5, :2]
    sum_ref[...] = (heads[0][...] + heads[1][...]).astype(jnp.bfloat16)
    small = ((beta_ref, beta_any), (bias_ref, bias_any), (sum_ref, frames_any))
    for i, (a, b) in enumerate(small):
        copies.append(pltpu.make_async_copy(a, b, sems.at[8 + i]))
        copies[-1].start()
    for copy in copies:
        copy.wait()


def lay(whole, heads):
    frames = jax.ShapeDtypeStruct((ROWS, DH), jnp.bfloat16)
    return pl.pallas_call(
        lay_kernel,
        out_shape=(
            f32(1024, DH), f32(1024, 2 * DH), f32(1024, 2 * DH), f32(2, 1024), f32(1, 2), frames,
        ),
        in_specs=[VMEM] * 3,
        out_specs=(HBM,) * 6,
        scratch_shapes=[
            held(f32(2, 1024)), held(f32(1, 2)), held(frames), pltpu.SemaphoreType.DMA((11,)),
        ],
        compiler_params=pltpu.CompilerParams(vmem_limit_bytes=SMALL_BYTES),
        name="lay",
    )(whole, *heads)


def spread(a, axis):
    return lax.all_to_all(jnp.broadcast_to(a[None], (PARTS, *a.shape)), axis, 0, 0, tiled=True)


def trade(a, axis):
    return lax.all_to_all(a, axis, 0, 0, tiled=True)


def shift(a, axis, steps):
    size = lax.axis_size(axis)
    return lax.ppermute(a, axis, [(i, (i + steps) % size) for i in range(size)])


def local(frames, w_query, w_keys, w_values, w_beta, beta_bias, cotangent):
    place = jnp.stack(
        [lax.axis_index("x"), lax.axis_index("zl"), lax.axis_index("zh")]
        + [lax.axis_index("y"), lax.axis_index("core")]
    )
    beta_turned = w_beta.T
    own, kept, wide_frames = prepare(
        beta_bias, beta_turned, frames, w_keys, w_query, w_values, cotangent
    )
    row, wide_frames = lax.optimization_barrier((lax.all_gather(own, "x"), wide_frames))
    group_frames = trade(wide_frames, "x")
    total, kept = group_scan(row, kept, place, 0, "own", DH)
    total, kept = group_scan(lax.all_gather(total, "zl"), kept, place, 1, "near", DH // PARTS)
    far = lax.all_gather(total, "zh")
    far = jnp.concatenate([far[1:-1, 0], far[:-1, 1], far[1:, 2]], axis=0)
    far = lax.all_gather(far, "x")
    outputs, pieces, tiles = finish(place, far, kept)
    own, *others = side(place, tiles, beta_turned, w_query, w_keys, w_values)
    for i, other in enumerate(others):
        own = own + shift(other, "y", i + 1)
    sums = weigh(place, trade(pieces, "x"), narrow(group_frames))
    part = jnp.sum(trade(sums, "zl"), axis=0)
    part, extra = part[:320], part[320:]
    part = jnp.concatenate(
        [part.reshape(PARTS, 80, DH), jnp.broadcast_to(extra[None], (PARTS, EXTRA, DH))], axis=1
    )
    part, own = lax.optimization_barrier((part, own))
    partial = (own[0], shift(own[1], "core", 1))
    part = jnp.sum(trade(part, "zh"), axis=0)
    part, extra = part[:80], part[80:]
    part = lax.all_gather(part, ("zh", "zl")).reshape(1280, DH)
    part, partial = lax.optimization_barrier((part, partial))
    whole = jnp.concatenate([part, extra], axis=0)
    grad_query, grad_keys, grad_values, beta_rows, bias_row, grad_frames = lay(
        spread(whole, "x"), partial
    )
    grad_beta = beta_rows.T
    grad_bias = bias_row.reshape(2)
    return (outputs, grad_frames, grad_query, grad_keys, grad_values, grad_beta, grad_bias)


def solution(mesh):
    fine = Mesh(mesh.devices.reshape(4, 4, 4, 4, 2), ("zh", "zl", "x", "y", "core"))
    ctx, head = ("zh", "zl", "x"), ("y", "core")
    in_specs = (
        P(ctx, None),
        P(None, head),
        P(None, head),
        P(None, head),
        P(None, head),
        P(head),
        P(ctx, head),
    )
    out_specs = (
        P(ctx, head),
        P(ctx, head),
        P(None, head),
        P(None, head),
        P(None, head),
        P(None, head),
        P(head),
    )
    return jax.shard_map(local, mesh=fine, in_specs=in_specs, out_specs=out_specs, check_vma=False)
```

```python
import functools

import jax
import jax.numpy as jnp
from jax import lax
from jax.experimental import pallas as pl
from jax.experimental.pallas import tpu as pltpu
from jax.sharding import Mesh, PartitionSpec as P

DH = 128
ROWS = 128
HALF = 64
REFL = 256
PARTS = 4
KEPT_ROWS = (
    ("q", ROWS), ("k", REFL), ("v", REFL), ("w", REFL), ("u", REFL), ("z", REFL), ("yg", REFL),
    ("cols", REFL), ("cot", ROWS), ("qt", ROWS), ("pu", ROWS), ("own", 4 * DH), ("near", 4 * DH),
)
KEPT, KEPT_SIZE = {}, 0
for _name, _rows in KEPT_ROWS:
    KEPT[_name] = slice(KEPT_SIZE, KEPT_SIZE + _rows)
    KEPT_SIZE += _rows
EPS = 1e-06
EXTRA = 8
LARGE_BYTES = 63 * 1024 * 1024
SMALL_BYTES = 16 * 1024 * 1024


def halves(a):
    high = a.astype(jnp.bfloat16)
    return high, (a - high.astype(jnp.float32)).astype(jnp.bfloat16)


def dot(a, b, ca=1, cb=0):
    return lax.dot_general(a, b, (((ca,), (cb,)), ((), ())), preferred_element_type=jnp.float32)


def mm(a, b, ca=1, cb=0):
    return mm_halves(halves(a), halves(b), ca, cb)


def mm_halves(a, b, ca=1, cb=0):
    return dot(a[0], b[0], ca, cb) + (dot(a[0], b[1], ca, cb) + dot(a[1], b[0], ca, cb))


def mix(first, second):
    return jnp.concatenate([first[:HALF], second[:HALF], first[HALF:], second[HALF:]], axis=0)


def unmix(rows):
    first = jnp.concatenate([rows[:HALF], rows[ROWS : ROWS + HALF]], axis=0)
    second = jnp.concatenate([rows[HALF:ROWS], rows[ROWS + HALF :]], axis=0)
    return first, second


def place(shape, axis):
    row = lax.broadcasted_iota(jnp.int32, shape, axis)
    return (row & ROWS) + 2 * (row & (HALF - 1)) + ((row >> 6) & 1)


def seen_mask():
    frame = lax.broadcasted_iota(jnp.int32, (ROWS, REFL), 0)
    return (place((ROWS, REFL), 1) >> 1) <= frame


def fetch(pairs, sems):
    copies = [pltpu.make_async_copy(a, b, sems.at[i]) for i, (a, b) in enumerate(pairs)]
    for copy in copies:
        copy.start()
    return copies


def prepare_kernel(
    bias_ref, wb_ref, frames_any, wk_any, wq_any, wv_any, cot_any,
    send_any, kept_any, wide_any,
    frames_ref, wk_ref, wq_ref, wv_ref, cot_ref, send_ref, kept_ref, wide_ref, in_sems, out_sems,
):
    arrive = fetch(
        (
            (frames_any, frames_ref), (wk_any, wk_ref), (wq_any, wq_ref), (wv_any, wv_ref),
            (cot_any, cot_ref),
        ),
        in_sems,
    )

    def keep(name, value):
        kept_ref[KEPT[name], :] = value

    arrive[0].wait()
    frames = frames_ref[...]
    wide_ref[...] = frames.astype(jnp.float32)
    out_copies = fetch([(wide_ref, wide_any.at[i]) for i in range(PARTS)], out_sems)
    logits = dot(frames, wb_ref[...], 1, 1)
    arrive[1].wait()
    k_raw = dot(frames, wk_ref[...])
    for copy in arrive[2:]:
        copy.wait()
    q_raw = dot(frames, wq_ref[...])
    v_raw = dot(frames, wv_ref[...])
    rq = lax.rsqrt(jnp.sum(q_raw * q_raw, axis=1, keepdims=True) + EPS)
    q = q_raw * rq
    keys = mix(k_raw[:, :DH], k_raw[:, DH:])
    rk = lax.rsqrt(jnp.sum(keys * keys, axis=1, keepdims=True) + EPS)
    k = keys * rk
    v = mix(v_raw[:, :DH], v_raw[:, DH:])
    beta = 2.0 * jax.nn.sigmoid(mix(logits[:, 0:1] + bias_ref[0], logits[:, 1:2] + bias_ref[1]))
    keep("q", q)
    keep("k", k)
    keep("v", v)
    lane = lax.broadcasted_iota(jnp.int32, (REFL, DH), 1)
    rq_long = jnp.concatenate([rq, rq], axis=0)
    keep("cols", jnp.where(lane == 0, beta, jnp.where(lane == 1, rk, rq_long)))

    gram = mm(k, k, 1, 1)
    system = beta * gram
    row, col = place((ROWS, ROWS), 0), place((ROWS, ROWS), 1)
    parts = [system[:ROWS, :ROWS], system[ROWS:, ROWS:]]
    pair = ((row >> 1) == (col >> 1)) & (row > col)
    eye = jnp.where(row == col, 1.0, 0.0)
    inverse = [eye - jnp.where(pair, part, 0.0) for part in parts]
    for level in range(1, 7):
        lower = ((row >> (level + 1)) == (col >> (level + 1))) & ((row >> level) > (col >> level))
        inner = [mm(jnp.where(lower, part, 0.0), inv) for part, inv in zip(parts, inverse)]
        inverse = [inv - mm(inv, mid) for inv, mid in zip(inverse, inner)]
    corner = -mm(inverse[1], mm(system[ROWS:, :ROWS], inverse[0]))
    zero = jnp.zeros((ROWS, ROWS), jnp.float32)
    inverse = jnp.concatenate(
        [
            jnp.concatenate([inverse[0], zero], axis=1),
            jnp.concatenate([corner, inverse[1]], axis=1),
        ],
        axis=0,
    )
    wu = mm(inverse, jnp.concatenate([beta * k, beta * v], axis=1))
    w, u = wu[:, :DH], wu[:, DH:]
    keep("w", w)
    keep("u", u)
    cot = cot_ref[...].astype(jnp.float32)
    keep("cot", cot)
    scores = jnp.where(seen_mask(), mm(q, k, 1, 1), 0.0)
    pg = mm(scores, cot, 0, 0)
    zy = mm(inverse, jnp.concatenate([k, pg], axis=1), 0, 0)
    keep("z", zy[:, :DH])
    keep("yg", zy[:, DH:])
    first, second = pl.ds(0, KEPT["qt"].start), pl.ds(KEPT["qt"].start, 2 * ROWS)
    out_copies.append(
        pltpu.make_async_copy(kept_ref.at[first], kept_any.at[first], out_sems.at[PARTS])
    )
    out_copies[-1].start()
    kwu = mm(k, wu, 0, 0)
    pwu = mm(scores, wu)
    qt = q - pwu[:, :DH]
    keep("qt", qt)
    keep("pu", pwu[:, DH:])
    send_ref[0] = eye_like() - kwu[:, :DH]
    send_ref[1] = kwu[:, DH:]
    send_ref[2] = mm(cot, qt, 0, 0)
    for i, (a, b) in enumerate(
        ((send_ref, send_any), (kept_ref.at[second], kept_any.at[second]))
    ):
        out_copies.append(pltpu.make_async_copy(a, b, out_sems.at[PARTS + 1 + i]))
        out_copies[-1].start()
    for copy in out_copies:
        copy.wait()


def eye_like():
    row = lax.broadcasted_iota(jnp.int32, (DH, DH), 0)
    col = lax.broadcasted_iota(jnp.int32, (DH, DH), 1)
    return jnp.where(row == col, 1.0, 0.0)


def compose_group(me, parts):
    last = len(parts) - 1
    maps = [halves(part[0]) for part in parts]
    ahead = [jnp.concatenate([parts[0][0], parts[0][1]], axis=1)]
    behind = [jnp.concatenate([parts[last][0], parts[last][2]], axis=0)]
    for i in range(1, last + 1):
        moved = mm_halves(maps[i], halves(ahead[-1]))
        ahead.append(jnp.concatenate([moved[:, :DH], moved[:, DH:] + parts[i][1]], axis=1))
        j = last - i
        moved = mm_halves(halves(behind[-1]), maps[j])
        behind.append(jnp.concatenate([moved[:DH], moved[DH:] + parts[j][2]], axis=0))
    whole = (ahead[last][:, :DH], ahead[last][:, DH:], behind[last][DH:])
    eye, zero = eye_like(), jnp.zeros((DH, DH), jnp.float32)
    before = jnp.concatenate([eye, zero], axis=1)
    after = jnp.concatenate([eye, zero], axis=0)
    for i in range(last):
        before = jnp.where(me == i + 1, ahead[i], before)
        after = jnp.where(me == last - 1 - i, behind[i], after)
    return whole, (before[:, :DH], before[:, DH:], after[:DH], after[DH:])


def group_kernel(
    place_ref, parts_ref, kept_in, total_ref, kept_any, whole_ref, around_ref, sem, *, axis, name
):
    del kept_in
    parts = [tuple(parts_ref[i, j] for j in range(3)) for i in range(PARTS)]
    whole, around = compose_group(place_ref[axis], parts)
    for i, value in enumerate(around):
        around_ref[DH * i : DH * i + DH] = value
    rows = pl.ds(KEPT[name].start, 4 * DH)
    copy = pltpu.make_async_copy(around_ref, kept_any.at[rows], sem)
    copy.start()
    if total_ref.shape[1] == DH:
        for i, value in enumerate(whole):
            total_ref[i] = value
    else:
        for i, value in enumerate(whole):
            whole_ref[i] = value
        rows = DH // PARTS
        mine = pl.ds(pl.multiple_of(place_ref[0] * rows, rows), rows)
        for i in range(3):
            total_ref[i] = whole_ref[i, mine, :]
    copy.wait()


def group_scan(parts, kept, place, axis, name, rows):
    return pl.pallas_call(
        functools.partial(group_kernel, axis=axis, name=name),
        out_shape=(f32(3, rows, DH), kept),
        in_specs=[SMEM, VMEM, HBM],
        out_specs=(VMEM, HBM),
        scratch_shapes=[
            pltpu.VMEM((3, DH, DH), jnp.float32),
            pltpu.VMEM((4 * DH, DH), jnp.float32),
            pltpu.SemaphoreType.DMA,
        ],
        input_output_aliases={2: 1},
        compiler_params=pltpu.CompilerParams(vmem_limit_bytes=SMALL_BYTES),
        name="group_scan",
    )(place, parts, kept)


def finish_kernel(place_ref, far_ref, kept_ref, out_ref, pieces_ref, tiles_ref):
    me = place_ref[2]
    own_ref = kept_ref[KEPT["own"], :].reshape(4, DH, DH)
    near_ref = kept_ref[KEPT["near"], :].reshape(4, DH, DH)
    inward = mm(own_ref[0], jnp.concatenate([near_ref[0], near_ref[1]], axis=1))
    inward_map, inward_shift = inward[:, :DH], inward[:, DH:] + own_ref[1]
    outward = mm(jnp.concatenate([near_ref[2], near_ref[3]], axis=0), own_ref[2])
    outward_map, outward_shift = outward[:DH], outward[DH:] + own_ref[3]

    def far(group, which):
        at = (-1, PARTS - 2, 2 * PARTS - 4)[which] + group
        return jnp.concatenate([far_ref[i, at] for i in range(PARTS)], axis=0)

    entering = jnp.where(me > 0, far(0, 1), 0.0)
    leaving = jnp.where(me < PARTS - 1, far(PARTS - 1, 2), 0.0)
    for i in range(1, PARTS - 1):
        j = PARTS - 1 - i
        entering = jnp.where(me > i, mm(far(i, 0), entering) + far(i, 1), entering)
        leaving = jnp.where(me < j, mm(leaving, far(j, 0)) + far(j, 2), leaving)
    entering = mm(inward_map, entering) + inward_shift
    leaving = mm(leaving, outward_map) + outward_shift
    q, k, v = kept_ref[KEPT["q"], :], kept_ref[KEPT["k"], :], kept_ref[KEPT["v"], :]
    cot = kept_ref[KEPT["cot"], :]
    cols = kept_ref[KEPT["cols"], :]
    beta, rk, rq = cols[:, 0:1], cols[:, 1:2], cols[:ROWS, 2:3]
    out_ref[...] = (mm(kept_ref[KEPT["qt"], :], entering) + kept_ref[KEPT["pu"], :]).astype(jnp.bfloat16)
    fresh = kept_ref[KEPT["u"], :] - mm(kept_ref[KEPT["w"], :], entering)
    y = kept_ref[KEPT["yg"], :] + mm(kept_ref[KEPT["z"], :], leaving, 1, 1)
    gram = mm(k, k, 1, 1)
    row, col = place((REFL, REFL), 0), place((REFL, REFL), 1)
    d_system = jnp.where(row > col, -mm(y, fresh, 1, 1), 0.0)
    d_scores = jnp.where(seen_mask(), mm(cot, fresh, 1, 1), 0.0)
    d_query = mm(cot, entering, 1, 1) + mm(d_scores, k)
    error = v - mm(k, entering)
    d_beta = jnp.sum(y * error, axis=1, keepdims=True) + jnp.sum(
        d_system * gram, axis=1, keepdims=True
    )
    by = beta * y
    d_gram = beta * d_system
    d_keys = (
        mm(d_scores, q, 0, 0)
        + mm(fresh, leaving)
        - mm(by, entering, 1, 1)
        + mm(d_gram, k)
        + mm(d_gram, k, 0, 0)
    )
    d_query = rq * (d_query - q * jnp.sum(d_query * q, axis=1, keepdims=True))
    d_keys = rk * (d_keys - k * jnp.sum(d_keys * k, axis=1, keepdims=True))
    d_logits = d_beta * beta * (1.0 - 0.5 * beta)
    l_first, l_second = unmix(d_logits)
    lane2 = lax.broadcasted_iota(jnp.int32, (ROWS, 2), 1)
    g_logits_f32 = jnp.where(lane2 == 0, l_first, l_second)
    g_query = d_query.astype(jnp.bfloat16)
    k_first, k_second = unmix(d_keys)
    v_first, v_second = unmix(by)
    g_keys = jnp.concatenate([k_first, k_second], axis=1).astype(jnp.bfloat16)
    g_values = jnp.concatenate([v_first, v_second], axis=1).astype(jnp.bfloat16)
    tiles_ref[:, :DH] = g_query
    tiles_ref[:, DH : 3 * DH] = g_keys
    tiles_ref[:, 3 * DH : 5 * DH] = g_values
    lane = lax.broadcasted_iota(jnp.int32, (ROWS, DH), 1)
    padded = jnp.where(lane == 0, l_first, jnp.where(lane == 1, l_second, 0.0))
    tiles_ref[:, 5 * DH :] = padded.astype(jnp.bfloat16)
    wide = jnp.float32
    tiles = (g_query, g_keys[:, :DH], g_keys[:, DH:], g_values[:, :DH])
    shared = g_values[:, DH:].astype(wide)
    turned = padded.astype(jnp.bfloat16).astype(wide).T
    bias_row = jnp.sum(g_logits_f32, axis=0, keepdims=True)
    bias_lanes = jnp.where(
        lax.broadcasted_iota(jnp.int32, (1, DH), 1) == 0, bias_row[:, 0:1], bias_row[:, 1:2]
    )
    for i in range(PARTS):
        pieces_ref[i, :ROWS] = tiles[i].astype(wide)
        pieces_ref[i, ROWS : 2 * ROWS] = shared
        pieces_ref[i, 2 * ROWS :] = jnp.concatenate(
            [turned[:2], bias_lanes, jnp.zeros((EXTRA - 3, DH), wide)], axis=0
        )


def f32(*shape):
    return jax.ShapeDtypeStruct(shape, jnp.float32)


SMEM = pl.BlockSpec(memory_space=pltpu.SMEM)
VMEM = pl.BlockSpec(memory_space=pltpu.VMEM)
ANY = pl.BlockSpec(memory_space=pl.ANY)
HBM = pl.BlockSpec(memory_space=pltpu.HBM)


def held(a):
    return pltpu.VMEM(a.shape, a.dtype)


def prepare(bias, w_beta, *large):
    send, kept, wide = f32(3, DH, DH), f32(KEPT_SIZE, DH), f32(PARTS, ROWS, 1024)
    return pl.pallas_call(
        prepare_kernel,
        out_shape=(send, kept, wide),
        in_specs=[SMEM, VMEM] + [HBM] * 5,
        out_specs=(HBM, HBM, HBM),
        scratch_shapes=[
            held(a) for a in (*large, send, f32(KEPT["own"].start, DH), f32(ROWS, 1024))
        ]
        + [pltpu.SemaphoreType.DMA((5,)), pltpu.SemaphoreType.DMA((PARTS + 3,))],
        compiler_params=pltpu.CompilerParams(vmem_limit_bytes=LARGE_BYTES),
        name="prepare",
    )(bias, w_beta, *large)


def finish(place, far, kept):
    return pl.pallas_call(
        finish_kernel,
        out_shape=(
            jax.ShapeDtypeStruct((ROWS, DH), jnp.bfloat16),
            f32(PARTS, 2 * ROWS + EXTRA, DH),
            jax.ShapeDtypeStruct((ROWS, 6 * DH), jnp.bfloat16),
        ),
        in_specs=[SMEM, VMEM, VMEM],
        compiler_params=pltpu.CompilerParams(vmem_limit_bytes=SMALL_BYTES),
        name="finish",
    )(place, far, kept)


def side_kernel(place_ref, tiles_ref, wb_ref, wq_ref, wk_ref, wv_ref, *refs):
    out_refs, sum_ref = refs[:-1], refs[-1]
    sum_ref[...] = (
        dot(tiles_ref[:, :DH], wq_ref[...], 1, 1)
        + dot(tiles_ref[:, DH : 3 * DH], wk_ref[...], 1, 1)
        + dot(tiles_ref[:, 3 * DH : 5 * DH], wv_ref[...], 1, 1)
        + dot(tiles_ref[:, 5 * DH : 5 * DH + 2], wb_ref[...])
    )
    chip, core = place_ref[3], place_ref[4]
    for i, out_ref in enumerate(out_refs):
        pair = 2 * lax.rem(chip + i, PARTS)
        for j, block in enumerate((pair + core, pair + 1 - core)):
            out_ref[j] = sum_ref[:, pl.ds(pl.multiple_of(block * DH, DH), DH)]


def side(place, *args):
    return pl.pallas_call(
        side_kernel,
        out_shape=(f32(2, ROWS, DH),) * PARTS,
        in_specs=[SMEM] + [VMEM] * len(args),
        scratch_shapes=[pltpu.VMEM((ROWS, 2 * PARTS * DH), jnp.float32)],
        compiler_params=pltpu.CompilerParams(vmem_limit_bytes=SMALL_BYTES),
        cost_estimate=pl.CostEstimate(flops=170_000_000, bytes_accessed=3_000_000, transcendentals=0),
        name="side",
    )(place, *args)


def narrow_kernel(frames_ref, narrow_ref):
    narrow_ref[...] = frames_ref[...].astype(jnp.bfloat16)


def narrow(frames):
    return pl.pallas_call(
        narrow_kernel,
        out_shape=jax.ShapeDtypeStruct(frames.shape, jnp.bfloat16),
        in_specs=[VMEM],
        out_specs=VMEM,
        compiler_params=pltpu.CompilerParams(vmem_limit_bytes=SMALL_BYTES),
        cost_estimate=pl.CostEstimate(flops=1_000_000, bytes_accessed=3_000_000, transcendentals=0),
        name="narrow",
    )(frames)


def weigh_kernel(place_ref, pieces_ref, frames_ref, sums_ref):
    quarter = pl.ds(pl.multiple_of(place_ref[0] * 256, 256), 256)
    total = jnp.zeros((1024, DH), jnp.float32)
    corner = jnp.zeros((256, DH), jnp.float32)
    beta = jnp.zeros((2, 256), jnp.float32)
    bias = jnp.zeros((1, DH), jnp.float32)
    for i in range(PARTS):
        piece = pieces_ref[i, : 2 * ROWS].astype(jnp.bfloat16)
        rows = pieces_ref[i, 2 * ROWS :]
        bias = bias + rows[2:3]
        beta = beta + dot(rows[:2].astype(jnp.bfloat16), frames_ref[i, :, quarter])
        total = total + dot(frames_ref[i], piece[:ROWS], 0, 0)
        corner = corner + dot(frames_ref[i, :, quarter], piece[ROWS:], 0, 0)
    extra = [beta[:, :DH], beta[:, DH:], bias, jnp.zeros((EXTRA - 5, DH), jnp.float32)]
    extra = jnp.concatenate(extra, axis=0)
    total = jnp.concatenate([total, corner], axis=0)
    rows = total.shape[0] // (PARTS * PARTS)
    for i in range(PARTS):
        for j in range(PARTS):
            block = PARTS * j + i
            sums_ref[i, rows * j : rows * j + rows] = total[rows * block : rows * block + rows]
        sums_ref[i, rows * PARTS :] = extra


def weigh(place, pieces, frames):
    return pl.pallas_call(
        weigh_kernel,
        out_shape=f32(PARTS, 1280 // PARTS + EXTRA, DH),
        in_specs=[SMEM, VMEM, VMEM],
        compiler_params=pltpu.CompilerParams(vmem_limit_bytes=SMALL_BYTES),
        name="weigh",
    )(place, pieces, frames)


def lay_kernel(whole_ref, *refs):
    heads = refs[:2]
    query_any, keys_any, values_any, beta_any, bias_any, frames_any = refs[2:8]
    beta_ref, bias_ref, sum_ref, sems = refs[8:]
    left, right = pl.ds(0, DH), pl.ds(DH, DH)
    full = pl.ds(0, 1024)
    pairs = [
        (whole_ref.at[0, full], query_any),
        (whole_ref.at[1, full], keys_any.at[:, left]),
        (whole_ref.at[2, full], keys_any.at[:, right]),
        (whole_ref.at[3, full], values_any.at[:, left]),
    ]
    for i in range(PARTS):
        pairs.append(
            (whole_ref.at[i, pl.ds(1024, 256)], values_any.at[pl.ds(256 * i, 256), right])
        )
    copies = fetch(pairs, sems)
    rows = [whole_ref[i, 1280:] for i in range(PARTS)]
    beta_ref[...] = jnp.concatenate(
        [row[2 * half : 2 * half + 2] for row in rows for half in range(2)], axis=1
    )
    bias_ref[...] = rows[0][4:5, :2]
    sum_ref[...] = (heads[0][...] + heads[1][...]).astype(jnp.bfloat16)
    small = ((beta_ref, beta_any), (bias_ref, bias_any), (sum_ref, frames_any))
    for i, (a, b) in enumerate(small):
        copies.append(pltpu.make_async_copy(a, b, sems.at[8 + i]))
        copies[-1].start()
    for copy in copies:
        copy.wait()


def lay(whole, heads):
    frames = jax.ShapeDtypeStruct((ROWS, DH), jnp.bfloat16)
    return pl.pallas_call(
        lay_kernel,
        out_shape=(
            f32(1024, DH), f32(1024, 2 * DH), f32(1024, 2 * DH), f32(2, 1024), f32(1, 2), frames,
        ),
        in_specs=[VMEM] * 3,
        out_specs=(HBM,) * 6,
        scratch_shapes=[
            held(f32(2, 1024)), held(f32(1, 2)), held(frames), pltpu.SemaphoreType.DMA((11,)),
        ],
        compiler_params=pltpu.CompilerParams(vmem_limit_bytes=SMALL_BYTES),
        name="lay",
    )(whole, *heads)


def spread(a, axis):
    return lax.all_to_all(jnp.broadcast_to(a[None], (PARTS, *a.shape)), axis, 0, 0, tiled=True)


def trade(a, axis):
    return lax.all_to_all(a, axis, 0, 0, tiled=True)


def shift(a, axis, steps):
    size = lax.axis_size(axis)
    return lax.ppermute(a, axis, [(i, (i + steps) % size) for i in range(size)])


def local(frames, w_query, w_keys, w_values, w_beta, beta_bias, cotangent):
    place = jnp.stack(
        [lax.axis_index("x"), lax.axis_index("zl"), lax.axis_index("zh")]
        + [lax.axis_index("y"), lax.axis_index("core")]
    )
    beta_turned = w_beta.T
    own, kept, wide_frames = prepare(
        beta_bias, beta_turned, frames, w_keys, w_query, w_values, cotangent
    )
    row, wide_frames = lax.optimization_barrier((lax.all_gather(own, "x"), wide_frames))
    group_frames = trade(wide_frames, "x")
    total, kept = group_scan(row, kept, place, 0, "own", DH)
    total, kept = group_scan(lax.all_gather(total, "zl"), kept, place, 1, "near", DH // PARTS)
    far = lax.all_gather(total, "zh")
    far = jnp.concatenate([far[1:-1, 0], far[:-1, 1], far[1:, 2]], axis=0)
    far = lax.all_gather(far, "x")
    outputs, pieces, tiles = finish(place, far, kept)
    pieces, group_frames = trade(pieces, "x"), narrow(group_frames)
    heads = side(place, tiles, beta_turned, w_query, w_keys, w_values)
    pieces, group_frames, heads = lax.optimization_barrier((pieces, group_frames, heads))
    sums = weigh(place, pieces, group_frames)
    shared = heads[0]
    for i in range(1, PARTS):
        shared = shared + shift(heads[i], "y", i)
    part = jnp.sum(trade(sums, "zl"), axis=0)
    part, extra = part[:320], part[320:]
    part = jnp.concatenate(
        [part.reshape(PARTS, 80, DH), jnp.broadcast_to(extra[None], (PARTS, EXTRA, DH))], axis=1
    )
    partial = (shared[0], shift(shared[1], "core", 1))
    part = jnp.sum(trade(part, "zh"), axis=0)
    part, extra = part[:80], part[80:]
    part = lax.all_gather(part, ("zh", "zl")).reshape(1280, DH)
    part, partial = lax.optimization_barrier((part, partial))
    whole = jnp.concatenate([part, extra], axis=0)
    grad_query, grad_keys, grad_values, beta_rows, bias_row, grad_frames = lay(
        spread(whole, "x"), partial
    )
    grad_beta = beta_rows.T
    grad_bias = bias_row.reshape(2)
    return (outputs, grad_frames, grad_query, grad_keys, grad_values, grad_beta, grad_bias)


def solution(mesh):
    fine = Mesh(mesh.devices.reshape(4, 4, 4, 4, 2), ("zh", "zl", "x", "y", "core"))
    ctx, head = ("zh", "zl", "x"), ("y", "core")
    in_specs = (
        P(ctx, None),
        P(None, head),
        P(None, head),
        P(None, head),
        P(None, head),
        P(head),
        P(ctx, head),
    )
    out_specs = (
        P(ctx, head),
        P(ctx, head),
        P(None, head),
        P(None, head),
        P(None, head),
        P(None, head),
        P(head),
    )
    return jax.shard_map(local, mesh=fine, in_specs=in_specs, out_specs=out_specs, check_vma=False)
```

```python
import functools

import jax
import jax.numpy as jnp
from jax import lax
from jax.experimental import pallas as pl
from jax.experimental.pallas import tpu as pltpu
from jax.sharding import Mesh, PartitionSpec as P

DH = 128
ROWS = 128
HALF = 64
REFL = 256
PARTS = 4
KEPT_ROWS = (
    ("q", ROWS), ("k", REFL), ("v", REFL), ("w", REFL), ("u", REFL), ("z", REFL), ("yg", REFL),
    ("cols", REFL), ("cot", ROWS), ("qt", ROWS), ("pu", ROWS), ("own", 4 * DH), ("near", 4 * DH),
)
KEPT, KEPT_SIZE = {}, 0
for _name, _rows in KEPT_ROWS:
    KEPT[_name] = slice(KEPT_SIZE, KEPT_SIZE + _rows)
    KEPT_SIZE += _rows
EPS = 1e-06
EXTRA = 8
LARGE_BYTES = 63 * 1024 * 1024
SMALL_BYTES = 16 * 1024 * 1024


def halves(a):
    high = a.astype(jnp.bfloat16)
    return high, (a - high.astype(jnp.float32)).astype(jnp.bfloat16)


def dot(a, b, ca=1, cb=0):
    return lax.dot_general(a, b, (((ca,), (cb,)), ((), ())), preferred_element_type=jnp.float32)


def mm(a, b, ca=1, cb=0):
    return mm_halves(halves(a), halves(b), ca, cb)


def mm_halves(a, b, ca=1, cb=0):
    return dot(a[0], b[0], ca, cb) + (dot(a[0], b[1], ca, cb) + dot(a[1], b[0], ca, cb))


def mix(first, second):
    return jnp.concatenate([first[:HALF], second[:HALF], first[HALF:], second[HALF:]], axis=0)


def unmix(rows):
    first = jnp.concatenate([rows[:HALF], rows[ROWS : ROWS + HALF]], axis=0)
    second = jnp.concatenate([rows[HALF:ROWS], rows[ROWS + HALF :]], axis=0)
    return first, second


def place(shape, axis):
    row = lax.broadcasted_iota(jnp.int32, shape, axis)
    return (row & ROWS) + 2 * (row & (HALF - 1)) + ((row >> 6) & 1)


def seen_mask():
    frame = lax.broadcasted_iota(jnp.int32, (ROWS, REFL), 0)
    return (place((ROWS, REFL), 1) >> 1) <= frame


def fetch(pairs, sems):
    copies = [pltpu.make_async_copy(a, b, sems.at[i]) for i, (a, b) in enumerate(pairs)]
    for copy in copies:
        copy.start()
    return copies


def prepare_kernel(
    bias_ref, wb_ref, frames_any, wk_any, wq_any, wv_any, cot_any,
    send_any, kept_any, wide_any,
    frames_ref, wk_ref, wq_ref, wv_ref, cot_ref, send_ref, kept_ref, wide_ref, in_sems, out_sems,
):
    arrive = fetch(
        (
            (frames_any, frames_ref), (wk_any, wk_ref), (wq_any, wq_ref), (wv_any, wv_ref),
            (cot_any, cot_ref),
        ),
        in_sems,
    )

    def keep(name, value):
        kept_ref[KEPT[name], :] = value

    arrive[0].wait()
    frames = frames_ref[...]
    wide_ref[...] = frames.astype(jnp.float32)
    out_copies = fetch([(wide_ref, wide_any.at[i]) for i in range(PARTS)], out_sems)
    logits = dot(frames, wb_ref[...], 1, 1)
    arrive[1].wait()
    k_raw = dot(frames, wk_ref[...])
    for copy in arrive[2:]:
        copy.wait()
    q_raw = dot(frames, wq_ref[...])
    v_raw = dot(frames, wv_ref[...])
    rq = lax.rsqrt(jnp.sum(q_raw * q_raw, axis=1, keepdims=True) + EPS)
    q = q_raw * rq
    keys = mix(k_raw[:, :DH], k_raw[:, DH:])
    rk = lax.rsqrt(jnp.sum(keys * keys, axis=1, keepdims=True) + EPS)
    k = keys * rk
    v = mix(v_raw[:, :DH], v_raw[:, DH:])
    beta = 2.0 * jax.nn.sigmoid(mix(logits[:, 0:1] + bias_ref[0], logits[:, 1:2] + bias_ref[1]))
    keep("q", q)
    keep("k", k)
    keep("v", v)
    lane = lax.broadcasted_iota(jnp.int32, (REFL, DH), 1)
    rq_long = jnp.concatenate([rq, rq], axis=0)
    keep("cols", jnp.where(lane == 0, beta, jnp.where(lane == 1, rk, rq_long)))

    gram = mm(k, k, 1, 1)
    system = beta * gram
    row, col = place((ROWS, ROWS), 0), place((ROWS, ROWS), 1)
    parts = [system[:ROWS, :ROWS], system[ROWS:, ROWS:]]
    pair = ((row >> 1) == (col >> 1)) & (row > col)
    eye = jnp.where(row == col, 1.0, 0.0)
    inverse = [eye - jnp.where(pair, part, 0.0) for part in parts]
    for level in range(1, 7):
        lower = ((row >> (level + 1)) == (col >> (level + 1))) & ((row >> level) > (col >> level))
        inner = [mm(jnp.where(lower, part, 0.0), inv) for part, inv in zip(parts, inverse)]
        inverse = [inv - mm(inv, mid) for inv, mid in zip(inverse, inner)]
    corner = -mm(inverse[1], mm(system[ROWS:, :ROWS], inverse[0]))
    zero = jnp.zeros((ROWS, ROWS), jnp.float32)
    inverse = jnp.concatenate(
        [
            jnp.concatenate([inverse[0], zero], axis=1),
            jnp.concatenate([corner, inverse[1]], axis=1),
        ],
        axis=0,
    )
    wu = mm(inverse, jnp.concatenate([beta * k, beta * v], axis=1))
    w, u = wu[:, :DH], wu[:, DH:]
    keep("w", w)
    keep("u", u)
    cot = cot_ref[...].astype(jnp.float32)
    keep("cot", cot)
    scores = jnp.where(seen_mask(), mm(q, k, 1, 1), 0.0)
    pg = mm(scores, cot, 0, 0)
    zy = mm(inverse, jnp.concatenate([k, pg], axis=1), 0, 0)
    keep("z", zy[:, :DH])
    keep("yg", zy[:, DH:])
    first, second = pl.ds(0, KEPT["qt"].start), pl.ds(KEPT["qt"].start, 2 * ROWS)
    out_copies.append(
        pltpu.make_async_copy(kept_ref.at[first], kept_any.at[first], out_sems.at[PARTS])
    )
    out_copies[-1].start()
    kwu = mm(k, wu, 0, 0)
    pwu = mm(scores, wu)
    qt = q - pwu[:, :DH]
    keep("qt", qt)
    keep("pu", pwu[:, DH:])
    send_ref[0] = eye_like() - kwu[:, :DH]
    send_ref[1] = kwu[:, DH:]
    send_ref[2] = mm(cot, qt, 0, 0)
    for i, (a, b) in enumerate(
        ((send_ref, send_any), (kept_ref.at[second], kept_any.at[second]))
    ):
        out_copies.append(pltpu.make_async_copy(a, b, out_sems.at[PARTS + 1 + i]))
        out_copies[-1].start()
    for copy in out_copies:
        copy.wait()


def eye_like():
    row = lax.broadcasted_iota(jnp.int32, (DH, DH), 0)
    col = lax.broadcasted_iota(jnp.int32, (DH, DH), 1)
    return jnp.where(row == col, 1.0, 0.0)


def compose_group(me, parts):
    last = len(parts) - 1
    maps = [halves(part[0]) for part in parts]
    ahead = [jnp.concatenate([parts[0][0], parts[0][1]], axis=1)]
    behind = [jnp.concatenate([parts[last][0], parts[last][2]], axis=0)]
    for i in range(1, last + 1):
        moved = mm_halves(maps[i], halves(ahead[-1]))
        ahead.append(jnp.concatenate([moved[:, :DH], moved[:, DH:] + parts[i][1]], axis=1))
        j = last - i
        moved = mm_halves(halves(behind[-1]), maps[j])
        behind.append(jnp.concatenate([moved[:DH], moved[DH:] + parts[j][2]], axis=0))
    whole = (ahead[last][:, :DH], ahead[last][:, DH:], behind[last][DH:])
    eye, zero = eye_like(), jnp.zeros((DH, DH), jnp.float32)
    before = jnp.concatenate([eye, zero], axis=1)
    after = jnp.concatenate([eye, zero], axis=0)
    for i in range(last):
        before = jnp.where(me == i + 1, ahead[i], before)
        after = jnp.where(me == last - 1 - i, behind[i], after)
    return whole, (before[:, :DH], before[:, DH:], after[:DH], after[DH:])


def group_kernel(
    place_ref, parts_ref, kept_in, total_ref, kept_any, whole_ref, around_ref, sem, *, axis, name
):
    del kept_in
    parts = [tuple(parts_ref[i, j] for j in range(3)) for i in range(PARTS)]
    whole, around = compose_group(place_ref[axis], parts)
    for i, value in enumerate(around):
        around_ref[DH * i : DH * i + DH] = value
    rows = pl.ds(KEPT[name].start, 4 * DH)
    copy = pltpu.make_async_copy(around_ref, kept_any.at[rows], sem)
    copy.start()
    if total_ref.shape[1] == DH:
        for i, value in enumerate(whole):
            total_ref[i] = value
    else:
        for i, value in enumerate(whole):
            whole_ref[i] = value
        rows = DH // PARTS
        mine = pl.ds(pl.multiple_of(place_ref[0] * rows, rows), rows)
        for i in range(3):
            total_ref[i] = whole_ref[i, mine, :]
    copy.wait()


def group_scan(parts, kept, place, axis, name, rows):
    return pl.pallas_call(
        functools.partial(group_kernel, axis=axis, name=name),
        out_shape=(f32(3, rows, DH), kept),
        in_specs=[SMEM, VMEM, HBM],
        out_specs=(VMEM, HBM),
        scratch_shapes=[
            pltpu.VMEM((3, DH, DH), jnp.float32),
            pltpu.VMEM((4 * DH, DH), jnp.float32),
            pltpu.SemaphoreType.DMA,
        ],
        input_output_aliases={2: 1},
        compiler_params=pltpu.CompilerParams(vmem_limit_bytes=SMALL_BYTES),
        name="group_scan",
    )(place, parts, kept)


def finish_kernel(place_ref, far_ref, kept_ref, out_ref, pieces_ref, tiles_ref):
    me = place_ref[2]
    own_ref = kept_ref[KEPT["own"], :].reshape(4, DH, DH)
    near_ref = kept_ref[KEPT["near"], :].reshape(4, DH, DH)
    inward = mm(own_ref[0], jnp.concatenate([near_ref[0], near_ref[1]], axis=1))
    inward_map, inward_shift = inward[:, :DH], inward[:, DH:] + own_ref[1]
    outward = mm(jnp.concatenate([near_ref[2], near_ref[3]], axis=0), own_ref[2])
    outward_map, outward_shift = outward[:DH], outward[DH:] + own_ref[3]

    def far(group, which):
        at = (-1, PARTS - 2, 2 * PARTS - 4)[which] + group
        return jnp.concatenate([far_ref[i, at] for i in range(PARTS)], axis=0)

    entering = jnp.where(me > 0, far(0, 1), 0.0)
    leaving = jnp.where(me < PARTS - 1, far(PARTS - 1, 2), 0.0)
    for i in range(1, PARTS - 1):
        j = PARTS - 1 - i
        entering = jnp.where(me > i, mm(far(i, 0), entering) + far(i, 1), entering)
        leaving = jnp.where(me < j, mm(leaving, far(j, 0)) + far(j, 2), leaving)
    entering = mm(inward_map, entering) + inward_shift
    leaving = mm(leaving, outward_map) + outward_shift
    q, k, v = kept_ref[KEPT["q"], :], kept_ref[KEPT["k"], :], kept_ref[KEPT["v"], :]
    cot = kept_ref[KEPT["cot"], :]
    cols = kept_ref[KEPT["cols"], :]
    beta, rk, rq = cols[:, 0:1], cols[:, 1:2], cols[:ROWS, 2:3]
    out_ref[...] = (mm(kept_ref[KEPT["qt"], :], entering) + kept_ref[KEPT["pu"], :]).astype(jnp.bfloat16)
    fresh = kept_ref[KEPT["u"], :] - mm(kept_ref[KEPT["w"], :], entering)
    y = kept_ref[KEPT["yg"], :] + mm(kept_ref[KEPT["z"], :], leaving, 1, 1)
    gram = mm(k, k, 1, 1)
    row, col = place((REFL, REFL), 0), place((REFL, REFL), 1)
    d_system = jnp.where(row > col, -mm(y, fresh, 1, 1), 0.0)
    d_scores = jnp.where(seen_mask(), mm(cot, fresh, 1, 1), 0.0)
    d_query = mm(cot, entering, 1, 1) + mm(d_scores, k)
    error = v - mm(k, entering)
    d_beta = jnp.sum(y * error, axis=1, keepdims=True) + jnp.sum(
        d_system * gram, axis=1, keepdims=True
    )
    by = beta * y
    d_gram = beta * d_system
    d_keys = (
        mm(d_scores, q, 0, 0)
        + mm(fresh, leaving)
        - mm(by, entering, 1, 1)
        + mm(d_gram, k)
        + mm(d_gram, k, 0, 0)
    )
    d_query = rq * (d_query - q * jnp.sum(d_query * q, axis=1, keepdims=True))
    d_keys = rk * (d_keys - k * jnp.sum(d_keys * k, axis=1, keepdims=True))
    d_logits = d_beta * beta * (1.0 - 0.5 * beta)
    l_first, l_second = unmix(d_logits)
    lane2 = lax.broadcasted_iota(jnp.int32, (ROWS, 2), 1)
    g_logits_f32 = jnp.where(lane2 == 0, l_first, l_second)
    g_query = d_query.astype(jnp.bfloat16)
    k_first, k_second = unmix(d_keys)
    v_first, v_second = unmix(by)
    g_keys = jnp.concatenate([k_first, k_second], axis=1).astype(jnp.bfloat16)
    g_values = jnp.concatenate([v_first, v_second], axis=1).astype(jnp.bfloat16)
    tiles_ref[:, :DH] = g_query
    tiles_ref[:, DH : 3 * DH] = g_keys
    tiles_ref[:, 3 * DH : 5 * DH] = g_values
    lane = lax.broadcasted_iota(jnp.int32, (ROWS, DH), 1)
    padded = jnp.where(lane == 0, l_first, jnp.where(lane == 1, l_second, 0.0))
    tiles_ref[:, 5 * DH :] = padded.astype(jnp.bfloat16)
    wide = jnp.float32
    tiles = (g_query, g_keys[:, :DH], g_keys[:, DH:], g_values[:, :DH])
    shared = g_values[:, DH:].astype(wide)
    turned = padded.astype(jnp.bfloat16).astype(wide).T
    bias_row = jnp.sum(g_logits_f32, axis=0, keepdims=True)
    bias_lanes = jnp.where(
        lax.broadcasted_iota(jnp.int32, (1, DH), 1) == 0, bias_row[:, 0:1], bias_row[:, 1:2]
    )
    for i in range(PARTS):
        pieces_ref[i, :ROWS] = tiles[i].astype(wide)
        pieces_ref[i, ROWS : 2 * ROWS] = shared
        pieces_ref[i, 2 * ROWS :] = jnp.concatenate(
            [turned[:2], bias_lanes, jnp.zeros((EXTRA - 3, DH), wide)], axis=0
        )


def f32(*shape):
    return jax.ShapeDtypeStruct(shape, jnp.float32)


SMEM = pl.BlockSpec(memory_space=pltpu.SMEM)
VMEM = pl.BlockSpec(memory_space=pltpu.VMEM)
ANY = pl.BlockSpec(memory_space=pl.ANY)
HBM = pl.BlockSpec(memory_space=pltpu.HBM)


def held(a):
    return pltpu.VMEM(a.shape, a.dtype)


def prepare(bias, w_beta, *large):
    send, kept, wide = f32(3, DH, DH), f32(KEPT_SIZE, DH), f32(PARTS, ROWS, 1024)
    return pl.pallas_call(
        prepare_kernel,
        out_shape=(send, kept, wide),
        in_specs=[SMEM, VMEM] + [HBM] * 5,
        out_specs=(HBM, HBM, HBM),
        scratch_shapes=[
            held(a) for a in (*large, send, f32(KEPT["own"].start, DH), f32(ROWS, 1024))
        ]
        + [pltpu.SemaphoreType.DMA((5,)), pltpu.SemaphoreType.DMA((PARTS + 3,))],
        compiler_params=pltpu.CompilerParams(vmem_limit_bytes=LARGE_BYTES),
        name="prepare",
    )(bias, w_beta, *large)


def finish(place, far, kept):
    return pl.pallas_call(
        finish_kernel,
        out_shape=(
            jax.ShapeDtypeStruct((ROWS, DH), jnp.bfloat16),
            f32(PARTS, 2 * ROWS + EXTRA, DH),
            jax.ShapeDtypeStruct((ROWS, 6 * DH), jnp.bfloat16),
        ),
        in_specs=[SMEM, VMEM, VMEM],
        compiler_params=pltpu.CompilerParams(vmem_limit_bytes=SMALL_BYTES),
        name="finish",
    )(place, far, kept)


def side_kernel(place_ref, tiles_ref, wb_ref, wq_ref, wk_ref, wv_ref, *refs):
    out_refs, sum_ref = refs[:-1], refs[-1]
    sum_ref[...] = (
        dot(tiles_ref[:, :DH], wq_ref[...], 1, 1)
        + dot(tiles_ref[:, DH : 3 * DH], wk_ref[...], 1, 1)
        + dot(tiles_ref[:, 3 * DH : 5 * DH], wv_ref[...], 1, 1)
        + dot(tiles_ref[:, 5 * DH : 5 * DH + 2], wb_ref[...])
    )
    chip, core = place_ref[3], place_ref[4]
    for i, out_ref in enumerate(out_refs):
        pair = 2 * lax.rem(chip + i, PARTS)
        for j, block in enumerate((pair + core, pair + 1 - core)):
            out_ref[j] = sum_ref[:, pl.ds(pl.multiple_of(block * DH, DH), DH)]


def side(place, *args):
    return pl.pallas_call(
        side_kernel,
        out_shape=(f32(2, ROWS, DH),) * PARTS,
        in_specs=[SMEM] + [VMEM] * len(args),
        scratch_shapes=[pltpu.VMEM((ROWS, 2 * PARTS * DH), jnp.float32)],
        compiler_params=pltpu.CompilerParams(vmem_limit_bytes=SMALL_BYTES),
        cost_estimate=pl.CostEstimate(flops=170_000_000, bytes_accessed=3_000_000, transcendentals=0),
        name="side",
    )(place, *args)


def narrow_kernel(frames_ref, narrow_ref):
    narrow_ref[...] = frames_ref[...].astype(jnp.bfloat16)


def narrow(frames):
    return pl.pallas_call(
        narrow_kernel,
        out_shape=jax.ShapeDtypeStruct(frames.shape, jnp.bfloat16),
        in_specs=[VMEM],
        out_specs=VMEM,
        compiler_params=pltpu.CompilerParams(vmem_limit_bytes=SMALL_BYTES),
        cost_estimate=pl.CostEstimate(flops=1_000_000, bytes_accessed=3_000_000, transcendentals=0),
        name="narrow",
    )(frames)


def weigh_kernel(place_ref, pieces_ref, frames_ref, sums_ref):
    quarter = pl.ds(pl.multiple_of(place_ref[0] * 256, 256), 256)
    total = jnp.zeros((1024, DH), jnp.float32)
    corner = jnp.zeros((256, DH), jnp.float32)
    beta = jnp.zeros((2, 256), jnp.float32)
    bias = jnp.zeros((1, DH), jnp.float32)
    for i in range(PARTS):
        piece = pieces_ref[i, : 2 * ROWS].astype(jnp.bfloat16)
        rows = pieces_ref[i, 2 * ROWS :]
        bias = bias + rows[2:3]
        beta = beta + dot(rows[:2].astype(jnp.bfloat16), frames_ref[i, :, quarter])
        total = total + dot(frames_ref[i], piece[:ROWS], 0, 0)
        corner = corner + dot(frames_ref[i, :, quarter], piece[ROWS:], 0, 0)
    extra = [beta[:, :DH], beta[:, DH:], bias, jnp.zeros((EXTRA - 5, DH), jnp.float32)]
    extra = jnp.concatenate(extra, axis=0)
    total = jnp.concatenate([total, corner], axis=0)
    rows = total.shape[0] // (PARTS * PARTS)
    for i in range(PARTS):
        for j in range(PARTS):
            block = PARTS * j + i
            sums_ref[i, rows * j : rows * j + rows] = total[rows * block : rows * block + rows]
        sums_ref[i, rows * PARTS :] = extra


def weigh(place, pieces, frames):
    return pl.pallas_call(
        weigh_kernel,
        out_shape=f32(PARTS, 1280 // PARTS + EXTRA, DH),
        in_specs=[SMEM, VMEM, VMEM],
        compiler_params=pltpu.CompilerParams(vmem_limit_bytes=SMALL_BYTES),
        name="weigh",
    )(place, pieces, frames)


def lay_kernel(whole_ref, *refs):
    heads = refs[:2]
    query_any, keys_any, values_any, beta_any, bias_any, frames_any = refs[2:8]
    beta_ref, bias_ref, sum_ref, sems = refs[8:]
    left, right = pl.ds(0, DH), pl.ds(DH, DH)
    full = pl.ds(0, 1024)
    pairs = [
        (whole_ref.at[0, full], query_any),
        (whole_ref.at[1, full], keys_any.at[:, left]),
        (whole_ref.at[2, full], keys_any.at[:, right]),
        (whole_ref.at[3, full], values_any.at[:, left]),
    ]
    for i in range(PARTS):
        pairs.append(
            (whole_ref.at[i, pl.ds(1024, 256)], values_any.at[pl.ds(256 * i, 256), right])
        )
    copies = fetch(pairs, sems)
    rows = [whole_ref[i, 1280:] for i in range(PARTS)]
    beta_ref[...] = jnp.concatenate(
        [row[2 * half : 2 * half + 2] for row in rows for half in range(2)], axis=1
    )
    bias_ref[...] = rows[0][4:5, :2]
    sum_ref[...] = (heads[0][...] + heads[1][...]).astype(jnp.bfloat16)
    small = ((beta_ref, beta_any), (bias_ref, bias_any), (sum_ref, frames_any))
    for i, (a, b) in enumerate(small):
        copies.append(pltpu.make_async_copy(a, b, sems.at[8 + i]))
        copies[-1].start()
    for copy in copies:
        copy.wait()


def lay(whole, heads):
    frames = jax.ShapeDtypeStruct((ROWS, DH), jnp.bfloat16)
    return pl.pallas_call(
        lay_kernel,
        out_shape=(
            f32(1024, DH), f32(1024, 2 * DH), f32(1024, 2 * DH), f32(2, 1024), f32(1, 2), frames,
        ),
        in_specs=[VMEM] * 3,
        out_specs=(HBM,) * 6,
        scratch_shapes=[
            held(f32(2, 1024)), held(f32(1, 2)), held(frames), pltpu.SemaphoreType.DMA((11,)),
        ],
        compiler_params=pltpu.CompilerParams(vmem_limit_bytes=SMALL_BYTES),
        name="lay",
    )(whole, *heads)


def spread(a, axis):
    return lax.all_to_all(jnp.broadcast_to(a[None], (PARTS, *a.shape)), axis, 0, 0, tiled=True)


def trade(a, axis):
    return lax.all_to_all(a, axis, 0, 0, tiled=True)


def shift(a, axis, steps):
    size = lax.axis_size(axis)
    return lax.ppermute(a, axis, [(i, (i + steps) % size) for i in range(size)])


def local(frames, w_query, w_keys, w_values, w_beta, beta_bias, cotangent):
    place = jnp.stack(
        [lax.axis_index("x"), lax.axis_index("zl"), lax.axis_index("zh")]
        + [lax.axis_index("y"), lax.axis_index("core")]
    )
    beta_turned = w_beta.T
    own, kept, wide_frames = prepare(
        beta_bias, beta_turned, frames, w_keys, w_query, w_values, cotangent
    )
    row, wide_frames = lax.optimization_barrier((lax.all_gather(own, "x"), wide_frames))
    group_frames = trade(wide_frames, "x")
    total, kept = group_scan(row, kept, place, 0, "own", DH)
    total, kept = group_scan(lax.all_gather(total, "zl"), kept, place, 1, "near", DH // PARTS)
    far = lax.all_gather(total, "zh")
    far = jnp.concatenate([far[1:-1, 0], far[:-1, 1], far[1:, 2]], axis=0)
    far = lax.all_gather(far, "x")
    outputs, pieces, tiles = finish(place, far, kept)
    pieces, group_frames = trade(pieces, "x"), narrow(group_frames)
    heads = side(place, tiles, beta_turned, w_query, w_keys, w_values)
    pieces, group_frames, heads = lax.optimization_barrier((pieces, group_frames, heads))
    sums = weigh(place, pieces, group_frames)
    shared = heads[0] + shift(heads[1], "y", 1) + shift(heads[2], "y", 2)
    shared, last = lax.optimization_barrier((shared, heads[3]))
    shared = shared + shift(last, "y", 3)
    part = jnp.sum(trade(sums, "zl"), axis=0)
    part, extra = part[:320], part[320:]
    part = jnp.concatenate(
        [part.reshape(PARTS, 80, DH), jnp.broadcast_to(extra[None], (PARTS, EXTRA, DH))], axis=1
    )
    partial = (shared[0], shift(shared[1], "core", 1))
    part = jnp.sum(trade(part, "zh"), axis=0)
    part, extra = part[:80], part[80:]
    part = lax.all_gather(part, ("zh", "zl")).reshape(1280, DH)
    part, partial = lax.optimization_barrier((part, partial))
    whole = jnp.concatenate([part, extra], axis=0)
    grad_query, grad_keys, grad_values, beta_rows, bias_row, grad_frames = lay(
        spread(whole, "x"), partial
    )
    grad_beta = beta_rows.T
    grad_bias = bias_row.reshape(2)
    return (outputs, grad_frames, grad_query, grad_keys, grad_values, grad_beta, grad_bias)


def solution(mesh):
    fine = Mesh(mesh.devices.reshape(4, 4, 4, 4, 2), ("zh", "zl", "x", "y", "core"))
    ctx, head = ("zh", "zl", "x"), ("y", "core")
    in_specs = (
        P(ctx, None),
        P(None, head),
        P(None, head),
        P(None, head),
        P(None, head),
        P(head),
        P(ctx, head),
    )
    out_specs = (
        P(ctx, head),
        P(ctx, head),
        P(None, head),
        P(None, head),
        P(None, head),
        P(None, head),
        P(head),
    )
    return jax.shard_map(local, mesh=fine, in_specs=in_specs, out_specs=out_specs, check_vma=False)
```
